32 devices in a mesh: batch: 16 (over z, y, x), blk: 2 (over core).
Axes of the slice: x: 2, y: 2, z: 4, core: 2. Of those that a mesh axis runs over, the one named last changes fastest.
Arguments:
- hidden: bfloat16 [32, 512, 1024], P('batch', 'blk'), may hold values from -6 to 6
- cotangent: bfloat16 [32, 512, 1024], P('batch', 'blk'), may hold values from -6 to 6
- lengths: int32 [32], P('batch'), may hold values from 257 to 512, as said below
- separators: int32 [32], P('batch'), may hold values from 1 to 510, as said below
- type_table: bfloat16 [2, 1024], replicated, may hold values from -3 to 3
- projection_weight: bfloat16 [2, 1024, 3072], P(None, 'batch'), may hold values from -0.1875 to 0.1875
- output_weight: bfloat16 [2, 1024, 1024], P(None, 'batch'), may hold values from -1.5 to 1.5
- inner_weight: bfloat16 [2, 1024, 4096], P(None, 'batch'), may hold values from -0.1875 to 0.1875
- outer_weight: bfloat16 [2, 4096, 1024], P(None, 'batch'), may hold values from -0.09375 to 0.09375
- query_bias: float32 [2, 1024], replicated, may hold values from -3 to 3
- value_bias: float32 [2, 1024], replicated, may hold values from -3 to 3
- output_bias: float32 [2, 1024], replicated, may hold values from -2 to 2
- inner_bias: float32 [2, 4096], replicated, may hold values from -3 to 3
- outer_bias: float32 [2, 1024], replicated, may hold values from -2 to 2
- first_gain: float32 [2, 1024], replicated, may hold values from 0.5 to 1.5
- first_shift: float32 [2, 1024], replicated, may hold values from -2 to 2
- second_gain: float32 [2, 1024], replicated, may hold values from 0.5 to 1.5
- second_shift: float32 [2, 1024], replicated, may hold values from -2 to 2
Outputs:
- layer_output: bfloat16 [32, 512, 1024], P('batch', 'blk')
- input_gradient: bfloat16 [32, 512, 1024], P('batch', 'blk')
- query_bias_gradient: float32 [2, 1024], replicated
- value_bias_gradient: float32 [2, 1024], replicated
- output_bias_gradient: float32 [2, 1024], replicated
- inner_bias_gradient: float32 [2, 4096], replicated
- outer_bias_gradient: float32 [2, 1024], replicated
- first_shift_gradient: float32 [2, 1024], replicated
- second_shift_gradient: float32 [2, 1024], replicated
The draws below stay inside these ranges and needn't reach their ends.
Inputs may be any that keep to these rules, and one draw needn't show every extreme that they name: `lengths`: every pair's length exceeds 256; in every draw some pair is 512 long. separators[s] <= lengths[s] - 2; in every draw some pair has its separator at 1 and some pair at 510.
All inputs are finite; a program needn't handle non-finite values.
Results may differ from the reference program's by a relative error of at most 0.019.
Values may be sent and summed in bfloat16 or wider, within the bound.
A program may use at most 192 MiB of HBM per device.

```python
import jax
import jax.numpy as jnp
from jax import lax

D = 1024
HEADS = 16
HEAD = 64
FF = 4096
LAYERS = 2
SEQ = 512
SEQ_GRP = 2
SPAN = 256
SEQS = 32


def length_pair(key):
    key_length, key_choice, key_mark = jax.random.split(key, 3)
    sampled = jax.random.randint(key_length, (SEQS,), SEQ - SPAN + 1, SEQ + 1)
    chosen = jax.random.randint(key_choice, (), 0, SEQS)
    rows = jnp.arange(SEQS)
    lengths = jnp.where(rows == chosen, SEQ, sampled).astype(jnp.int32)
    separator_at = jax.random.randint(key_mark, (SEQS,), 1, lengths - 1).astype(jnp.int32)
    separator_at = jnp.where(rows == chosen, SEQ - 2, separator_at)
    separator_at = jnp.where(rows == (chosen + 1) % SEQS, 1, separator_at).astype(jnp.int32)
    return (lengths, separator_at)


def draw_lengths(key, part):
    return length_pair(key)[0]


def draw_separators(key, part):
    return length_pair(key)[1]


def block_scale(own_key, shape, cuts, low, top_value):
    gain = 1.0
    for dim, parts in cuts:
        draws = jax.random.uniform(jax.random.fold_in(jax.random.fold_in(own_key, 6), dim), (parts,), jnp.float32, low / len(cuts), top_value / len(cuts))
        gain = gain * jnp.repeat(jnp.exp(draws), shape[dim] // parts).reshape((-1,) + (1,) * (len(shape) - 1 - dim))
    return gain


def bell_draw(rng, dims, width, bound, cuts=(), held_as=jnp.bfloat16):
    entries = width * jax.random.normal(rng, dims, jnp.float32)
    if cuts:
        entries = entries * block_scale(rng, dims, cuts, -0.22, 0.18)
    return jnp.clip(entries, -bound, bound).astype(held_as)


def setup_inputs(seed: int = 0) -> dict:
    key_of = jax.random.split(jax.random.key(seed), 19)
    hidden = bell_draw(key_of[0], (SEQS, SEQ, D), 1.0, 6.0, ((0, 16), (1, 2)))
    cotangent = bell_draw(key_of[1], (SEQS, SEQ, D), 1.0, 6.0, ((0, 16), (1, 2)))
    lengths = draw_lengths(jax.random.fold_in(key_of[18], 71), 0)
    separators = draw_separators(jax.random.fold_in(key_of[18], 71), 0)
    type_table = bell_draw(key_of[4], (2, D), 0.5, 3.0)
    projection_weight = bell_draw(key_of[5], (LAYERS, D, 3 * D), D ** -0.5, 0.1875, ((1, 16),))
    output_weight = bell_draw(key_of[6], (LAYERS, D, D), (D // 64) ** -0.5, 1.5, ((1, 16),))
    inner_weight = bell_draw(key_of[7], (LAYERS, D, FF), D ** -0.5, 0.1875, ((1, 16),))
    outer_weight = bell_draw(key_of[8], (LAYERS, FF, D), FF ** -0.5, 0.09375, ((1, 16),))
    query_bias = bell_draw(key_of[9], (LAYERS, D), 0.5, 3.0, (), jnp.float32)
    value_bias = bell_draw(key_of[10], (LAYERS, D), 0.5, 3.0, (), jnp.float32)
    output_bias = bell_draw(key_of[11], (LAYERS, D), 0.3, 2.0, (), jnp.float32)
    inner_bias = bell_draw(key_of[12], (LAYERS, FF), 0.5, 3.0, (), jnp.float32)
    outer_bias = bell_draw(key_of[13], (LAYERS, D), 0.3, 2.0, (), jnp.float32)
    first_gain = jnp.clip(1.0 + 0.1 * jax.random.normal(key_of[14], (LAYERS, D), jnp.float32), 0.5, 1.5)
    first_shift = bell_draw(key_of[15], (LAYERS, D), 0.3, 2.0, (), jnp.float32)
    second_gain = jnp.clip(1.0 + 0.1 * jax.random.normal(key_of[16], (LAYERS, D), jnp.float32), 0.5, 1.5)
    second_shift = bell_draw(key_of[17], (LAYERS, D), 0.3, 2.0, (), jnp.float32)
    return {"hidden": hidden, "cotangent": cotangent, "lengths": lengths, "separators": separators, "type_table": type_table, "projection_weight": projection_weight, "output_weight": output_weight, "inner_weight": inner_weight, "outer_weight": outer_weight, "query_bias": query_bias, "value_bias": value_bias, "output_bias": output_bias, "inner_bias": inner_bias, "outer_bias": outer_bias, "first_gain": first_gain, "first_shift": first_shift, "second_gain": second_gain, "second_shift": second_shift}


EPSILON = 1e-12
PRECISE = lax.Precision.HIGHEST

@jax.custom_vjp
def low(v):
    return lax.optimization_barrier(v.astype(jnp.bfloat16)).astype(jnp.float32)

@jax.custom_vjp
def low_back(v):
    return v

def low_keep(v):
    return (low(v), None)

def low_pass(kept, grad):
    return (grad,)

def back_keep(v):
    return (v, None)

def back_low(kept, grad):
    return (low(grad),)
low.defvjp(low_keep, low_pass)
low_back.defvjp(back_keep, back_low)

def matmul(left, weight):
    return jnp.einsum('gtd,de->gte', left, weight, precision=PRECISE)

def layer_norm(summed, norm_gain, norm_shift):
    average = lax.optimization_barrier(jnp.mean(summed, axis=-1, keepdims=True))
    centred = summed - average
    variance = lax.optimization_barrier(jnp.mean(centred * centred, axis=-1, keepdims=True))
    return centred * lax.rsqrt(variance + EPSILON) * norm_gain + norm_shift

def encoder_layer(states, key_valid, frozen_layer, trained_layer, gain_first, gain_second):
    w_triple, w_output, w_inner, w_outer = frozen_layer
    bias_query, bias_value, bias_output, bias_inner, bias_outer, shift_first, shift_second = trained_layer
    group_count = states.shape[0]
    lowered = low(states)
    queries = low(low_back(matmul(lowered, w_triple[:, :D])) + bias_query)
    keys = low(low_back(matmul(lowered, w_triple[:, D:2 * D])))
    values = low(low_back(matmul(lowered, w_triple[:, 2 * D:])) + bias_value)
    query_heads = queries.reshape(group_count, SEQ, HEADS, HEAD)
    key_heads = keys.reshape(group_count, SEQ, HEADS, HEAD)
    value_heads = values.reshape(group_count, SEQ, HEADS, HEAD)
    product = low_back(jnp.einsum('gqhe,gkhe->ghqk', query_heads, key_heads, precision=PRECISE))
    scores = jnp.where(key_valid[:, None, None, :], product * HEAD ** (-0.5), -1000000000.0)
    largest = lax.optimization_barrier(jnp.max(scores, axis=-1, keepdims=True))
    exponent = jnp.exp(scores - largest)
    probability = low(exponent / lax.optimization_barrier(jnp.sum(exponent, axis=-1, keepdims=True)))
    context = low(low_back(jnp.einsum('ghqk,gkhe->gqhe', probability, value_heads, precision=PRECISE)))
    context = context.reshape(group_count, SEQ, D)
    attended = low_back(matmul(context, w_output)) + bias_output
    middle = layer_norm(states + attended, gain_first, shift_first)
    hidden_pre = low_back(matmul(low(middle), w_inner)) + bias_inner
    activated = low(jax.nn.gelu(hidden_pre, approximate=False))
    outer_part = low_back(matmul(activated, w_outer)) + bias_outer
    return layer_norm(middle + outer_part, gain_second, shift_second)

def reference(hidden, cotangent, lengths, separators, type_table, projection_weight, output_weight, inner_weight, outer_weight, query_bias, value_bias, output_bias, inner_bias, outer_bias, first_gain, first_shift, second_gain, second_shift):
    position = jnp.arange(SEQ)
    second_part = (position[None, :] > separators[:, None]).astype(jnp.float32)
    type_rows = type_table.astype(jnp.float32)
    start = hidden.astype(jnp.float32) + type_rows[0] + second_part[:, :, None] * (type_rows[1] - type_rows[0])
    key_valid = position[None, :] < lengths[:, None]
    frozen = tuple(((projection_weight[layer_index].astype(jnp.float32), output_weight[layer_index].astype(jnp.float32), inner_weight[layer_index].astype(jnp.float32), outer_weight[layer_index].astype(jnp.float32)) for layer_index in range(LAYERS)))
    trained = (query_bias, value_bias, output_bias, inner_bias, outer_bias, first_shift, second_shift)
    group_count = SEQS // SEQ_GRP

    def forward(trained_now, inputs):

        def group_layers(group_pair):
            states, valid_group = group_pair
            for layer_index in range(LAYERS):
                states = encoder_layer(states, valid_group, frozen[layer_index], tuple((member[layer_index] for member in trained_now)), first_gain[layer_index], second_gain[layer_index])
            return states
        mapped = lax.map(jax.checkpoint(group_layers), (inputs.reshape(group_count, SEQ_GRP, SEQ, D), key_valid.reshape(group_count, SEQ_GRP, SEQ)))
        return mapped.reshape(SEQS, SEQ, D)
    result, pullback = jax.vjp(forward, trained, start)
    grad_trained, grad_start = pullback(cotangent.astype(jnp.float32))
    return (result.astype(jnp.bfloat16), grad_start.astype(jnp.bfloat16), grad_trained[0], grad_trained[1], grad_trained[2], grad_trained[3], grad_trained[4], grad_trained[5], grad_trained[6])
```

```python
import functools

import jax
import jax.numpy as jnp
from jax import lax
from jax.experimental import pallas as pl
from jax.experimental.pallas import tpu as pltpu
from jax.sharding import PartitionSpec as P

D = 1024
HEADS = 16
HEAD = 64
FF = 4096
LAYERS = 2
UNITS = 24
PER = 12
SPLIT = 640
BLK = 256
ROWS = 64
EPSILON = 1e-12
MASKED = -1000000000.0
MESH = pl.DeviceIdType.MESH
BF = jnp.bfloat16
F32 = jnp.float32


def sizes(batch):
    side = 2 ** ((batch.bit_length() - 1) // 3)
    return batch // (side * side), side


def lane(n):
    return 1 if n == 2 else 2 * (n - 1)


class Comm:
    def __init__(self, nz, n, gathered, ssem, rsem, sib_s, sib_r, slots, gap):
        self.nz, self.n, self.G = nz, n, gathered
        self.ssem, self.rsem, self.sib_s, self.sib_r = ssem, rsem, sib_s, sib_r
        self.slots, self.gap = slots, gap
        self.b = lax.axis_index("batch")
        self.c = lax.axis_index("blk")
        self.z, self.y, self.x = self.b // (n * n), (self.b // n) % n, self.b % n
        self.stages = 1 + (n - 1) + (nz - 1) + (n - 1)
        self.fbase = 2 * (nz - 1)

    @staticmethod
    def sems(nz, n):
        return 2 * (nz - 1) + 2 * nz * lane(n)

    def cols(self, core):
        return pl.ds(0, SPLIT) if core == 0 else pl.ds(SPLIT, D - SPLIT)

    def setup(self, core, par, u):
        first_x = (core == 0) == (par == 0)
        cs, g, n = self.cols(core), self.G, self.n
        self.f, self.s = (self.x, self.y) if first_x else (self.y, self.x)
        self.fstr, self.sstr = (1, n) if first_x else (n, 1)
        if first_x:
            self.sl = lambda zi, fi, si: g.at[u, zi, si, fi, :, cs]
        else:
            self.sl = lambda zi, fi, si: g.at[u, zi, fi, si, :, cs]
        self.slot = u % self.slots

    def copy(self, ref, idx, to):
        return pltpu.make_async_remote_copy(
            src_ref=ref,
            dst_ref=ref,
            send_sem=self.ssem.at[self.slot, idx],
            recv_sem=self.rsem.at[self.slot, idx],
            device_id=(to, self.c),
            device_id_type=MESH,
        )

    def dirs(self, length):
        return (0,) if length == 2 else (0, 1)

    def act(self, cp, mode):
        if mode == "start":
            cp.start()
        else:
            cp.wait_send()

    def arrive(self, ref, base, pos, length, stride, j, e, mode):
        if length == 2:
            to = self.b + stride * (1 - 2 * pos)
            if j == 0:
                self.act(self.copy(ref(pos), base, to), mode)
            elif mode == "start":
                self.copy(ref(1 - pos), base, to).wait_recv()
            return
        if j == 0:
            for d in (0, 1):

                @pl.when((pos + 1 < length) if d == 0 else (pos >= 1))
                def _():
                    self.act(self.copy(ref(pos), base + d, self.b + (stride if d == 0 else -stride)), mode)

            return
        src = pos - j if e == 0 else pos + j
        ok = (src >= 0) if e == 0 else (src < length)
        fwd = (pos + 1 < length) if e == 0 else (pos >= 1)
        to = self.b + (stride if e == 0 else -stride)
        if mode == "start":

            @pl.when(ok)
            def _():
                self.copy(ref(src), base + 2 * (j - 1) + e, to).wait_recv()

        if j < length - 1:

            @pl.when(ok & fwd)
            def _():
                self.act(self.copy(ref(src), base + 2 * j + e, to), mode)

    def hops(self):
        yield 0, 0
        for h in range(1, self.nz):
            for d in (0, 1):
                yield h, d

    def run(self, core, par, u, k, mode):
        self.setup(core, par, u)
        n, nz, z, b = self.n, self.nz, self.z, self.b
        lw = lane(n)
        sbase = self.fbase + nz * lw
        f, s = self.f, self.s
        pre = 0
        if core == 0:
            for j in range(n):
                if k is None or k == j:
                    for e in self.dirs(n) if j else (0,):
                        self.arrive(lambda i: self.sl(z, i, s), self.fbase, f, n, self.fstr, j, e, mode)
            pre = n - 1
        last = (n - 1) if core == 0 else 2 * (n - 1)
        for h, d in self.hops():
            zi = z - h if d == 0 else z + h
            fi = f if core == 1 else slice(None)

            def along_z():
                ref = self.sl(zi, fi, s)
                if h and mode == "start":
                    self.copy(ref, 2 * (h - 1) + d, b).wait_recv()
                if h < nz - 1:
                    for dd in (0, 1) if h == 0 else (d,):

                        @pl.when((z + 1 < nz) if dd == 0 else (z >= 1))
                        def _():
                            self.act(self.copy(ref, 2 * h + dd, b + (n * n if dd == 0 else -n * n)), mode)

            def in_plane(step):
                q = step
                if core == 1:
                    if step < n:
                        for e in self.dirs(n) if step else (0,):
                            self.arrive(
                                lambda i: self.sl(zi, i, s), self.fbase + zi * lw, f, n, self.fstr, step, e, mode
                            )
                    q = step - (n - 1)
                if q >= 0:
                    for e in self.dirs(n) if q else (0,):
                        self.arrive(
                            lambda i: self.sl(zi, slice(None), i), sbase + zi * lw, s, n, self.sstr, q, e, mode
                        )

            def events():
                for step in range(last + 1):
                    if k is None or k == pre + h + step:
                        if step == 0:
                            along_z()
                        in_plane(step)

            if k is None or 0 <= k - pre - h <= last:
                if h == 0:
                    events()
                else:
                    pl.when((zi >= 0) if d == 0 else (zi < nz))(events)
        if k == self.stages - 1:
            self.sibling(core, u).start()
        if k is None:
            self.sibling(core, u).wait_send()

    def sibling(self, core, u):
        ref = self.G.at[u, :, :, :, :, self.cols(core)]
        return pltpu.make_async_remote_copy(
            src_ref=ref,
            dst_ref=ref,
            send_sem=self.sib_s.at[u % self.slots],
            recv_sem=self.sib_r.at[u],
            device_id=(self.b, 1 - self.c),
            device_id_type=MESH,
        )

    def tick(self, t):
        for core in (0, 1):

            @pl.when(self.c == core)
            def _():
                for k in [self.stages, *reversed(range(self.stages))]:
                    u = t - k * self.gap
                    for par in (0, 1):

                        @pl.when((u >= 0) & (u < UNITS) & (u % 2 == par))
                        def _():
                            if k == self.stages:
                                self.run(core, par, u, None, "drain")
                            else:
                                self.run(core, par, u, k, "start")

    def partners(self):
        yield (self.b, 1 - self.c)
        step = 1
        while step < self.nz * self.n * self.n:
            yield (self.b + step * (1 - 2 * ((self.b // step) % 2)), self.c)
            step *= 2

    def barrier(self):
        bar = pltpu.get_barrier_semaphore()
        n, nz = self.n, self.nz
        total = jnp.int32(0)
        for to in self.partners():
            pl.semaphore_signal(bar, inc=1, device_id=to, device_id_type=MESH)
            total = total + 1
        for length, pos, stride in ((n, self.x, 1), (n, self.y, n), (nz, self.z, n * n)):
            for d in (0, 1):
                ok = (pos + 1 < length) if d == 0 else (pos >= 1)
                total = total + ok.astype(jnp.int32)

                @pl.when(ok)
                def _():
                    to = (self.b + (stride if d == 0 else -stride), self.c)
                    pl.semaphore_signal(bar, inc=1, device_id=to, device_id_type=MESH)

        pl.semaphore_wait(bar, total)


def dot(a, b, ca=1, cb=0):
    return lax.dot_general(a, b, (((ca,), (cb,)), ((), ())), preferred_element_type=F32)


def fold(values):
    rows, cols = values.shape
    return jnp.sum(values.reshape(rows // 8, 8, cols), axis=0)


def colsum(values):
    return jnp.sum(values, axis=0, keepdims=True)


def kernel(
    nz,
    n,
    gap,
    slots,
    lengths,
    separators,
    hidden,
    cotangent,
    type_table,
    proj,
    outw,
    inner,
    outer,
    query_bias,
    value_bias,
    output_bias,
    inner_bias,
    outer_bias,
    first_gain,
    first_shift,
    second_gain,
    second_shift,
    layer_output,
    input_gradient,
    grads,
    G,
    P0,
    stg,
    xin,
    cot,
    xs,
    xb,
    qkv,
    qT,
    prob,
    mid,
    act,
    gp,
    n1,
    n2,
    r1,
    r2,
    gcT,
    dkT,
    dvT,
    wbuf,
    bg,
    arb,
    dqs8,
    ssem,
    rsem,
    sib_s,
    sib_r,
    lsem,
    wsem,
    xsem,
    psem,
    osem,
    asem,
):
    nb = nz * n * n
    R = D // nb
    T = xs.shape[0]
    half = T // 2
    quarter = nb // 4
    comm = Comm(nz, n, G, ssem, rsem, sib_s, sib_r, slots, gap)
    c = comm.c
    other = (comm.b, 1 - c)
    ctx = xin

    def stage_in(op):
        for l in range(LAYERS):
            for u in range(8):
                m, j = (proj, u) if u < 3 else (outw, 0) if u == 3 else (inner, u - 4)
                cp = pltpu.make_async_copy(m.at[l, :, pl.ds(j * D, D)], stg.at[l * PER + u], lsem.at[l * PER + u])
                getattr(cp, op)()
            for j in range(4):
                for g in range(4):
                    cp = pltpu.make_async_copy(
                        outer.at[l, pl.ds(g * R, R), pl.ds(j * BLK, BLK)],
                        stg.at[l * PER + 8 + j, :, pl.ds(g * BLK, BLK)],
                        lsem.at[UNITS + (l * 4 + j) * 4 + g],
                    )
                    getattr(cp, op)()

    def place(op):
        for core in (0, 1):

            @pl.when(c == core)
            def _():
                def one(u, carry):
                    cs = comm.cols(core)
                    cp = pltpu.make_async_copy(
                        stg.at[u, :, cs], G.at[u, comm.z, comm.y, comm.x, :, cs], lsem.at[u]
                    )
                    getattr(cp, op)()
                    return carry

                lax.fori_loop(0, UNITS, one, 0)

    def exchange(op):
        for i, (src, dst) in enumerate(((hidden, xin), (cotangent, cot))):
            rows = pl.ds(pl.multiple_of(c * half, half), half)
            lc = pltpu.make_async_copy(src.at[c], dst.at[rows], xsem.at[3 * i])
            rc = pltpu.make_async_remote_copy(
                src_ref=src.at[1 - c],
                dst_ref=dst.at[rows],
                send_sem=xsem.at[3 * i + 1],
                recv_sem=xsem.at[3 * i + 2],
                device_id=other,
                device_id_type=MESH,
            )
            getattr(lc, op)()
            getattr(rc, op)()

    stage_in("start")
    comm.barrier()
    exchange("start")
    stage_in("wait")
    place("start")
    place("wait")

    def row(ref, l):
        return ref[pl.ds(l, 1), :]

    def cols(i, width=BLK):
        return pl.ds(pl.multiple_of(i * width, width), width)

    lanes = lax.broadcasted_iota(jnp.int32, (T, 2 * HEAD), 1)
    halves = (lanes < HEAD, lanes >= HEAD)

    def init_x():
        exchange("wait")
        t0 = type_table[0:1, :].astype(F32)
        t1 = type_table[1:2, :].astype(F32)
        sep = separators[c]

        def rows_of(i, carry):
            rs = pl.ds(pl.multiple_of(i * ROWS, ROWS), ROWS)
            at = i * ROWS + lax.broadcasted_iota(jnp.int32, (ROWS, D), 0)
            second = (at > sep).astype(F32)
            x = xin[rs, :].astype(F32) + t0 + second * (t1 - t0)
            xs[rs, :] = x
            xb[rs, :] = x.astype(BF)
            return carry

        lax.fori_loop(0, T // ROWS, rows_of, 0)

    def load_unit(u, slot, op):
        def one(g, carry):
            cp = pltpu.make_async_copy(
                G.at[u, :, :, :, :, cols(g)], wbuf.at[slot, :, :, :, g], wsem.at[slot, g]
            )
            getattr(cp, op)()
            return carry

        lax.fori_loop(0, 4, one, 0)

    def load_rows(l, f, slot, op):
        zs = pl.ds(f * (nz // 4), nz // 4)

        def one(i, carry):
            j, g = i // 4, i % 4
            cp = pltpu.make_async_copy(
                G.at[l * PER + 8 + j, zs, :, :, :, cols(g)],
                wbuf.at[slot, pl.ds(j * (nz // 4), nz // 4), :, :, g],
                wsem.at[slot, i],
            )
            getattr(cp, op)()
            return carry

        lax.fori_loop(0, 16, one, 0)

    def w_cols(slot, g):
        return wbuf[slot, :, :, :, g].reshape(D, BLK)

    def w_rows(slot, i):
        q = nz // 4
        return jnp.concatenate(
            [wbuf[slot, pl.ds(i * q, q), :, :, g].reshape(BLK, BLK) for g in range(4)], axis=1
        )

    def o_rows(slot, i):
        if nz == 4:
            parts = [wbuf[slot, j, i // n, i % n].reshape(BLK, BLK) for j in range(4)]
        else:
            q = nz // 4
            parts = [wbuf[slot, pl.ds(j * q, q)].reshape(D, BLK)[i * BLK : (i + 1) * BLK] for j in range(4)]
        return jnp.concatenate(parts, axis=1)

    def norm_rows(z, gain, shift):
        average = jnp.mean(z, axis=1, keepdims=True)
        centred = z - average
        r = lax.rsqrt(jnp.mean(centred * centred, axis=1, keepdims=True) + EPSILON)
        normed = centred * r
        return normed, r, normed * gain + shift

    def do_qkv(l, j, slot):
        is_q, is_v = (j == 0).astype(F32), (j == 2).astype(F32)
        at = jnp.where(j == 0, 0, 2 * l + j)
        for g in range(4):
            sl = slice(g * BLK, (g + 1) * BLK)
            bias = query_bias[pl.ds(l, 1), sl] * is_q + value_bias[pl.ds(l, 1), sl] * is_v
            qkv[at, :, sl] = (dot(xb[...], w_cols(slot, g)) + bias).astype(BF)

    def do_attention(l, lo, hi):
        key_ok = lax.broadcasted_iota(jnp.int32, (1, T), 1) < lengths[c]

        def pair(hp, carry):
            cs = cols(hp, 2 * HEAD)
            q2, k2, v2 = qkv[0, :, cs], qkv[2 * l + 1, :, cs], qkv[2 * l + 2, :, cs]
            outs = []
            for hh in (0, 1):
                qm = jnp.where(halves[hh], q2 * BF(HEAD**-0.5), BF(0))
                s = jnp.where(key_ok, dot(qm, k2, 1, 1), MASKED)
                e = jnp.exp(s - jnp.max(s, axis=1, keepdims=True))
                p = (e * (1.0 / jnp.sum(e, axis=1, keepdims=True))).astype(BF)
                prob[2 * hp + hh] = p
                outs.append(dot(p, v2))
            ctx[:, cs] = jnp.where(halves[0], outs[0], outs[1]).astype(BF)
            qT[l, cs, :] = q2.T
            return carry

        lax.fori_loop(lo, hi, pair, 0)

    def do_out(l, slot):
        for g in range(4):
            sl = slice(g * BLK, (g + 1) * BLK)
            mid[:, sl] = xs[:, sl] + dot(ctx[...], w_cols(slot, g)) + output_bias[pl.ds(l, 1), sl]
        gain, shift = row(first_gain, l), row(first_shift, l)

        def rows_of(i, carry):
            rs = pl.ds(pl.multiple_of(i * ROWS, ROWS), ROWS)
            normed, r, y = norm_rows(mid[rs, :], gain, shift)
            n1[l, rs, :] = normed.astype(BF)
            r1[l, rs, :] = r
            mid[rs, :] = y
            xb[rs, :] = y.astype(BF)
            return carry

        lax.fori_loop(0, T // ROWS, rows_of, 0)

    def do_inner(l, i, slot):
        for g in range(4):
            cs = cols(i * 4 + g)
            h = dot(xb[...], w_cols(slot, g)) + inner_bias[pl.ds(l, 1), cs]
            cdf = 0.5 + 0.5 * lax.erf(h * (0.5**0.5))
            act[:, cs] = (h * cdf).astype(BF)
            gp[l, :, cs] = (cdf + h * (jnp.exp(-0.5 * h * h) * 0.3989422804014327)).astype(BF)

    def do_outer(l, j, slot):
        cs = cols(j)
        w = wbuf[slot].reshape(FF, BLK)
        xs[:, cs] = mid[:, cs] + dot(act[...], w) + outer_bias[pl.ds(l, 1), cs]

    def do_norm2(l):
        gain, shift = row(second_gain, l), row(second_shift, l)

        def rows_of(i, carry):
            rs = pl.ds(pl.multiple_of(i * ROWS, ROWS), ROWS)
            normed, r, y = norm_rows(xs[rs, :], gain, shift)
            n2[l, rs, :] = normed.astype(BF)
            r2[l, rs, :] = r
            xb[rs, :] = y.astype(BF)
            xs[rs, :] = jnp.where(l == LAYERS - 1, cot[rs, :].astype(F32), y)
            return carry

        lax.fori_loop(0, T // ROWS, rows_of, 0)

    def save_prob(op):
        getattr(pltpu.make_async_copy(prob, P0, psem), op)()

    def compute(v, slot):
        l, k = v // PER, v % PER
        pl.when(k < 3)(lambda: do_qkv(l, k, slot))

        @pl.when((k >= 2) & (k <= 4))
        def _():
            lo = jnp.where(k == 2, 0, jnp.where(k == 3, 2, 5))
            hi = jnp.where(k == 2, 2, jnp.where(k == 3, 5, 8))
            do_attention(l, lo, hi)

        @pl.when(k == 4)
        def _():
            pl.when(l == 0)(lambda: save_prob("start"))
            do_out(l, 1 - slot)

        pl.when((k >= 4) & (k < 8))(lambda: do_inner(l, k - 4, slot))
        pl.when(k >= 8)(lambda: do_outer(l, k - 8, slot))

        @pl.when(k == PER - 1)
        def _():
            pl.when(l == 0)(lambda: save_prob("wait"))
            do_norm2(l)

    lag = (comm.stages - 1) * gap + 1

    def main(t, carry):
        v = t - lag
        slot = (v + 2 * lag) % 2
        ready = (v >= 0) & (v < UNITS)

        @pl.when(ready)
        def _():
            for core in (0, 1):

                @pl.when(c == core)
                def _():
                    comm.sibling(1 - core, v).wait_recv()

            load_unit(v, slot, "start")

        comm.tick(t)
        pl.when(t == 1)(init_x)

        @pl.when(ready)
        def _():
            load_unit(v, slot, "wait")
            compute(v, slot)

        return carry

    lax.fori_loop(0, UNITS + comm.stages * gap, main, 0)

    def results(src, out, base, op):
        mine = pl.ds(pl.multiple_of(c * half, half), half)
        theirs = pl.ds(pl.multiple_of((1 - c) * half, half), half)
        lc = pltpu.make_async_copy(src.at[mine], out.at[c], osem.at[base])
        rc = pltpu.make_async_remote_copy(
            src_ref=src.at[theirs],
            dst_ref=out.at[c],
            send_sem=osem.at[base + 1],
            recv_sem=osem.at[base + 2],
            device_id=other,
            device_id_type=MESH,
        )
        if op == "start":
            rc.start()
            lc.start()
        else:
            rc.wait_send()
            lc.wait()

    def arrived(src, out, base):
        rows = pl.ds(0, half)
        pltpu.make_async_remote_copy(
            src_ref=src.at[rows],
            dst_ref=out.at[1 - c],
            send_sem=osem.at[base + 1],
            recv_sem=osem.at[base + 2],
            device_id=other,
            device_id_type=MESH,
        ).wait_recv()

    def load(s, slot, op):
        l, k = 1 - s // PER, s % PER
        rows = (k < 8) & (k % 2 == 0)
        pl.when(rows)(lambda: load_rows(l, k // 2, slot, op))
        unit = l * PER + jnp.where(k < 8, 4 + k // 2, jnp.where(k == 8, 3, k - 9))
        pl.when(jnp.logical_not(rows))(lambda: load_unit(unit, slot, op))

    def next_weights(s):
        slot = s % 2
        load(s, slot, "wait")
        pl.when(s + 1 < UNITS)(lambda: load(s + 1, 1 - slot, "start"))
        return slot

    def norm_back(l, source, normed, r_ref, gain_ref, at_shift, at_bias, keep):
        gain = row(gain_ref, l)

        def rows_of(i, carry):
            sum_g, sum_z = carry
            rs = pl.ds(pl.multiple_of(i * ROWS, ROWS), ROWS)
            g = source[rs, :]
            nv = normed[l, rs, :].astype(F32)
            u = g * gain
            gz = r_ref[l, rs, :] * (
                u - jnp.mean(u, axis=1, keepdims=True) - nv * jnp.mean(u * nv, axis=1, keepdims=True)
            )
            keep[rs, :] = gz
            xb[rs, :] = gz.astype(BF)
            return sum_g + fold(g), sum_z + fold(gz)

        zero = jnp.zeros((8, D), F32)
        sum_g, sum_z = lax.fori_loop(0, T // ROWS, rows_of, (zero, zero))
        bg[pl.ds(l * 10 + at_shift, 1), :] = colsum(sum_g)
        bg[pl.ds(l * 10 + at_bias, 1), :] = colsum(sum_z)

    results(xb, layer_output, 0, "start")
    load(0, 0, "start")
    results(xb, layer_output, 0, "wait")

    def layer_back(i, carry):
        l = LAYERS - 1 - i
        s0 = i * PER
        norm_back(l, xs, n2, r2, second_gain, 9, 7, mid)

        def ff(f, carry):
            slot = next_weights(s0 + 2 * f)
            for i4 in range(4):
                cs = cols(f * 4 + i4)
                gh = dot(xb[...], o_rows(slot, i4), 1, 1) * gp[l, :, cs].astype(F32)
                bg[pl.ds(l * 10 + 3 + f, 1), i4 * BLK : (i4 + 1) * BLK] = colsum(fold(gh))
                act[:, cs] = gh.astype(BF)
            slot = next_weights(s0 + 2 * f + 1)
            for i4 in range(4):
                sl = slice(i4 * BLK, (i4 + 1) * BLK)
                mid[:, sl] += dot(act[:, cols(f, D)], w_rows(slot, i4), 1, 1)
            return carry

        lax.fori_loop(0, 4, ff, 0)
        norm_back(l, mid, n1, r1, first_gain, 8, 2, mid)
        slot = next_weights(s0 + 8)
        for i4 in range(4):
            sl = slice(i4 * BLK, (i4 + 1) * BLK)
            gc = dot(xb[...], w_rows(slot, i4), 1, 1).astype(BF)
            bg[pl.ds(l * 10 + 1, 1), sl] = colsum(fold(gc.astype(F32)))
            qkv[0, :, sl] = gc
            gcT[sl, :] = gc.T

        pl.when(i == 1)(lambda: load_prob("wait"))

        def pair(hp, carry):
            cs = cols(hp, 2 * HEAD)
            gc2, k2, v2 = qkv[0, :, cs], qkv[2 * l + 1, :, cs], qkv[2 * l + 2, :, cs]
            dqs = []
            for hh in (0, 1):
                hs = pl.ds(pl.multiple_of((2 * hp + hh) * HEAD, HEAD), HEAD)
                p = prob[2 * hp + hh]
                pf = p.astype(F32)
                gm = jnp.where(halves[hh], gc2 * BF(HEAD**-0.5), BF(0))
                dp = dot(gm, v2, 1, 1)
                total = jnp.sum(dp * pf, axis=1, keepdims=True)
                ds = (pf * (dp - total)).astype(BF)
                dqs.append(dot(ds, k2))
                dkT[hs, :] = dot(qT[l, hs, :], ds).astype(BF)
                dvT[hs, :] = dot(gcT[hs, :], p).astype(BF)
            dq = jnp.where(halves[0], dqs[0], dqs[1])
            dqs8[:, cs] = fold(dq)
            ctx[:, cs] = dq.astype(BF)
            return carry

        lax.fori_loop(0, HEADS // 2, pair, 0)
        bg[pl.ds(l * 10, 1), :] = colsum(dqs8[...])
        pl.when(i == 0)(lambda: load_prob("start"))

        slot = next_weights(s0 + 9)
        for i4 in range(4):
            sl = slice(i4 * BLK, (i4 + 1) * BLK)
            mid[:, sl] += dot(ctx[...], w_rows(slot, i4), 1, 1)
        slot = next_weights(s0 + 10)
        for i4 in range(4):
            sl = slice(i4 * BLK, (i4 + 1) * BLK)
            mid[:, sl] += dot(dkT[...], w_rows(slot, i4), 0, 1)
        slot = next_weights(s0 + 11)
        for i4 in range(4):
            sl = slice(i4 * BLK, (i4 + 1) * BLK)
            y = mid[:, sl] + dot(dvT[...], w_rows(slot, i4), 0, 1)
            xs[:, sl] = y
            xb[:, sl] = y.astype(BF)
        return carry

    def load_prob(op):
        getattr(pltpu.make_async_copy(P0, prob, psem), op)()

    bg[...] = jnp.zeros_like(bg)
    lax.fori_loop(0, LAYERS, layer_back, 0)
    results(xb, input_gradient, 3, "start")

    for r, to in enumerate(comm.partners()):
        cp = pltpu.make_async_remote_copy(
            src_ref=bg,
            dst_ref=arb.at[r],
            send_sem=asem.at[0, r],
            recv_sem=asem.at[1, r],
            device_id=to,
            device_id_type=MESH,
        )
        cp.start()
        cp.wait()
        bg[...] += arb[r]
    grads[...] = bg[...]
    results(xb, input_gradient, 3, "wait")
    arrived(xb, layer_output, 0)
    arrived(xb, input_gradient, 3)


def on_device(
    hidden,
    cotangent,
    lengths,
    separators,
    type_table,
    projection_weight,
    output_weight,
    inner_weight,
    outer_weight,
    query_bias,
    value_bias,
    output_bias,
    inner_bias,
    outer_bias,
    first_gain,
    first_shift,
    second_gain,
    second_shift,
):
    nb = lax.axis_size("batch")
    nz, n = sizes(nb)
    gap = 2 if nb <= 16 else 1
    stages = 1 + (n - 1) + (nz - 1) + (n - 1)
    slots = (stages + 1) * gap
    rounds = 1 + (nb.bit_length() - 1)
    T = 2 * hidden.shape[1]
    R = D // nb
    smem = pl.BlockSpec(memory_space=pltpu.SMEM)
    vmem = pl.BlockSpec(memory_space=pltpu.VMEM)
    hbm = pl.BlockSpec(memory_space=pl.ANY)
    sems = Comm.sems(nz, n)
    out_shape = (
        jax.ShapeDtypeStruct(hidden.shape, BF),
        jax.ShapeDtypeStruct(hidden.shape, BF),
        jax.ShapeDtypeStruct((24, D), F32),
        jax.ShapeDtypeStruct((UNITS, nz, n, n, R, D), BF),
        jax.ShapeDtypeStruct((HEADS, T, T), BF),
    )
    dma = pltpu.SemaphoreType.DMA
    scratch = [
        pltpu.VMEM((UNITS, R, D), BF),
        pltpu.VMEM((T, D), BF),
        pltpu.VMEM((T, D), BF),
        pltpu.VMEM((T, D), F32),
        pltpu.VMEM((T, D), BF),
        pltpu.VMEM((5, T, D), BF),
        pltpu.VMEM((LAYERS, D, T), BF),
        pltpu.VMEM((HEADS, T, T), BF),
        pltpu.VMEM((T, D), F32),
        pltpu.VMEM((T, FF), BF),
        pltpu.VMEM((LAYERS, T, FF), BF),
        pltpu.VMEM((LAYERS, T, D), BF),
        pltpu.VMEM((LAYERS, T, D), BF),
        pltpu.VMEM((LAYERS, T, 1), F32),
        pltpu.VMEM((LAYERS, T, 1), F32),
        pltpu.VMEM((D, T), BF),
        pltpu.VMEM((D, T), BF),
        pltpu.VMEM((D, T), BF),
        pltpu.VMEM((2, nz, n, n, 4, R, BLK), BF),
        pltpu.VMEM((24, D), F32),
        pltpu.VMEM((rounds, 24, D), F32),
        pltpu.VMEM((8, D), F32),
        dma((slots, sems)),
        dma((slots, sems)),
        dma((slots,)),
        dma((UNITS,)),
        dma((UNITS + 32,)),
        dma((2, 16)),
        dma((6,)),
        dma(()),
        dma((6,)),
        dma((2, rounds)),
    ]
    out = pl.pallas_call(
        functools.partial(kernel, nz, n, gap, slots),
        out_shape=out_shape,
        in_specs=[smem, smem, hbm, hbm, vmem, hbm, hbm, hbm, hbm] + [vmem] * 9,
        out_specs=(hbm, hbm, vmem, hbm, hbm),
        scratch_shapes=scratch,
        compiler_params=pltpu.CompilerParams(
            collective_id=0, has_side_effects=True, vmem_limit_bytes=60 * 2**20
        ),
        cost_estimate=pl.CostEstimate(flops=60 * 10**9, bytes_accessed=200 * 10**6, transcendentals=20 * 10**6),
    )(
        lengths,
        separators,
        hidden,
        cotangent,
        type_table,
        projection_weight,
        output_weight,
        inner_weight,
        outer_weight,
        query_bias,
        value_bias,
        output_bias,
        inner_bias,
        outer_bias,
        first_gain,
        first_shift,
        second_gain,
        second_shift,
    )
    by_layer = out[2][: LAYERS * 10].reshape(LAYERS, 10, D)
    return (
        out[0],
        out[1],
        by_layer[:, 0],
        by_layer[:, 1],
        by_layer[:, 2],
        by_layer[:, 3:7].reshape(LAYERS, FF),
        by_layer[:, 7],
        by_layer[:, 8],
        by_layer[:, 9],
    )


def solution(mesh):
    batched = P("batch", "blk", None)
    rows = P(None, "batch", None)
    return jax.shard_map(
        on_device,
        mesh=mesh,
        in_specs=(batched, batched, P("batch"), P("batch"), P(), rows, rows, rows, rows) + (P(),) * 9,
        out_specs=(batched, batched) + (P(),) * 7,
        check_vma=False,
    )
```

```python
import functools

import jax
import jax.numpy as jnp
from jax import lax
from jax.experimental import pallas as pl
from jax.experimental.pallas import tpu as pltpu
from jax.sharding import PartitionSpec as P

D = 1024
HEADS = 16
HEAD = 64
FF = 4096
LAYERS = 2
UNITS = 24
PER = 12
SPLIT = 640
BLK = 256
ROWS = 64
EPSILON = 1e-12
MASKED = -1000000000.0
MESH = pl.DeviceIdType.MESH
BF = jnp.bfloat16
F32 = jnp.float32


def sizes(batch):
    side = 2 ** ((batch.bit_length() - 1) // 3)
    return batch // (side * side), side


def lane(n):
    return 1 if n == 2 else 2 * (n - 1)


class Comm:
    def __init__(self, nz, n, gathered, ssem, rsem, sib_s, sib_r, slots, gap):
        self.nz, self.n, self.G = nz, n, gathered
        self.ssem, self.rsem, self.sib_s, self.sib_r = ssem, rsem, sib_s, sib_r
        self.slots, self.gap = slots, gap
        self.b = lax.axis_index("batch")
        self.c = lax.axis_index("blk")
        self.z, self.y, self.x = self.b // (n * n), (self.b // n) % n, self.b % n
        self.stages = 1 + (n - 1) + (nz - 1) + (n - 1)
        self.fbase = 2 * (nz - 1)

    @staticmethod
    def sems(nz, n):
        return 2 * (nz - 1) + 2 * nz * lane(n)

    def cols(self, core):
        return pl.ds(0, SPLIT) if core == 0 else pl.ds(SPLIT, D - SPLIT)

    def setup(self, core, par, u):
        first_x = (core == 0) == (par == 0)
        cs, g, n = self.cols(core), self.G, self.n
        self.f, self.s = (self.x, self.y) if first_x else (self.y, self.x)
        self.fstr, self.sstr = (1, n) if first_x else (n, 1)
        if first_x:
            self.sl = lambda zi, fi, si: g.at[u, zi, si, fi, :, cs]
        else:
            self.sl = lambda zi, fi, si: g.at[u, zi, fi, si, :, cs]
        self.slot = u % self.slots

    def copy(self, ref, idx, to):
        return pltpu.make_async_remote_copy(
            src_ref=ref,
            dst_ref=ref,
            send_sem=self.ssem.at[self.slot, idx],
            recv_sem=self.rsem.at[self.slot, idx],
            device_id=(to, self.c),
            device_id_type=MESH,
        )

    def dirs(self, length):
        return (0,) if length == 2 else (0, 1)

    def act(self, cp, mode):
        if mode == "start":
            cp.start()
        else:
            cp.wait_send()

    def arrive(self, ref, base, pos, length, stride, j, e, mode):
        if length == 2:
            to = self.b + stride * (1 - 2 * pos)
            if j == 0:
                self.act(self.copy(ref(pos), base, to), mode)
            elif mode == "start":
                self.copy(ref(1 - pos), base, to).wait_recv()
            return
        if j == 0:
            for d in (0, 1):

                @pl.when((pos + 1 < length) if d == 0 else (pos >= 1))
                def _():
                    self.act(self.copy(ref(pos), base + d, self.b + (stride if d == 0 else -stride)), mode)

            return
        src = pos - j if e == 0 else pos + j
        ok = (src >= 0) if e == 0 else (src < length)
        fwd = (pos + 1 < length) if e == 0 else (pos >= 1)
        to = self.b + (stride if e == 0 else -stride)
        if mode == "start":

            @pl.when(ok)
            def _():
                self.copy(ref(src), base + 2 * (j - 1) + e, to).wait_recv()

        if j < length - 1:

            @pl.when(ok & fwd)
            def _():
                self.act(self.copy(ref(src), base + 2 * j + e, to), mode)

    def hops(self):
        yield 0, 0
        for h in range(1, self.nz):
            for d in (0, 1):
                yield h, d

    def run(self, core, par, u, k, mode):
        self.setup(core, par, u)
        n, nz, z, b = self.n, self.nz, self.z, self.b
        lw = lane(n)
        sbase = self.fbase + nz * lw
        f, s = self.f, self.s
        pre = 0
        if core == 0:
            for j in range(n):
                if k is None or k == j:
                    for e in self.dirs(n) if j else (0,):
                        self.arrive(lambda i: self.sl(z, i, s), self.fbase, f, n, self.fstr, j, e, mode)
            pre = n - 1
        last = (n - 1) if core == 0 else 2 * (n - 1)
        for h, d in self.hops():
            zi = z - h if d == 0 else z + h
            fi = f if core == 1 else slice(None)

            def along_z():
                ref = self.sl(zi, fi, s)
                if h and mode == "start":
                    self.copy(ref, 2 * (h - 1) + d, b).wait_recv()
                if h < nz - 1:
                    for dd in (0, 1) if h == 0 else (d,):

                        @pl.when((z + 1 < nz) if dd == 0 else (z >= 1))
                        def _():
                            self.act(self.copy(ref, 2 * h + dd, b + (n * n if dd == 0 else -n * n)), mode)

            def in_plane(step):
                q = step
                if core == 1:
                    if step < n:
                        for e in self.dirs(n) if step else (0,):
                            self.arrive(
                                lambda i: self.sl(zi, i, s), self.fbase + zi * lw, f, n, self.fstr, step, e, mode
                            )
                    q = step - (n - 1)
                if q >= 0:
                    for e in self.dirs(n) if q else (0,):
                        self.arrive(
                            lambda i: self.sl(zi, slice(None), i), sbase + zi * lw, s, n, self.sstr, q, e, mode
                        )

            def events():
                for step in range(last + 1):
                    if k is None or k == pre + h + step:
                        if step == 0:
                            along_z()
                        in_plane(step)

            if k is None or 0 <= k - pre - h <= last:
                if h == 0:
                    events()
                else:
                    pl.when((zi >= 0) if d == 0 else (zi < nz))(events)
        if k == self.stages - 1:
            self.sibling(core, u).start()
        if k is None:
            self.sibling(core, u).wait_send()

    def sibling(self, core, u):
        ref = self.G.at[u, :, :, :, :, self.cols(core)]
        return pltpu.make_async_remote_copy(
            src_ref=ref,
            dst_ref=ref,
            send_sem=self.sib_s.at[u % self.slots],
            recv_sem=self.sib_r.at[u],
            device_id=(self.b, 1 - self.c),
            device_id_type=MESH,
        )

    def tick(self, t, part):
        order = [self.stages, *reversed(range(self.stages))]
        cut = len(order) // 2
        for core in (0, 1):

            @pl.when(self.c == core)
            def _():
                for k in order[:cut] if part == 0 else order[cut:]:
                    u = t - k * self.gap
                    for par in (0, 1):

                        @pl.when((u >= 0) & (u < UNITS) & (u % 2 == par))
                        def _():
                            if k == self.stages:
                                self.run(core, par, u, None, "drain")
                            else:
                                self.run(core, par, u, k, "start")

    def barrier(self):
        bar = pltpu.get_barrier_semaphore()
        plane, me = 2 * self.n * self.n, self.place()

        def in_plane(i, carry):
            to = (me + i) % plane
            pl.semaphore_signal(bar, inc=1, device_id=self.at(to), device_id_type=MESH)
            return carry

        def along_z(i, carry):
            pl.semaphore_signal(bar, inc=1, device_id=self.along((self.z + i) % self.nz), device_id_type=MESH)
            return carry

        lax.fori_loop(1, plane, in_plane, 0)
        lax.fori_loop(1, self.nz, along_z, 0)
        pl.semaphore_wait(bar, plane - 1 + self.nz - 1)

    def place(self):
        return (self.b % (self.n * self.n)) * 2 + self.c

    def at(self, p):
        return (self.z * self.n * self.n + p // 2, p % 2)

    def along(self, z):
        return (z * self.n * self.n + self.b % (self.n * self.n), self.c)


class Total:
    def __init__(self, comm, phase, l, lo, hi, bg, planes, part, lines, total, sems):
        self.comm, self.phase, self.l, self.rows = comm, phase, l, pl.ds(lo, hi - lo)
        self.bg, self.planes, self.part, self.lines, self.total = bg, planes, part, lines, total
        self.sems = sems

    def copies(self, second, op):
        comm, l, rows = self.comm, self.l, self.rows
        me, count = (comm.z, comm.nz) if second else (comm.place(), 2 * comm.n * comm.n)
        src, dst = (self.part, self.lines) if second else (self.bg, self.planes)

        def one(i, carry):
            peer = (me + i) % count
            to = comm.along(peer) if second else comm.at(peer)
            slot = peer if op == "wait_recv" else me
            cp = pltpu.make_async_remote_copy(
                src_ref=src.at[l, rows],
                dst_ref=dst.at[l, slot, rows],
                send_sem=self.sems[2 * second].at[self.phase, i],
                recv_sem=self.sems[2 * second + 1].at[self.phase, slot],
                device_id=to,
                device_id_type=MESH,
            )
            getattr(cp, op)()
            return carry

        lax.fori_loop(1, count, one, 0)

    def add(self, second):
        me, count = (self.comm.z, self.comm.nz) if second else (self.comm.place(), 2 * self.comm.n * self.comm.n)
        src, buf, dst = (self.part, self.lines, self.total) if second else (self.bg, self.planes, self.part)
        self.copies(second, "wait_recv")
        buf[self.l, me, self.rows] = src[self.l, self.rows]

        def one(i, acc):
            return acc + buf[self.l, i, self.rows]

        dst[self.l, self.rows] = lax.fori_loop(1, count, one, buf[self.l, 0, self.rows])
        self.copies(second, "wait_send")

    def start(self):
        self.copies(0, "start")

    def middle(self):
        self.add(0)
        self.copies(1, "start")

    def finish(self):
        self.add(1)


def dot(a, b, ca=1, cb=0):
    return lax.dot_general(a, b, (((ca,), (cb,)), ((), ())), preferred_element_type=F32)


def fold(values):
    rows, cols = values.shape
    return jnp.sum(values.reshape(rows // 8, 8, cols), axis=0)


def colsum(values):
    return jnp.sum(values, axis=0, keepdims=True)


def kernel(
    nz,
    n,
    gap,
    slots,
    lengths,
    separators,
    hidden,
    cotangent,
    type_table,
    proj,
    outw,
    inner,
    outer,
    query_bias,
    value_bias,
    output_bias,
    inner_bias,
    outer_bias,
    first_gain,
    first_shift,
    second_gain,
    second_shift,
    layer_output,
    input_gradient,
    total,
    G,
    P0,
    stg,
    xin,
    cot,
    xs,
    xb,
    qkv,
    qT,
    prob,
    mid,
    act,
    gp,
    n1,
    n2,
    r1,
    r2,
    gcT,
    dkT,
    dvT,
    wbuf,
    bg,
    planes,
    part,
    lines,
    dqs8,
    ssem,
    rsem,
    sib_s,
    sib_r,
    lsem,
    wsem,
    xsem,
    psem,
    osem,
    *asems,
):
    nb = nz * n * n
    R = D // nb
    T = xs.shape[0]
    half = T // 2
    quarter = nb // 4
    comm = Comm(nz, n, G, ssem, rsem, sib_s, sib_r, slots, gap)
    c = comm.c
    other = (comm.b, 1 - c)
    ctx = xin

    def stage_in(op):
        for l in range(LAYERS):
            for u in range(8):
                m, j = (proj, u) if u < 3 else (outw, 0) if u == 3 else (inner, u - 4)
                cp = pltpu.make_async_copy(m.at[l, :, pl.ds(j * D, D)], stg.at[l * PER + u], lsem.at[l * PER + u])
                getattr(cp, op)()
            for j in range(4):
                for g in range(4):
                    cp = pltpu.make_async_copy(
                        outer.at[l, pl.ds(g * R, R), pl.ds(j * BLK, BLK)],
                        stg.at[l * PER + 8 + j, :, pl.ds(g * BLK, BLK)],
                        lsem.at[UNITS + (l * 4 + j) * 4 + g],
                    )
                    getattr(cp, op)()

    def place(op):
        for core in (0, 1):

            @pl.when(c == core)
            def _():
                def one(u, carry):
                    cs = comm.cols(core)
                    cp = pltpu.make_async_copy(
                        stg.at[u, :, cs], G.at[u, comm.z, comm.y, comm.x, :, cs], lsem.at[u]
                    )
                    getattr(cp, op)()
                    return carry

                lax.fori_loop(0, UNITS, one, 0)

    def exchange(op):
        for i, (src, dst) in enumerate(((hidden, xin), (cotangent, cot))):
            rows = pl.ds(pl.multiple_of(c * half, half), half)
            lc = pltpu.make_async_copy(src.at[c], dst.at[rows], xsem.at[3 * i])
            rc = pltpu.make_async_remote_copy(
                src_ref=src.at[1 - c],
                dst_ref=dst.at[rows],
                send_sem=xsem.at[3 * i + 1],
                recv_sem=xsem.at[3 * i + 2],
                device_id=other,
                device_id_type=MESH,
            )
            getattr(lc, op)()
            getattr(rc, op)()

    stage_in("start")
    comm.barrier()
    exchange("start")
    stage_in("wait")
    place("start")
    place("wait")

    def row(ref, l):
        return ref[pl.ds(l, 1), :]

    def cols(i, width=BLK):
        return pl.ds(pl.multiple_of(i * width, width), width)

    lanes = lax.broadcasted_iota(jnp.int32, (T, 2 * HEAD), 1)
    halves = (lanes < HEAD, lanes >= HEAD)

    def init_x():
        exchange("wait")
        t0 = type_table[0:1, :].astype(F32)
        t1 = type_table[1:2, :].astype(F32)
        sep = separators[c]

        def rows_of(i, carry):
            rs = pl.ds(pl.multiple_of(i * ROWS, ROWS), ROWS)
            at = i * ROWS + lax.broadcasted_iota(jnp.int32, (ROWS, D), 0)
            second = (at > sep).astype(F32)
            x = xin[rs, :].astype(F32) + t0 + second * (t1 - t0)
            xs[rs, :] = x
            xb[rs, :] = x.astype(BF)
            return carry

        lax.fori_loop(0, T // ROWS, rows_of, 0)

    def load_unit(u, slot, op):
        def one(g, carry):
            cp = pltpu.make_async_copy(
                G.at[u, :, :, :, :, cols(g)], wbuf.at[slot, :, :, :, g], wsem.at[slot, g]
            )
            getattr(cp, op)()
            return carry

        lax.fori_loop(0, 4, one, 0)

    def load_rows(l, f, slot, op):
        zs = pl.ds(f * (nz // 4), nz // 4)

        def one(i, carry):
            j, g = i // 4, i % 4
            cp = pltpu.make_async_copy(
                G.at[l * PER + 8 + j, zs, :, :, :, cols(g)],
                wbuf.at[slot, pl.ds(j * (nz // 4), nz // 4), :, :, g],
                wsem.at[slot, i],
            )
            getattr(cp, op)()
            return carry

        lax.fori_loop(0, 16, one, 0)

    def w_cols(slot, g):
        return wbuf[slot, :, :, :, g].reshape(D, BLK)

    def w_rows(slot, i):
        q = nz // 4
        return jnp.concatenate(
            [wbuf[slot, pl.ds(i * q, q), :, :, g].reshape(BLK, BLK) for g in range(4)], axis=1
        )

    def o_rows(slot, i):
        if nz == 4:
            parts = [wbuf[slot, j, i // n, i % n].reshape(BLK, BLK) for j in range(4)]
        else:
            q = nz // 4
            parts = [wbuf[slot, pl.ds(j * q, q)].reshape(D, BLK)[i * BLK : (i + 1) * BLK] for j in range(4)]
        return jnp.concatenate(parts, axis=1)

    def norm_rows(z, gain, shift):
        average = jnp.mean(z, axis=1, keepdims=True)
        centred = z - average
        r = lax.rsqrt(jnp.mean(centred * centred, axis=1, keepdims=True) + EPSILON)
        normed = centred * r
        return normed, r, normed * gain + shift

    def do_qkv(l, j, slot, lo, hi):
        is_q, is_v = (j == 0).astype(F32), (j == 2).astype(F32)
        at = jnp.where(j == 0, 0, 2 * l + j)

        for g in range(lo, hi):
            sl = slice(g * BLK, (g + 1) * BLK)
            bias = query_bias[pl.ds(l, 1), sl] * is_q + value_bias[pl.ds(l, 1), sl] * is_v
            qkv[at, :, sl] = (dot(xb[...], w_cols(slot, g)) + bias).astype(BF)

    def do_attention(l, lo, hi):
        key_ok = lax.broadcasted_iota(jnp.int32, (1, T), 1) < lengths[c]

        def pair(hp, carry):
            cs = cols(hp, 2 * HEAD)
            q2, k2, v2 = qkv[0, :, cs], qkv[2 * l + 1, :, cs], qkv[2 * l + 2, :, cs]
            outs = []
            for hh in (0, 1):
                qm = jnp.where(halves[hh], q2 * BF(HEAD**-0.5), BF(0))
                s = jnp.where(key_ok, dot(qm, k2, 1, 1), MASKED)
                e = jnp.exp(s - jnp.max(s, axis=1, keepdims=True))
                p = (e * (1.0 / jnp.sum(e, axis=1, keepdims=True))).astype(BF)
                prob[2 * hp + hh] = p
                outs.append(dot(p, v2))
            ctx[:, cs] = jnp.where(halves[0], outs[0], outs[1]).astype(BF)
            qT[l, cs, :] = q2.T
            return carry

        lax.fori_loop(lo, hi, pair, 0)

    def do_out(l, slot):
        for g in range(4):
            sl = slice(g * BLK, (g + 1) * BLK)
            mid[:, sl] = xs[:, sl] + dot(ctx[...], w_cols(slot, g)) + output_bias[pl.ds(l, 1), sl]
        gain, shift = row(first_gain, l), row(first_shift, l)

        def rows_of(i, carry):
            rs = pl.ds(pl.multiple_of(i * ROWS, ROWS), ROWS)
            normed, r, y = norm_rows(mid[rs, :], gain, shift)
            n1[l, rs, :] = normed.astype(BF)
            r1[l, rs, :] = r
            mid[rs, :] = y
            xb[rs, :] = y.astype(BF)
            return carry

        lax.fori_loop(0, T // ROWS, rows_of, 0)

    def do_inner(l, lo, hi):
        def block(i, carry):
            cs = cols(i)
            h = dot(xb[...], w_cols((l * PER + 4 + i // 4) % 3, i % 4)) + inner_bias[pl.ds(l, 1), cs]
            cdf = 0.5 + 0.5 * lax.erf(h * (0.5**0.5))
            act[:, cs] = (h * cdf).astype(BF)
            gp[l, :, cs] = (cdf + h * (jnp.exp(-0.5 * h * h) * 0.3989422804014327)).astype(BF)
            return carry

        lax.fori_loop(lo, hi, block, 0)

    def do_outer(l, j, slot, part):
        cs = cols(j)
        rs = slice(part * half, (part + 1) * half)
        w = wbuf[slot].reshape(FF, BLK)
        xs[rs, cs] = mid[rs, cs] + dot(act[rs, :], w) + outer_bias[pl.ds(l, 1), cs]

    def do_norm2(l):
        gain, shift = row(second_gain, l), row(second_shift, l)

        def rows_of(i, carry):
            rs = pl.ds(pl.multiple_of(i * ROWS, ROWS), ROWS)
            normed, r, y = norm_rows(xs[rs, :], gain, shift)
            n2[l, rs, :] = normed.astype(BF)
            r2[l, rs, :] = r
            xb[rs, :] = y.astype(BF)
            xs[rs, :] = jnp.where(l == LAYERS - 1, cot[rs, :].astype(F32), y)
            return carry

        lax.fori_loop(0, T // ROWS, rows_of, 0)

    def save_prob(op):
        getattr(pltpu.make_async_copy(prob, P0, psem), op)()

    def compute(v, slot, part):
        l, k = v // PER, v % PER
        pl.when(k < 3)(lambda: do_qkv(l, k, slot, 2 * part, 2 * part + 2))

        @pl.when((k >= 2) & (k <= 4))
        def _():
            if part == 0:
                do_attention(l, jnp.where(k == 2, 0, jnp.where(k == 3, 1, 5)), jnp.where(k == 2, 0, jnp.where(k == 3, 3, 8)))
            else:
                do_attention(l, jnp.where(k == 2, 0, 3), jnp.where(k == 2, 1, jnp.where(k == 3, 5, 3)))

        if part == 1:

            @pl.when(k == 4)
            def _():
                pl.when(l == 0)(lambda: save_prob("start"))
                do_out(l, (v + 2) % 3)

        @pl.when((k >= 5) & (k < 8))
        def _():
            if part == 0:
                do_inner(l, jnp.where(k == 5, 0, 4 * (k - 4)), jnp.where(k == 5, 4, 4 * (k - 4) + 2))
            else:
                do_inner(l, jnp.where(k == 5, 4, 4 * (k - 4) + 2), 4 * (k - 4) + 4)

        pl.when(k >= 8)(lambda: do_outer(l, k - 8, slot, part))
        if part == 1:

            @pl.when(k == PER - 1)
            def _():
                pl.when(l == 0)(lambda: save_prob("wait"))
                do_norm2(l)

    lag = (comm.stages - 1) * gap + 1

    def main(t, carry):
        v = t - lag
        slot = (v + 3 * lag) % 3
        ready = (v >= 0) & (v < UNITS)

        @pl.when(ready)
        def _():
            for core in (0, 1):

                @pl.when(c == core)
                def _():
                    comm.sibling(1 - core, v).wait_recv()

            load_unit(v, slot, "start")

        comm.tick(t, 0)
        pl.when(t == 1)(init_x)

        @pl.when(ready)
        def _():
            load_unit(v, slot, "wait")
            compute(v, slot, 0)

        comm.tick(t, 1)
        pl.when(ready)(lambda: compute(v, slot, 1))

        return carry

    lax.fori_loop(0, UNITS + comm.stages * gap, main, 0)

    def results(src, out, base, op):
        mine = pl.ds(pl.multiple_of(c * half, half), half)
        theirs = pl.ds(pl.multiple_of((1 - c) * half, half), half)
        lc = pltpu.make_async_copy(src.at[mine], out.at[c], osem.at[base])
        rc = pltpu.make_async_remote_copy(
            src_ref=src.at[theirs],
            dst_ref=out.at[c],
            send_sem=osem.at[base + 1],
            recv_sem=osem.at[base + 2],
            device_id=other,
            device_id_type=MESH,
        )
        if op == "start":
            rc.start()
            lc.start()
        else:
            rc.wait_send()
            lc.wait()

    def arrived(src, out, base):
        rows = pl.ds(0, half)
        pltpu.make_async_remote_copy(
            src_ref=src.at[rows],
            dst_ref=out.at[1 - c],
            send_sem=osem.at[base + 1],
            recv_sem=osem.at[base + 2],
            device_id=other,
            device_id_type=MESH,
        ).wait_recv()

    def load(s, slot, op):
        l, k = 1 - s // PER, s % PER
        rows = (k < 8) & (k % 2 == 0)
        pl.when(rows)(lambda: load_rows(l, k // 2, slot, op))
        unit = l * PER + jnp.where(k < 8, 4 + k // 2, jnp.where(k == 8, 3, k - 9))
        pl.when(jnp.logical_not(rows))(lambda: load_unit(unit, slot, op))

    def next_weights(s):
        load(s, s % 3, "wait")
        pl.when(s + 2 < UNITS)(lambda: load(s + 2, (s + 2) % 3, "start"))
        return s % 3

    def keep_sum(l, k, values):
        for i in range(values.shape[1] // 128):
            bg[l, k, i : i + 1, :] = values[:, i * 128 : (i + 1) * 128]

    def norm_back(l, source, normed, r_ref, gain_ref, at_shift, at_bias, keep):
        gain = row(gain_ref, l)

        def rows_of(i, carry):
            sum_g, sum_z = carry
            rs = pl.ds(pl.multiple_of(i * ROWS, ROWS), ROWS)
            g = source[rs, :]
            nv = normed[l, rs, :].astype(F32)
            u = g * gain
            gz = r_ref[l, rs, :] * (
                u - jnp.mean(u, axis=1, keepdims=True) - nv * jnp.mean(u * nv, axis=1, keepdims=True)
            )
            keep[rs, :] = gz
            xb[rs, :] = gz.astype(BF)
            return sum_g + fold(g), sum_z + fold(gz)

        zero = jnp.zeros((8, D), F32)
        sum_g, sum_z = lax.fori_loop(0, T // ROWS, rows_of, (zero, zero))
        keep_sum(l, at_shift, colsum(sum_g))
        keep_sum(l, at_bias, colsum(sum_z))

    results(xb, layer_output, 0, "start")
    load(0, 0, "start")
    load(1, 1, "start")
    results(xb, layer_output, 0, "wait")

    def layer_back(i, carry):
        l = LAYERS - 1 - i
        s0 = i * PER
        norm_back(l, xs, n2, r2, second_gain, 8, 6, mid)
        pl.when(i == 1)(totals[0].start)

        def ff(f, carry):
            slot = next_weights(s0 + 2 * f)
            for i4 in range(4):
                cs = cols(f * 4 + i4)
                gh = dot(xb[...], o_rows(slot, i4), 1, 1) * gp[l, :, cs].astype(F32)
                sums = colsum(fold(gh))
                bg[l, 2 + f, 2 * i4 : 2 * i4 + 1, :] = sums[:, :128]
                bg[l, 2 + f, 2 * i4 + 1 : 2 * i4 + 2, :] = sums[:, 128:]
                act[:, cs] = gh.astype(BF)
            slot = next_weights(s0 + 2 * f + 1)
            for i4 in range(4):
                sl = slice(i4 * BLK, (i4 + 1) * BLK)
                mid[:, sl] += dot(act[:, cols(f, D)], w_rows(slot, i4), 1, 1)
            return carry

        lax.fori_loop(0, 4, ff, 0)
        pl.when(i == 1)(totals[0].middle)
        norm_back(l, mid, n1, r1, first_gain, 7, 1, mid)
        slot = next_weights(s0 + 8)
        for i4 in range(4):
            sl = slice(i4 * BLK, (i4 + 1) * BLK)
            gc = dot(xb[...], w_rows(slot, i4), 1, 1).astype(BF)
            sums = colsum(fold(gc.astype(F32)))
            bg[l, 0, 2 * i4 : 2 * i4 + 1, :] = sums[:, :128]
            bg[l, 0, 2 * i4 + 1 : 2 * i4 + 2, :] = sums[:, 128:]
            qkv[0, :, sl] = gc
            gcT[sl, :] = gc.T

        @pl.when(i == 1)
        def _():
            load_prob("wait")
            totals[0].finish()
            totals[1].start()

        def pair(hp, carry):
            cs = cols(hp, 2 * HEAD)
            gc2, k2, v2 = qkv[0, :, cs], qkv[2 * l + 1, :, cs], qkv[2 * l + 2, :, cs]
            dqs = []
            for hh in (0, 1):
                hs = pl.ds(pl.multiple_of((2 * hp + hh) * HEAD, HEAD), HEAD)
                p = prob[2 * hp + hh]
                pf = p.astype(F32)
                gm = jnp.where(halves[hh], gc2 * BF(HEAD**-0.5), BF(0))
                dp = dot(gm, v2, 1, 1)
                total = jnp.sum(dp * pf, axis=1, keepdims=True)
                ds = (pf * (dp - total)).astype(BF)
                dqs.append(dot(ds, k2))
                dkT[hs, :] = dot(qT[l, hs, :], ds).astype(BF)
                dvT[hs, :] = dot(gcT[hs, :], p).astype(BF)
            dq = jnp.where(halves[0], dqs[0], dqs[1])
            dqs8[:, cs] = fold(dq)
            ctx[:, cs] = dq.astype(BF)
            return carry

        lax.fori_loop(0, HEADS // 2, pair, 0)
        keep_sum(l, 9, colsum(dqs8[...]))

        @pl.when(i == 0)
        def _():
            load_prob("start")

        @pl.when(i == 1)
        def _():
            totals[2].start()
            totals[1].middle()


        slot = next_weights(s0 + 9)
        for i4 in range(4):
            sl = slice(i4 * BLK, (i4 + 1) * BLK)
            mid[:, sl] += dot(ctx[...], w_rows(slot, i4), 1, 1)
        slot = next_weights(s0 + 10)
        for i4 in range(4):
            sl = slice(i4 * BLK, (i4 + 1) * BLK)
            mid[:, sl] += dot(dkT[...], w_rows(slot, i4), 0, 1)
        pl.when(i == 1)(totals[2].middle)
        slot = next_weights(s0 + 11)
        for i4 in range(4):
            sl = slice(i4 * BLK, (i4 + 1) * BLK)
            y = mid[:, sl] + dot(dvT[...], w_rows(slot, i4), 0, 1)
            xs[:, sl] = y
            xb[:, sl] = y.astype(BF)
        return carry

    def load_prob(op):
        getattr(pltpu.make_async_copy(P0, prob, psem), op)()

    totals = [
        Total(comm, phase, l, lo, hi, bg, planes, part, lines, total, asems)
        for phase, (l, lo, hi) in enumerate(((1, 0, 10), (0, 0, 9), (0, 9, 10)))
    ]
    lax.fori_loop(0, LAYERS, layer_back, 0)
    results(xb, input_gradient, 3, "start")
    totals[1].finish()
    totals[2].finish()
    results(xb, input_gradient, 3, "wait")
    arrived(xb, layer_output, 0)
    arrived(xb, input_gradient, 3)


def finish(first, second, total, *rest):
    outs, (buf, into, outof) = rest[:9], rest[9:]
    half = first.shape[1] // 2
    moves = []
    for i, (src, dst) in enumerate(((first, outs[0]), (second, outs[1]))):
        for j in range(2):
            rows = pl.ds(j * half, half)
            k = 2 * i + j
            moves.append(
                (
                    pltpu.make_async_copy(src.at[:, rows], buf.at[k], into.at[k]),
                    pltpu.make_async_copy(buf.at[k], dst.at[:, rows], outof.at[k]),
                )
            )
    for here, _ in moves:
        here.start()
    for l in range(LAYERS):
        for k, out, at in (
            (9, outs[2], 0),
            (0, outs[3], 0),
            (1, outs[4], 0),
            (2, outs[5], 0),
            (3, outs[5], 1),
            (4, outs[5], 2),
            (5, outs[5], 3),
            (6, outs[6], 0),
            (7, outs[7], 0),
            (8, outs[8], 0),
        ):
            for i in range(8):
                out[l : l + 1, at * D + i * 128 : at * D + (i + 1) * 128] = total[l, k, i : i + 1, :]
    for here, there in moves:
        here.wait()
        there.start()
    for _, there in moves:
        there.wait()


def on_device(
    hidden,
    cotangent,
    lengths,
    separators,
    type_table,
    projection_weight,
    output_weight,
    inner_weight,
    outer_weight,
    query_bias,
    value_bias,
    output_bias,
    inner_bias,
    outer_bias,
    first_gain,
    first_shift,
    second_gain,
    second_shift,
):
    nb = lax.axis_size("batch")
    nz, n = sizes(nb)
    gap = 2 if nb <= 16 else 1
    stages = 1 + (n - 1) + (nz - 1) + (n - 1)
    slots = (stages + 1) * gap
    plane = 2 * n * n
    T = 2 * hidden.shape[1]
    R = D // nb
    smem = pl.BlockSpec(memory_space=pltpu.SMEM)
    vmem = pl.BlockSpec(memory_space=pltpu.VMEM)
    hbm = pl.BlockSpec(memory_space=pl.ANY)
    sems = Comm.sems(nz, n)
    out_shape = (
        jax.ShapeDtypeStruct(hidden.shape, BF),
        jax.ShapeDtypeStruct(hidden.shape, BF),
        jax.ShapeDtypeStruct((LAYERS, 10, 8, 128), F32),
        jax.ShapeDtypeStruct((UNITS, nz, n, n, R, D), BF),
        jax.ShapeDtypeStruct((HEADS, T, T), BF),
    )
    dma = pltpu.SemaphoreType.DMA
    scratch = [
        pltpu.VMEM((UNITS, R, D), BF),
        pltpu.VMEM((T, D), BF),
        pltpu.VMEM((T, D), BF),
        pltpu.VMEM((T, D), F32),
        pltpu.VMEM((T, D), BF),
        pltpu.VMEM((5, T, D), BF),
        pltpu.VMEM((LAYERS, D, T), BF),
        pltpu.VMEM((HEADS, T, T), BF),
        pltpu.VMEM((T, D), F32),
        pltpu.VMEM((T, FF), BF),
        pltpu.VMEM((LAYERS, T, FF), BF),
        pltpu.VMEM((LAYERS, T, D), BF),
        pltpu.VMEM((LAYERS, T, D), BF),
        pltpu.VMEM((LAYERS, T, 1), F32),
        pltpu.VMEM((LAYERS, T, 1), F32),
        pltpu.VMEM((D, T), BF),
        pltpu.VMEM((D, T), BF),
        pltpu.VMEM((D, T), BF),
        pltpu.VMEM((3, nz, n, n, 4, R, BLK), BF),
        pltpu.VMEM((LAYERS, 10, 8, 128), F32),
        pltpu.VMEM((LAYERS, plane, 10, 8, 128), F32),
        pltpu.VMEM((LAYERS, 10, 8, 128), F32),
        pltpu.VMEM((LAYERS, nz, 10, 8, 128), F32),
        pltpu.VMEM((8, D), F32),
        dma((slots, sems)),
        dma((slots, sems)),
        dma((slots,)),
        dma((UNITS,)),
        dma((UNITS + 32,)),
        dma((3, 16)),
        dma((6,)),
        dma(()),
        dma((6,)),
        dma((3, plane)),
        dma((3, plane)),
        dma((3, nz)),
        dma((3, nz)),
    ]
    out = pl.pallas_call(
        functools.partial(kernel, nz, n, gap, slots),
        out_shape=out_shape,
        in_specs=[smem, smem, hbm, hbm, vmem, hbm, hbm, hbm, hbm] + [vmem] * 9,
        out_specs=(hbm, hbm, vmem, hbm, hbm),
        scratch_shapes=scratch,
        compiler_params=pltpu.CompilerParams(
            collective_id=0, has_side_effects=True, vmem_limit_bytes=60 * 2**20
        ),
        cost_estimate=pl.CostEstimate(flops=60 * 10**9, bytes_accessed=200 * 10**6, transcendentals=20 * 10**6),
    )(
        lengths,
        separators,
        hidden,
        cotangent,
        type_table,
        projection_weight,
        output_weight,
        inner_weight,
        outer_weight,
        query_bias,
        value_bias,
        output_bias,
        inner_bias,
        outer_bias,
        first_gain,
        first_shift,
        second_gain,
        second_shift,
    )
    half = hidden.shape[1] // 2
    return tuple(
        pl.pallas_call(
            finish,
            out_shape=(
                jax.ShapeDtypeStruct(hidden.shape, BF),
                jax.ShapeDtypeStruct(hidden.shape, BF),
                *(jax.ShapeDtypeStruct(b.shape, F32) for b in (
                    query_bias, value_bias, output_bias, inner_bias, outer_bias, first_shift, second_shift
                )),
            ),
            in_specs=[hbm, hbm, vmem],
            out_specs=(hbm, hbm) + (vmem,) * 7,
            scratch_shapes=[pltpu.VMEM((4, 2, half, D), BF), dma((4,)), dma((4,))],
        )(out[0], out[1], out[2])
    )


def solution(mesh):
    batched = P("batch", "blk", None)
    rows = P(None, "batch", None)
    return jax.shard_map(
        on_device,
        mesh=mesh,
        in_specs=(batched, batched, P("batch"), P("batch"), P(), rows, rows, rows, rows) + (P(),) * 9,
        out_specs=(batched, batched) + (P(),) * 7,
        check_vma=False,
    )
```

```python
import functools

import jax
import jax.numpy as jnp
from jax import lax
from jax.experimental import pallas as pl
from jax.experimental.pallas import tpu as pltpu
from jax.sharding import PartitionSpec as P

D = 1024
HEADS = 16
HEAD = 64
FF = 4096
LAYERS = 2
UNITS = 24
PER = 12
SPLIT = 640
BLK = 256
ROWS = 64
EPSILON = 1e-12
MASKED = -1000000000.0
MESH = pl.DeviceIdType.MESH
BF = jnp.bfloat16
F32 = jnp.float32


def sizes(batch):
    side = 2 ** ((batch.bit_length() - 1) // 3)
    return batch // (side * side), side


def lane(n):
    return 1 if n == 2 else 2 * (n - 1)


class Comm:
    def __init__(self, nz, n, gathered, stg, ssem, rsem, sib_s, sib_r, slots, gap):
        self.nz, self.n, self.G, self.stg = nz, n, gathered, stg
        self.ssem, self.rsem, self.sib_s, self.sib_r = ssem, rsem, sib_s, sib_r
        self.slots, self.gap = slots, gap
        self.b = lax.axis_index("batch")
        self.c = lax.axis_index("blk")
        self.z, self.y, self.x = self.b // (n * n), (self.b // n) % n, self.b % n
        self.stages = 1 + (n - 1) + (nz - 1) + (n - 1)
        self.fbase = nz

    @staticmethod
    def sems(nz, n):
        return 2 * nz + 1 if n == 2 else nz + 2 * nz * lane(n)

    def cols(self, core):
        return pl.ds(0, SPLIT) if core == 0 else pl.ds(SPLIT, D - SPLIT)

    def setup(self, core, par, u):
        first_x = (core == 0) == (par == 0)
        cs, g, n = self.cols(core), self.G, self.n
        self.f, self.s = (self.x, self.y) if first_x else (self.y, self.x)
        self.fstr, self.sstr = (1, n) if first_x else (n, 1)
        if first_x:
            self.sl = lambda zi, fi, si: g.at[u, zi, si, fi, :, cs]
        else:
            self.sl = lambda zi, fi, si: g.at[u, zi, fi, si, :, cs]
        self.slot = u % self.slots

    def copy(self, ref, idx, to):
        return pltpu.make_async_remote_copy(
            src_ref=ref,
            dst_ref=ref,
            send_sem=self.ssem.at[self.slot],
            recv_sem=self.rsem.at[self.slot, idx],
            device_id=(to, self.c),
            device_id_type=MESH,
        )

    def dirs(self, length):
        return (0,) if length == 2 else (0, 1)

    def act(self, cp, mode):
        if mode == "start":
            cp.start()
        else:
            cp.wait_send()

    def arrive(self, ref, base, pos, length, stride, j, e, mode, last=False):
        if length == 2:
            to = self.b + stride * (1 - 2 * pos)
            if j == 0:
                self.act(self.copy(ref(pos), base, to), mode)
            elif mode == "start" and not last:
                self.copy(ref(1 - pos), base, to).wait_recv()
            return
        if j == 0:
            for d in (0, 1):

                @pl.when((pos + 1 < length) if d == 0 else (pos >= 1))
                def _():
                    self.act(self.copy(ref(pos), base + d, self.b + (stride if d == 0 else -stride)), mode)

            return
        src = pos - j if e == 0 else pos + j
        ok = (src >= 0) if e == 0 else (src < length)
        fwd = (pos + 1 < length) if e == 0 else (pos >= 1)
        to = self.b + (stride if e == 0 else -stride)
        if mode == "start":

            @pl.when(ok)
            def _():
                self.copy(ref(src), base + 2 * (j - 1) + e, to).wait_recv()

        if j < length - 1:

            @pl.when(ok & fwd)
            def _():
                self.act(self.copy(ref(src), base + 2 * j + e, to), mode)

    def hops(self):
        yield 0, 0
        for h in range(1, self.nz):
            for d in (0, 1):
                yield h, d

    def run(self, core, par, u, k, mode):
        self.setup(core, par, u)
        n, nz, z, b = self.n, self.nz, self.z, self.b
        lw = lane(n)
        sbase = self.fbase + nz * lw
        f, s = self.f, self.s
        pre = 0
        if core == 0:
            for j in range(n):
                if k is None or k == j:
                    for e in self.dirs(n) if j else (0,):
                        self.arrive(lambda i: self.sl(z, i, s), self.fbase, f, n, self.fstr, j, e, mode)
            pre = n - 1
        last = (n - 1) if core == 0 else 2 * (n - 1)
        for h, d in self.hops():
            zi = z - h if d == 0 else z + h
            fi = f if core == 1 else slice(None)

            def along_z():
                ref = self.sl(zi, fi, s)
                if h and mode == "start":
                    self.copy(ref, zi, b).wait_recv()
                if h < nz - 1:
                    for dd in (0, 1) if h == 0 else (d,):

                        @pl.when((z + 1 < nz) if dd == 0 else (z >= 1))
                        def _():
                            self.act(self.copy(ref, zi, b + (n * n if dd == 0 else -n * n)), mode)

            def in_plane(step):
                q = step
                if core == 1:
                    if step < n:
                        for e in self.dirs(n) if step else (0,):
                            self.arrive(
                                lambda i: self.sl(zi, i, s), self.fbase + zi * lw, f, n, self.fstr, step, e, mode
                            )
                    q = step - (n - 1)
                if q >= 0:
                    for e in self.dirs(n) if q else (0,):
                        at = sbase if n == 2 else sbase + zi * lw
                        self.arrive(lambda i: self.sl(zi, slice(None), i), at, s, n, self.sstr, q, e, mode, True)

            def events():
                for step in range(last + 1):
                    if k is None or k == pre + h + step:
                        if step == 0:
                            along_z()
                        in_plane(step)

            if k is None or 0 <= k - pre - h <= last:
                if h == 0:
                    events()
                else:
                    pl.when((zi >= 0) if d == 0 else (zi < nz))(events)
        if k == self.stages - 1:
            if n == 2:
                self.copy(self.sl(slice(None), slice(None), 1 - s), sbase, b).wait_recv()
            self.sibling(core, u).start()

    def drain(self, core, par, u):
        n, nz = self.n, self.nz
        if n == 2:
            slot, cs = u % self.slots, self.cols(core)
            for z in range(nz):
                along = (z + 1 if z < nz - 1 else 0) + (nz - z if z else 0)
                pieces = 1 + 2 * along + 2 * nz if core == 0 else along + 3 * nz
                same = self.stg.at[0:pieces, :, cs]

                @pl.when(self.z == z)
                def _():
                    pltpu.make_async_remote_copy(
                        src_ref=same,
                        dst_ref=same,
                        send_sem=self.ssem.at[slot],
                        recv_sem=self.rsem.at[slot, 0],
                        device_id=(self.b, 1 - self.c),
                        device_id_type=MESH,
                    ).wait_send()

        else:
            self.run(core, par, u, None, "drain")
        self.sibling(core, u).wait_send()

    def sibling(self, core, u):
        ref = self.G.at[u, :, :, :, :, self.cols(core)]
        return pltpu.make_async_remote_copy(
            src_ref=ref,
            dst_ref=ref,
            send_sem=self.sib_s.at[u % self.slots],
            recv_sem=self.sib_r.at[u % self.slots],
            device_id=(self.b, 1 - self.c),
            device_id_type=MESH,
        )

    def tick(self, t, part):
        order = [self.stages, *reversed(range(self.stages))]
        cut = len(order) // 2
        for core in (0, 1):

            @pl.when(self.c == core)
            def _():
                for k in order[:cut] if part == 0 else order[cut:]:
                    u = t - k * self.gap
                    for par in (0, 1):

                        @pl.when((u >= 0) & (u < UNITS) & (u % 2 == par))
                        def _():
                            if k == self.stages:
                                self.drain(core, par, u)
                            else:
                                self.run(core, par, u, k, "start")

    def barrier(self):
        bar = pltpu.get_barrier_semaphore()
        plane, me = 2 * self.n * self.n, self.place()

        def in_plane(i, carry):
            to = (me + i) % plane
            pl.semaphore_signal(bar, inc=1, device_id=self.at(to), device_id_type=MESH)
            return carry

        def along_z(i, carry):
            pl.semaphore_signal(bar, inc=1, device_id=self.along((self.z + i) % self.nz), device_id_type=MESH)
            return carry

        lax.fori_loop(1, plane, in_plane, 0)
        lax.fori_loop(1, self.nz, along_z, 0)
        pl.semaphore_wait(bar, plane - 1 + self.nz - 1)

    def place(self):
        return (self.b % (self.n * self.n)) * 2 + self.c

    def at(self, p):
        return (self.z * self.n * self.n + p // 2, p % 2)

    def along(self, z):
        return (z * self.n * self.n + self.b % (self.n * self.n), self.c)


class Total:
    def __init__(self, comm, phase, l, lo, hi, bg, planes, part, lines, total, sems):
        self.comm, self.phase, self.l, self.rows = comm, phase, l, pl.ds(lo, hi - lo)
        self.bg, self.planes, self.part, self.lines, self.total = bg, planes, part, lines, total
        self.sems = sems

    def ends(self, second):
        if second:
            return self.part, self.lines, self.comm.z, self.comm.nz
        return self.bg, self.planes, self.comm.place(), 2 * self.comm.n * self.comm.n

    def copy(self, second, src, dst, to):
        return pltpu.make_async_remote_copy(
            src_ref=src,
            dst_ref=dst,
            send_sem=self.sems.at[self.phase, 2 * second],
            recv_sem=self.sems.at[self.phase, 2 * second + 1],
            device_id=to,
            device_id_type=MESH,
        )

    def send(self, second):
        comm, l, rows = self.comm, self.l, self.rows
        src, dst, me, count = self.ends(second)

        def one(i, carry):
            peer = (me + i) % count
            to = comm.along(peer) if second else comm.at(peer)
            self.copy(second, src.at[l, rows], dst.at[l, me, rows], to).start()
            return carry

        lax.fori_loop(1, count, one, 0)

    def every(self, second):
        _, dst, _, count = self.ends(second)
        all_of = dst.at[self.l, pl.ds(0, count - 1), self.rows]
        return self.copy(second, all_of, all_of, (self.comm.b, 1 - self.comm.c))

    def add(self, second):
        src, buf, me, count = self.ends(second)
        out = self.total if second else self.part
        self.every(second).wait_recv()
        buf[self.l, me, self.rows] = src[self.l, self.rows]

        def one(i, acc):
            return acc + buf[self.l, i, self.rows]

        out[self.l, self.rows] = lax.fori_loop(1, count, one, buf[self.l, 0, self.rows])
        self.every(second).wait_send()

    def start(self):
        self.send(0)

    def middle(self):
        self.add(0)
        self.send(1)

    def finish(self):
        self.add(1)


def dot(a, b, ca=1, cb=0):
    return lax.dot_general(a, b, (((ca,), (cb,)), ((), ())), preferred_element_type=F32)


def fold(values):
    rows, cols = values.shape
    return jnp.sum(values.reshape(rows // 8, 8, cols), axis=0)


def colsum(values):
    return jnp.sum(values, axis=0, keepdims=True)


def kernel(
    nz,
    n,
    gap,
    slots,
    lengths,
    separators,
    hidden,
    cotangent,
    type_table_in,
    proj,
    outw,
    inner,
    outer,
    query_bias_in,
    value_bias_in,
    output_bias_in,
    inner_bias_in,
    outer_bias_in,
    first_gain_in,
    first_shift_in,
    second_gain_in,
    second_shift_in,
    layer_output,
    input_gradient,
    total,
    G,
    P0,
    type_table,
    query_bias,
    value_bias,
    output_bias,
    inner_bias,
    outer_bias,
    first_gain,
    first_shift,
    second_gain,
    second_shift,
    stg,
    xin,
    cot,
    xs,
    xb,
    qkv,
    qT,
    prob,
    mid,
    act,
    gp,
    n1,
    n2,
    r1,
    r2,
    gcT,
    dkT,
    dvT,
    wbuf,
    bg,
    planes,
    part,
    lines,
    dqs8,
    ssem,
    rsem,
    sib_s,
    sib_r,
    lsem,
    wsem,
    xsem,
    psem,
    vsem,
    osem,
    asems,
):
    nb = nz * n * n
    R = D // nb
    T = xs.shape[0]
    half = T // 2
    quarter = nb // 4
    comm = Comm(nz, n, G, stg, ssem, rsem, sib_s, sib_r, slots, gap)
    c = comm.c
    other = (comm.b, 1 - c)
    ctx = xin

    def stage_in():
        for l in range(LAYERS):
            for u in range(8):
                m, j = (proj, u) if u < 3 else (outw, 0) if u == 3 else (inner, u - 4)
                pltpu.make_async_copy(m.at[l, :, pl.ds(j * D, D)], stg.at[l * PER + u], lsem.at[0]).start()
            for j in range(4):
                for g in range(4):
                    pltpu.make_async_copy(
                        outer.at[l, pl.ds(g * R, R), pl.ds(j * BLK, BLK)],
                        stg.at[l * PER + 8 + j, :, pl.ds(g * BLK, BLK)],
                        lsem.at[0],
                    ).start()

    def place():
        pltpu.make_async_copy(stg, stg, lsem.at[0]).wait()
        for core in (0, 1):

            @pl.when(c == core)
            def _():
                cs = comm.cols(core)
                to = G.at[:, comm.z, comm.y, comm.x, :, cs]
                cp = pltpu.make_async_copy(stg.at[:, :, cs], to, lsem.at[1])
                cp.start()
                cp.wait()

    def exchange(op):
        for i, (src, dst) in enumerate(((hidden, xin), (cotangent, cot))):
            rows = pl.ds(pl.multiple_of(c * half, half), half)
            lc = pltpu.make_async_copy(src.at[c], dst.at[rows], xsem.at[3 * i])
            rc = pltpu.make_async_remote_copy(
                src_ref=src.at[1 - c],
                dst_ref=dst.at[rows],
                send_sem=xsem.at[3 * i + 1],
                recv_sem=xsem.at[3 * i + 2],
                device_id=other,
                device_id_type=MESH,
            )
            getattr(lc, op)()
            getattr(rc, op)()

    vectors = (
        (type_table_in, type_table),
        (query_bias_in, query_bias),
        (value_bias_in, value_bias),
        (output_bias_in, output_bias),
        (inner_bias_in, inner_bias),
        (outer_bias_in, outer_bias),
        (first_gain_in, first_gain),
        (first_shift_in, first_shift),
        (second_gain_in, second_gain),
        (second_shift_in, second_shift),
    )

    def small(op):
        for i, (src, dst) in enumerate(vectors):
            getattr(pltpu.make_async_copy(src, dst, vsem.at[i]), op)()

    stage_in()
    small("start")
    comm.barrier()
    exchange("start")
    place()

    def row(ref, l):
        return ref[pl.ds(l, 1), :]

    def cols(i, width=BLK):
        return pl.ds(pl.multiple_of(i * width, width), width)

    lanes = lax.broadcasted_iota(jnp.int32, (T, 2 * HEAD), 1)
    halves = (lanes < HEAD, lanes >= HEAD)

    def init_x():
        exchange("wait")
        small("wait")
        t0 = type_table[0:1, :].astype(F32)
        t1 = type_table[1:2, :].astype(F32)
        sep = separators[c]

        def rows_of(i, carry):
            rs = pl.ds(pl.multiple_of(i * ROWS, ROWS), ROWS)
            at = i * ROWS + lax.broadcasted_iota(jnp.int32, (ROWS, D), 0)
            second = (at > sep).astype(F32)
            x = xin[rs, :].astype(F32) + t0 + second * (t1 - t0)
            xs[rs, :] = x
            xb[rs, :] = x.astype(BF)
            return carry

        lax.fori_loop(0, T // ROWS, rows_of, 0)

    def load_unit(u, slot):
        pltpu.make_async_copy(G.at[u], wbuf.at[slot], wsem.at[slot]).start()

    def load_rows(l, f, slot):
        q = nz // 4
        for j in range(4):
            pltpu.make_async_copy(
                G.at[l * PER + 8 + j, pl.ds(f * q, q)], wbuf.at[slot, pl.ds(j * q, q)], wsem.at[slot]
            ).start()

    def loaded(slot):
        pltpu.make_async_copy(G.at[0], wbuf.at[slot], wsem.at[slot]).wait()

    def w_cols(slot, g):
        return wbuf[slot, :, :, :, :, cols(g)].reshape(D, BLK)

    def w_rows(slot, i):
        return wbuf[slot, pl.ds(i * (nz // 4), nz // 4)].reshape(BLK, D)

    def stacked(chips):
        return jnp.concatenate([w[:, g * BLK : (g + 1) * BLK] for w in chips for g in range(4)], axis=0)

    def chip(slot, i):
        return wbuf[slot, i // (n * n), (i // n) % n, i % n]

    def o_rows(slot, i):
        per = nb // 16
        return jnp.concatenate(
            [stacked([chip(slot, j * quarter + i * per + w) for w in range(per)]) for j in range(4)], axis=1
        )

    def o_cols(slot, i):
        return stacked([chip(slot, i * quarter + w) for w in range(quarter)])

    def norm_rows(z, gain, shift):
        average = jnp.mean(z, axis=1, keepdims=True)
        centred = z - average
        r = lax.rsqrt(jnp.mean(centred * centred, axis=1, keepdims=True) + EPSILON)
        normed = centred * r
        return normed, r, normed * gain + shift

    def do_qkv(l, j, slot, lo, hi):
        is_q, is_v = (j == 0).astype(F32), (j == 2).astype(F32)
        at = jnp.where(j == 0, 0, 2 * l + j)

        for g in range(lo, hi):
            sl = slice(g * BLK, (g + 1) * BLK)
            bias = query_bias[pl.ds(l, 1), sl] * is_q + value_bias[pl.ds(l, 1), sl] * is_v
            qkv[at, :, sl] = (dot(xb[...], w_cols(slot, g)) + bias).astype(BF)

    def do_attention(l, lo, hi):
        key_ok = lax.broadcasted_iota(jnp.int32, (1, T), 1) < lengths[c]

        def pair(hp, carry):
            cs = cols(hp, 2 * HEAD)
            q2, k2, v2 = qkv[0, :, cs], qkv[2 * l + 1, :, cs], qkv[2 * l + 2, :, cs]
            outs = []
            for hh in (0, 1):
                qm = jnp.where(halves[hh], q2 * BF(HEAD**-0.5), BF(0))
                s = jnp.where(key_ok, dot(qm, k2, 1, 1), MASKED)
                e = jnp.exp(s - jnp.max(s, axis=1, keepdims=True))
                p = (e * (1.0 / jnp.sum(e, axis=1, keepdims=True))).astype(BF)
                prob[2 * hp + hh] = p
                outs.append(dot(p, v2))
            ctx[:, cs] = jnp.where(halves[0], outs[0], outs[1]).astype(BF)
            qT[l, cs, :] = q2.T
            return carry

        lax.fori_loop(lo, hi, pair, 0)

    def do_out(l, slot):
        for g in range(4):
            sl = slice(g * BLK, (g + 1) * BLK)
            mid[:, sl] = xs[:, sl] + dot(ctx[...], w_cols(slot, g)) + output_bias[pl.ds(l, 1), sl]
        gain, shift = row(first_gain, l), row(first_shift, l)

        def rows_of(i, carry):
            rs = pl.ds(pl.multiple_of(i * ROWS, ROWS), ROWS)
            normed, r, y = norm_rows(mid[rs, :], gain, shift)
            n1[l, rs, :] = normed.astype(BF)
            r1[l, rs, :] = r
            mid[rs, :] = y
            xb[rs, :] = y.astype(BF)
            return carry

        lax.fori_loop(0, T // ROWS, rows_of, 0)

    def do_inner(l, lo, hi):
        def block(i, carry):
            cs = cols(i)
            h = dot(xb[...], w_cols((l * PER + 4 + i // 4) % 3, i % 4)) + inner_bias[pl.ds(l, 1), cs]
            cdf = 0.5 + 0.5 * lax.erf(h * (0.5**0.5))
            act[:, cs] = (h * cdf).astype(BF)
            gp[l, :, cs] = (cdf + h * (jnp.exp(-0.5 * h * h) * 0.3989422804014327)).astype(BF)
            return carry

        lax.fori_loop(lo, hi, block, 0)

    def do_outer(l, j, slot, part):
        cs = cols(j)
        rs = slice(part * half, (part + 1) * half)
        y = mid[rs, cs] + outer_bias[pl.ds(l, 1), cs]
        for i in range(4):
            y = y + dot(act[rs, i * D : (i + 1) * D], o_cols(slot, i))
        xs[rs, cs] = y

    def do_norm2(l):
        gain, shift = row(second_gain, l), row(second_shift, l)

        def rows_of(i, carry):
            rs = pl.ds(pl.multiple_of(i * ROWS, ROWS), ROWS)
            normed, r, y = norm_rows(xs[rs, :], gain, shift)
            n2[l, rs, :] = normed.astype(BF)
            r2[l, rs, :] = r
            yb = y.astype(BF)
            xb[rs, :] = yb
            ctx[rs, :] = yb
            xs[rs, :] = jnp.where(l == LAYERS - 1, cot[rs, :].astype(F32), y)
            return carry

        lax.fori_loop(0, T // ROWS, rows_of, 0)

    def save_prob(op):
        getattr(pltpu.make_async_copy(prob, P0, psem), op)()

    def compute(v, slot, part):
        l, k = v // PER, v % PER
        pl.when(k < 3)(lambda: do_qkv(l, k, slot, 2 * part, 2 * part + 2))

        @pl.when((k >= 2) & (k <= 4))
        def _():
            if part == 0:
                do_attention(l, jnp.where(k == 2, 0, jnp.where(k == 3, 1, 5)), jnp.where(k == 2, 0, jnp.where(k == 3, 3, 8)))
            else:
                do_attention(l, jnp.where(k == 2, 0, 3), jnp.where(k == 2, 1, jnp.where(k == 3, 5, 3)))

        if part == 1:

            @pl.when(k == 4)
            def _():
                pl.when(l == 0)(lambda: save_prob("start"))
                do_out(l, (v + 2) % 3)

        @pl.when((k >= 5) & (k < 8))
        def _():
            if part == 0:
                do_inner(l, jnp.where(k == 5, 0, 4 * (k - 4)), jnp.where(k == 5, 4, 4 * (k - 4) + 2))
            else:
                do_inner(l, jnp.where(k == 5, 4, 4 * (k - 4) + 2), 4 * (k - 4) + 4)

        pl.when(k >= 8)(lambda: do_outer(l, k - 8, slot, part))
        if part == 1:

            @pl.when(k == PER - 1)
            def _():
                pl.when(l == 0)(lambda: save_prob("wait"))
                do_norm2(l)

    def load(s, slot):
        l, k = 1 - s // PER, s % PER
        rows = (k < 8) & (k % 2 == 0)
        pl.when(rows)(lambda: load_rows(l, k // 2, slot))
        unit = l * PER + jnp.where(k < 8, 4 + k // 2, jnp.where(k == 8, 3, k - 9))
        pl.when(jnp.logical_not(rows))(lambda: load_unit(unit, slot))

    lag = (comm.stages - 1) * gap + 1

    def main(t, carry):
        v = t - lag
        slot = (v + 3 * lag) % 3
        ready = (v >= 0) & (v < UNITS)

        @pl.when(ready)
        def _():
            for core in (0, 1):

                @pl.when(c == core)
                def _():
                    comm.sibling(1 - core, v).wait_recv()

            load_unit(v, slot)

        comm.tick(t, 0)
        pl.when(t == 1)(init_x)

        @pl.when(ready)
        def _():
            loaded(slot)

            @pl.when(v == UNITS - 1)
            def _():
                load(0, 0)
                load(1, 1)

            compute(v, slot, 0)

        comm.tick(t, 1)
        pl.when(ready)(lambda: compute(v, slot, 1))

        return carry

    lax.fori_loop(0, UNITS + comm.stages * gap, main, 0)

    def results(src, out, base, op):
        mine = pl.ds(pl.multiple_of(c * half, half), half)
        theirs = pl.ds(pl.multiple_of((1 - c) * half, half), half)
        lc = pltpu.make_async_copy(src.at[mine], out.at[c], osem.at[base])
        rc = pltpu.make_async_remote_copy(
            src_ref=src.at[theirs],
            dst_ref=out.at[c],
            send_sem=osem.at[base + 1],
            recv_sem=osem.at[base + 2],
            device_id=other,
            device_id_type=MESH,
        )
        if op == "start":
            rc.start()
            lc.start()
        else:
            rc.wait_send()
            lc.wait()

    def arrived(src, out, base):
        rows = pl.ds(0, half)
        pltpu.make_async_remote_copy(
            src_ref=src.at[rows],
            dst_ref=out.at[1 - c],
            send_sem=osem.at[base + 1],
            recv_sem=osem.at[base + 2],
            device_id=other,
            device_id_type=MESH,
        ).wait_recv()

    def next_weights(s):
        loaded(s % 3)
        pl.when(s + 2 < UNITS)(lambda: load(s + 2, (s + 2) % 3))
        return s % 3

    def keep_sum(l, k, values):
        for i in range(values.shape[1] // 128):
            bg[l, k, i : i + 1, :] = values[:, i * 128 : (i + 1) * 128]

    def norm_back(l, source, normed, r_ref, gain_ref, at_shift, at_bias, keep):
        gain = row(gain_ref, l)

        def rows_of(i, carry):
            sum_g, sum_z = carry
            rs = pl.ds(pl.multiple_of(i * ROWS, ROWS), ROWS)
            g = source[rs, :]
            nv = normed[l, rs, :].astype(F32)
            u = g * gain
            gz = r_ref[l, rs, :] * (
                u - jnp.mean(u, axis=1, keepdims=True) - nv * jnp.mean(u * nv, axis=1, keepdims=True)
            )
            keep[rs, :] = gz
            xb[rs, :] = gz.astype(BF)
            return sum_g + fold(g), sum_z + fold(gz)

        zero = jnp.zeros((8, D), F32)
        sum_g, sum_z = lax.fori_loop(0, T // ROWS, rows_of, (zero, zero))
        keep_sum(l, at_shift, colsum(sum_g))
        keep_sum(l, at_bias, colsum(sum_z))

    results(ctx, layer_output, 0, "start")

    def layer_back(i, carry):
        l = LAYERS - 1 - i
        s0 = i * PER
        norm_back(l, xs, n2, r2, second_gain, 8, 6, mid)
        pl.when(i == 1)(totals[0].start)

        def ff(f, carry):
            slot = next_weights(s0 + 2 * f)
            for i4 in range(4):
                cs = cols(f * 4 + i4)
                gh = dot(xb[...], o_rows(slot, i4), 1, 1) * gp[l, :, cs].astype(F32)
                sums = colsum(fold(gh))
                bg[l, 2 + f, 2 * i4 : 2 * i4 + 1, :] = sums[:, :128]
                bg[l, 2 + f, 2 * i4 + 1 : 2 * i4 + 2, :] = sums[:, 128:]
                act[:, cs] = gh.astype(BF)
            slot = next_weights(s0 + 2 * f + 1)
            for i4 in range(4):
                sl = slice(i4 * BLK, (i4 + 1) * BLK)
                mid[:, sl] += dot(act[:, cols(f, D)], w_rows(slot, i4), 1, 1)
            return carry

        lax.fori_loop(0, 4, ff, 0)
        pl.when(i == 1)(totals[0].middle)
        norm_back(l, mid, n1, r1, first_gain, 7, 1, mid)
        slot = next_weights(s0 + 8)
        for i4 in range(4):
            sl = slice(i4 * BLK, (i4 + 1) * BLK)
            gc = dot(xb[...], w_rows(slot, i4), 1, 1).astype(BF)
            sums = colsum(fold(gc.astype(F32)))
            bg[l, 0, 2 * i4 : 2 * i4 + 1, :] = sums[:, :128]
            bg[l, 0, 2 * i4 + 1 : 2 * i4 + 2, :] = sums[:, 128:]
            qkv[0, :, sl] = gc
            gcT[sl, :] = gc.T

        pl.when(i == 0)(lambda: results(ctx, layer_output, 0, "wait"))

        @pl.when(i == 1)
        def _():
            load_prob("wait")
            totals[0].finish()
            totals[1].start()

        def pair(hp, carry):
            cs = cols(hp, 2 * HEAD)
            gc2, k2, v2 = qkv[0, :, cs], qkv[2 * l + 1, :, cs], qkv[2 * l + 2, :, cs]
            dqs = []
            for hh in (0, 1):
                hs = pl.ds(pl.multiple_of((2 * hp + hh) * HEAD, HEAD), HEAD)
                p = prob[2 * hp + hh]
                pf = p.astype(F32)
                gm = jnp.where(halves[hh], gc2 * BF(HEAD**-0.5), BF(0))
                dp = dot(gm, v2, 1, 1)
                total = jnp.sum(dp * pf, axis=1, keepdims=True)
                ds = (pf * (dp - total)).astype(BF)
                dqs.append(dot(ds, k2))
                dkT[hs, :] = dot(qT[l, hs, :], ds).astype(BF)
                dvT[hs, :] = dot(gcT[hs, :], p).astype(BF)
            dq = jnp.where(halves[0], dqs[0], dqs[1])
            dqs8[:, cs] = fold(dq)
            ctx[:, cs] = dq.astype(BF)
            return carry

        lax.fori_loop(0, HEADS // 2, pair, 0)
        keep_sum(l, 9, colsum(dqs8[...]))

        @pl.when(i == 0)
        def _():
            load_prob("start")

        @pl.when(i == 1)
        def _():
            totals[2].start()
            totals[1].middle()


        slot = next_weights(s0 + 9)
        for i4 in range(4):
            sl = slice(i4 * BLK, (i4 + 1) * BLK)
            mid[:, sl] += dot(ctx[...], w_rows(slot, i4), 1, 1)
        slot = next_weights(s0 + 10)
        for i4 in range(4):
            sl = slice(i4 * BLK, (i4 + 1) * BLK)
            mid[:, sl] += dot(dkT[...], w_rows(slot, i4), 0, 1)
        pl.when(i == 1)(totals[2].middle)
        slot = next_weights(s0 + 11)
        for i4 in range(4):
            sl = slice(i4 * BLK, (i4 + 1) * BLK)
            y = mid[:, sl] + dot(dvT[...], w_rows(slot, i4), 0, 1)
            xs[:, sl] = y
            xb[:, sl] = y.astype(BF)
        return carry

    def load_prob(op):
        getattr(pltpu.make_async_copy(P0, prob, psem), op)()

    totals = [
        Total(comm, phase, l, lo, hi, bg, planes, part, lines, total, asems)
        for phase, (l, lo, hi) in enumerate(((1, 0, 10), (0, 0, 9), (0, 9, 10)))
    ]
    lax.fori_loop(0, LAYERS, layer_back, 0)
    results(xb, input_gradient, 3, "start")
    totals[1].finish()
    totals[2].finish()
    results(xb, input_gradient, 3, "wait")
    arrived(xb, layer_output, 0)
    arrived(xb, input_gradient, 3)


def finish(first, second, total, *rest):
    outs, (buf, into, outof) = rest[:9], rest[9:]
    half = first.shape[1] // 2
    moves = []
    for i, (src, dst) in enumerate(((first, outs[0]), (second, outs[1]))):
        for j in range(2):
            rows = pl.ds(j * half, half)
            k = 2 * i + j
            moves.append(
                (
                    pltpu.make_async_copy(src.at[:, rows], buf.at[k], into.at[k]),
                    pltpu.make_async_copy(buf.at[k], dst.at[:, rows], outof.at[k]),
                )
            )
    for here, _ in moves:
        here.start()
    for l in range(LAYERS):
        for k, out, at in (
            (9, outs[2], 0),
            (0, outs[3], 0),
            (1, outs[4], 0),
            (2, outs[5], 0),
            (3, outs[5], 1),
            (4, outs[5], 2),
            (5, outs[5], 3),
            (6, outs[6], 0),
            (7, outs[7], 0),
            (8, outs[8], 0),
        ):
            for i in range(8):
                out[l : l + 1, at * D + i * 128 : at * D + (i + 1) * 128] = total[l, k, i : i + 1, :]
    for here, there in moves:
        here.wait()
        there.start()
    for _, there in moves:
        there.wait()


def on_device(
    hidden,
    cotangent,
    lengths,
    separators,
    type_table,
    projection_weight,
    output_weight,
    inner_weight,
    outer_weight,
    query_bias,
    value_bias,
    output_bias,
    inner_bias,
    outer_bias,
    first_gain,
    first_shift,
    second_gain,
    second_shift,
):
    nb = lax.axis_size("batch")
    nz, n = sizes(nb)
    gap = 2 if nb <= 16 else 1
    stages = 1 + (n - 1) + (nz - 1) + (n - 1)
    slots = (stages + 1) * gap
    plane = 2 * n * n
    T = 2 * hidden.shape[1]
    R = D // nb
    smem = pl.BlockSpec(memory_space=pltpu.SMEM)
    vmem = pl.BlockSpec(memory_space=pltpu.VMEM)
    hbm = pl.BlockSpec(memory_space=pl.ANY)
    sems = Comm.sems(nz, n)
    out_shape = (
        jax.ShapeDtypeStruct(hidden.shape, BF),
        jax.ShapeDtypeStruct(hidden.shape, BF),
        jax.ShapeDtypeStruct((LAYERS, 10, 8, 128), F32),
        jax.ShapeDtypeStruct((UNITS, nz, n, n, R, D), BF),
        jax.ShapeDtypeStruct((HEADS, T, T), BF),
    )
    dma = pltpu.SemaphoreType.DMA
    scratch = [
        pltpu.VMEM((2, D), BF),
        *(pltpu.VMEM((LAYERS, w), F32) for w in (D, D, D, FF, D, D, D, D, D)),
        pltpu.VMEM((UNITS, R, D), BF),
        pltpu.VMEM((T, D), BF),
        pltpu.VMEM((T, D), BF),
        pltpu.VMEM((T, D), F32),
        pltpu.VMEM((T, D), BF),
        pltpu.VMEM((5, T, D), BF),
        pltpu.VMEM((LAYERS, D, T), BF),
        pltpu.VMEM((HEADS, T, T), BF),
        pltpu.VMEM((T, D), F32),
        pltpu.VMEM((T, FF), BF),
        pltpu.VMEM((LAYERS, T, FF), BF),
        pltpu.VMEM((LAYERS, T, D), BF),
        pltpu.VMEM((LAYERS, T, D), BF),
        pltpu.VMEM((LAYERS, T, 1), F32),
        pltpu.VMEM((LAYERS, T, 1), F32),
        pltpu.VMEM((D, T), BF),
        pltpu.VMEM((D, T), BF),
        pltpu.VMEM((D, T), BF),
        pltpu.VMEM((3, nz, n, n, R, D), BF),
        pltpu.VMEM((LAYERS, 10, 8, 128), F32),
        pltpu.VMEM((LAYERS, plane, 10, 8, 128), F32),
        pltpu.VMEM((LAYERS, 10, 8, 128), F32),
        pltpu.VMEM((LAYERS, nz, 10, 8, 128), F32),
        pltpu.VMEM((8, D), F32),
        dma((slots,)),
        dma((slots, sems)),
        dma((slots,)),
        dma((slots,)),
        dma((2,)),
        dma((3,)),
        dma((6,)),
        dma(()),
        dma((10,)),
        dma((6,)),
        dma((3, 4)),
    ]
    out = pl.pallas_call(
        functools.partial(kernel, nz, n, gap, slots),
        out_shape=out_shape,
        in_specs=[smem, smem] + [hbm] * 16,
        out_specs=(hbm, hbm, vmem, hbm, hbm),
        scratch_shapes=scratch,
        compiler_params=pltpu.CompilerParams(
            collective_id=0, has_side_effects=True, vmem_limit_bytes=60 * 2**20
        ),
        cost_estimate=pl.CostEstimate(flops=60 * 10**9, bytes_accessed=200 * 10**6, transcendentals=20 * 10**6),
    )(
        lengths,
        separators,
        hidden,
        cotangent,
        type_table,
        projection_weight,
        output_weight,
        inner_weight,
        outer_weight,
        query_bias,
        value_bias,
        output_bias,
        inner_bias,
        outer_bias,
        first_gain,
        first_shift,
        second_gain,
        second_shift,
    )
    half = hidden.shape[1] // 2
    return tuple(
        pl.pallas_call(
            finish,
            out_shape=(
                jax.ShapeDtypeStruct(hidden.shape, BF),
                jax.ShapeDtypeStruct(hidden.shape, BF),
                *(jax.ShapeDtypeStruct(b.shape, F32) for b in (
                    query_bias, value_bias, output_bias, inner_bias, outer_bias, first_shift, second_shift
                )),
            ),
            in_specs=[hbm, hbm, vmem],
            out_specs=(hbm, hbm) + (vmem,) * 7,
            scratch_shapes=[pltpu.VMEM((4, 2, half, D), BF), dma((4,)), dma((4,))],
        )(out[0], out[1], out[2])
    )


def solution(mesh):
    batched = P("batch", "blk", None)
    rows = P(None, "batch", None)
    return jax.shard_map(
        on_device,
        mesh=mesh,
        in_specs=(batched, batched, P("batch"), P("batch"), P(), rows, rows, rows, rows) + (P(),) * 9,
        out_specs=(batched, batched) + (P(),) * 7,
        check_vma=False,
    )
```

```python
import functools

import jax
import jax.numpy as jnp
from jax import lax
from jax.experimental import pallas as pl
from jax.experimental.pallas import tpu as pltpu
from jax.sharding import PartitionSpec as P

D = 1024
HEADS = 16
HEAD = 64
FF = 4096
LAYERS = 2
UNITS = 24
PER = 12
SPLIT = 640
BLK = 256
ROWS = 256
EPSILON = 1e-12
MASKED = -1000000000.0
MESH = pl.DeviceIdType.MESH
BF = jnp.bfloat16
F32 = jnp.float32


def sizes(batch):
    side = 2 ** ((batch.bit_length() - 1) // 3)
    return batch // (side * side), side


def lane(n):
    return 1 if n == 2 else 2 * (n - 1)


class Comm:
    def __init__(self, nz, n, gathered, stg, ssem, rsem, sib_s, sib_r, slots, gap):
        self.nz, self.n, self.G, self.stg = nz, n, gathered, stg
        self.ssem, self.rsem, self.sib_s, self.sib_r = ssem, rsem, sib_s, sib_r
        self.slots, self.gap = slots, gap
        self.b = lax.axis_index("batch")
        self.c = lax.axis_index("blk")
        self.z, self.y, self.x = self.b // (n * n), (self.b // n) % n, self.b % n
        self.stages = 1 + (n - 1) + (nz - 1) + (n - 1)
        self.fbase = nz

    @staticmethod
    def sems(nz, n):
        return 2 * nz + 1 if n == 2 else nz + 2 * nz * lane(n)

    def cols(self, core):
        return pl.ds(0, SPLIT) if core == 0 else pl.ds(SPLIT, D - SPLIT)

    def setup(self, core, par, u):
        first_x = (core == 0) == (par == 0)
        cs, g, n = self.cols(core), self.G, self.n
        self.f, self.s = (self.x, self.y) if first_x else (self.y, self.x)
        self.fstr, self.sstr = (1, n) if first_x else (n, 1)
        if first_x:
            self.sl = lambda zi, fi, si: g.at[u, zi, si, fi, :, cs]
        else:
            self.sl = lambda zi, fi, si: g.at[u, zi, fi, si, :, cs]
        self.slot = u % self.slots

    def copy(self, ref, idx, to):
        return pltpu.make_async_remote_copy(
            src_ref=ref,
            dst_ref=ref,
            send_sem=self.ssem.at[self.slot],
            recv_sem=self.rsem.at[self.slot, idx],
            device_id=(to, self.c),
            device_id_type=MESH,
        )

    def dirs(self, length):
        return (0,) if length == 2 else (0, 1)

    def act(self, cp, mode):
        if mode == "start":
            cp.start()
        else:
            cp.wait_send()

    def arrive(self, ref, base, pos, length, stride, j, e, mode, last=False):
        if length == 2:
            to = self.b + stride * (1 - 2 * pos)
            if j == 0:
                self.act(self.copy(ref(pos), base, to), mode)
            elif mode == "start" and not last:
                self.copy(ref(1 - pos), base, to).wait_recv()
            return
        if j == 0:
            for d in (0, 1):

                @pl.when((pos + 1 < length) if d == 0 else (pos >= 1))
                def _():
                    self.act(self.copy(ref(pos), base + d, self.b + (stride if d == 0 else -stride)), mode)

            return
        src = pos - j if e == 0 else pos + j
        ok = (src >= 0) if e == 0 else (src < length)
        fwd = (pos + 1 < length) if e == 0 else (pos >= 1)
        to = self.b + (stride if e == 0 else -stride)
        if mode == "start":

            @pl.when(ok)
            def _():
                self.copy(ref(src), base + 2 * (j - 1) + e, to).wait_recv()

        if j < length - 1:

            @pl.when(ok & fwd)
            def _():
                self.act(self.copy(ref(src), base + 2 * j + e, to), mode)

    def hops(self):
        yield 0, 0
        for h in range(1, self.nz):
            for d in (0, 1):
                yield h, d

    def run(self, core, par, u, k, mode):
        self.setup(core, par, u)
        n, nz, z, b = self.n, self.nz, self.z, self.b
        lw = lane(n)
        sbase = self.fbase + nz * lw
        f, s = self.f, self.s
        pre = 0
        if core == 0:
            for j in range(n):
                if k is None or k == j:
                    for e in self.dirs(n) if j else (0,):
                        self.arrive(lambda i: self.sl(z, i, s), self.fbase, f, n, self.fstr, j, e, mode)
            pre = n - 1
        last = (n - 1) if core == 0 else 2 * (n - 1)
        for h, d in self.hops():
            zi = z - h if d == 0 else z + h
            fi = f if core == 1 else slice(None)

            def along_z():
                ref = self.sl(zi, fi, s)
                if h and mode == "start":
                    self.copy(ref, zi, b).wait_recv()
                if h < nz - 1:
                    for dd in (0, 1) if h == 0 else (d,):

                        @pl.when((z + 1 < nz) if dd == 0 else (z >= 1))
                        def _():
                            self.act(self.copy(ref, zi, b + (n * n if dd == 0 else -n * n)), mode)

            def in_plane(step):
                q = step
                if core == 1:
                    if step < n:
                        for e in self.dirs(n) if step else (0,):
                            self.arrive(
                                lambda i: self.sl(zi, i, s), self.fbase + zi * lw, f, n, self.fstr, step, e, mode
                            )
                    q = step - (n - 1)
                if q >= 0:
                    for e in self.dirs(n) if q else (0,):
                        at = sbase if n == 2 else sbase + zi * lw
                        self.arrive(lambda i: self.sl(zi, slice(None), i), at, s, n, self.sstr, q, e, mode, True)

            def events():
                for step in range(last + 1):
                    if k is None or k == pre + h + step:
                        if step == 0:
                            along_z()
                        in_plane(step)

            if k is None or 0 <= k - pre - h <= last:
                if h == 0:
                    events()
                else:
                    pl.when((zi >= 0) if d == 0 else (zi < nz))(events)
        if k == self.stages - 1:
            if n == 2:
                self.copy(self.sl(slice(None), slice(None), 1 - s), sbase, b).wait_recv()
            self.sibling(core, u).start()

    def drain(self, core, par, u):
        n, nz = self.n, self.nz
        if n == 2:
            slot, cs = u % self.slots, self.cols(core)
            for z in range(nz):
                along = (z + 1 if z < nz - 1 else 0) + (nz - z if z else 0)
                pieces = 1 + 2 * along + 2 * nz if core == 0 else along + 3 * nz
                same = self.stg.at[0:pieces, :, cs]

                @pl.when(self.z == z)
                def _():
                    pltpu.make_async_remote_copy(
                        src_ref=same,
                        dst_ref=same,
                        send_sem=self.ssem.at[slot],
                        recv_sem=self.rsem.at[slot, 0],
                        device_id=(self.b, 1 - self.c),
                        device_id_type=MESH,
                    ).wait_send()

        else:
            self.run(core, par, u, None, "drain")
        self.sibling(core, u).wait_send()

    def sibling(self, core, u):
        ref = self.G.at[u, :, :, :, :, self.cols(core)]
        return pltpu.make_async_remote_copy(
            src_ref=ref,
            dst_ref=ref,
            send_sem=self.sib_s.at[u % self.slots],
            recv_sem=self.sib_r.at[u % self.slots],
            device_id=(self.b, 1 - self.c),
            device_id_type=MESH,
        )

    def tick(self, t, part):
        order = [self.stages, *reversed(range(self.stages))]
        cuts = (0, len(order) // 3 + 1, 2 * len(order) // 3 + 1, len(order))
        for core in (0, 1):

            @pl.when(self.c == core)
            def _():
                for k in order[cuts[part] : cuts[part + 1]]:
                    u = t - k * self.gap
                    for par in (0, 1):

                        @pl.when((u >= 0) & (u < UNITS) & (u % 2 == par))
                        def _():
                            if k == self.stages:
                                self.drain(core, par, u)
                            else:
                                self.run(core, par, u, k, "start")

    def barrier(self):
        bar = pltpu.get_barrier_semaphore()
        plane, me = 2 * self.n * self.n, self.place()

        def in_plane(i, carry):
            to = (me + i) % plane
            pl.semaphore_signal(bar, inc=1, device_id=self.at(to), device_id_type=MESH)
            return carry

        def along_z(i, carry):
            pl.semaphore_signal(bar, inc=1, device_id=self.along((self.z + i) % self.nz), device_id_type=MESH)
            return carry

        lax.fori_loop(1, plane, in_plane, 0)
        lax.fori_loop(1, self.nz, along_z, 0)
        pl.semaphore_wait(bar, plane - 1 + self.nz - 1)

    def place(self):
        return (self.b % (self.n * self.n)) * 2 + self.c

    def at(self, p):
        return (self.z * self.n * self.n + p // 2, p % 2)

    def along(self, z):
        return (z * self.n * self.n + self.b % (self.n * self.n), self.c)


class Total:
    def __init__(self, comm, phase, l, lo, hi, bg, planes, part, lines, total, sems):
        self.comm, self.phase, self.l, self.rows = comm, phase, l, pl.ds(lo, hi - lo)
        self.bg, self.planes, self.part, self.lines, self.total = bg, planes, part, lines, total
        self.sems = sems

    def ends(self, second):
        if second:
            return self.part, self.lines, self.comm.z, self.comm.nz
        return self.bg, self.planes, self.comm.place(), 2 * self.comm.n * self.comm.n

    def copy(self, second, src, dst, to):
        return pltpu.make_async_remote_copy(
            src_ref=src,
            dst_ref=dst,
            send_sem=self.sems.at[self.phase, 2 * second],
            recv_sem=self.sems.at[self.phase, 2 * second + 1],
            device_id=to,
            device_id_type=MESH,
        )

    def send(self, second):
        comm, l, rows = self.comm, self.l, self.rows
        src, dst, me, count = self.ends(second)

        def one(i, carry):
            peer = (me + i) % count
            to = comm.along(peer) if second else comm.at(peer)
            self.copy(second, src.at[l, rows], dst.at[l, me, rows], to).start()
            return carry

        lax.fori_loop(1, count, one, 0)

    def every(self, second):
        _, dst, _, count = self.ends(second)
        all_of = dst.at[self.l, pl.ds(0, count - 1), self.rows]
        return self.copy(second, all_of, all_of, (self.comm.b, 1 - self.comm.c))

    def add(self, second):
        src, buf, me, count = self.ends(second)
        out = self.total if second else self.part
        self.every(second).wait_recv()
        buf[self.l, me, self.rows] = src[self.l, self.rows]

        def one(i, acc):
            return acc + buf[self.l, i, self.rows]

        out[self.l, self.rows] = lax.fori_loop(1, count, one, buf[self.l, 0, self.rows])
        self.every(second).wait_send()

    def start(self):
        self.send(0)

    def middle(self):
        self.add(0)
        self.send(1)

    def finish(self):
        self.add(1)


def dot(a, b, ca=1, cb=0):
    return lax.dot_general(a, b, (((ca,), (cb,)), ((), ())), preferred_element_type=F32)


def fold(values):
    rows, cols = values.shape
    return jnp.sum(values.reshape(rows // 8, 8, cols), axis=0)


def colsum(values):
    return jnp.sum(values, axis=0, keepdims=True)


def kernel(
    nz,
    n,
    gap,
    slots,
    lengths,
    separators,
    hidden,
    cotangent,
    type_table_in,
    proj,
    outw,
    inner,
    outer,
    query_bias_in,
    value_bias_in,
    output_bias_in,
    inner_bias_in,
    outer_bias_in,
    first_gain_in,
    first_shift_in,
    second_gain_in,
    second_shift_in,
    layer_output,
    input_gradient,
    total,
    G,
    P0,
    type_table,
    query_bias,
    value_bias,
    output_bias,
    inner_bias,
    outer_bias,
    first_gain,
    first_shift,
    second_gain,
    second_shift,
    stg,
    xin,
    cot,
    xs,
    xb,
    qkv,
    qT,
    prob,
    mid,
    act,
    gp,
    n1,
    n2,
    r1,
    r2,
    gcT,
    dkT,
    dvT,
    wbuf,
    bg,
    planes,
    part,
    lines,
    dqs8,
    ssem,
    rsem,
    sib_s,
    sib_r,
    lsem,
    wsem,
    xsem,
    psem,
    vsem,
    osem,
    asems,
):
    nb = nz * n * n
    R = D // nb
    T = xs.shape[0]
    half = T // 2
    quarter = nb // 4
    comm = Comm(nz, n, G, stg, ssem, rsem, sib_s, sib_r, slots, gap)
    c = comm.c
    other = (comm.b, 1 - c)
    ctx = xin

    def stage_in():
        for l in range(LAYERS):
            for u in range(8):
                m, j = (proj, u) if u < 3 else (outw, 0) if u == 3 else (inner, u - 4)
                pltpu.make_async_copy(m.at[l, :, pl.ds(j * D, D)], stg.at[l * PER + u], lsem.at[0]).start()
            for j in range(4):
                for g in range(4):
                    pltpu.make_async_copy(
                        outer.at[l, pl.ds(g * R, R), pl.ds(j * BLK, BLK)],
                        stg.at[l * PER + 8 + j, :, pl.ds(g * BLK, BLK)],
                        lsem.at[0],
                    ).start()

    def place():
        pltpu.make_async_copy(stg, stg, lsem.at[0]).wait()
        for core in (0, 1):

            @pl.when(c == core)
            def _():
                cs = comm.cols(core)
                to = G.at[:, comm.z, comm.y, comm.x, :, cs]
                cp = pltpu.make_async_copy(stg.at[:, :, cs], to, lsem.at[1])
                cp.start()
                cp.wait()

    def exchange(op):
        for i, (src, dst) in enumerate(((hidden, xin), (cotangent, cot))):
            rows = pl.ds(pl.multiple_of(c * half, half), half)
            lc = pltpu.make_async_copy(src.at[c], dst.at[rows], xsem.at[3 * i])
            rc = pltpu.make_async_remote_copy(
                src_ref=src.at[1 - c],
                dst_ref=dst.at[rows],
                send_sem=xsem.at[3 * i + 1],
                recv_sem=xsem.at[3 * i + 2],
                device_id=other,
                device_id_type=MESH,
            )
            getattr(lc, op)()
            getattr(rc, op)()

    vectors = (
        (type_table_in, type_table),
        (query_bias_in, query_bias),
        (value_bias_in, value_bias),
        (output_bias_in, output_bias),
        (inner_bias_in, inner_bias),
        (outer_bias_in, outer_bias),
        (first_gain_in, first_gain),
        (first_shift_in, first_shift),
        (second_gain_in, second_gain),
        (second_shift_in, second_shift),
    )

    def small(op):
        for i, (src, dst) in enumerate(vectors):
            getattr(pltpu.make_async_copy(src, dst, vsem.at[i]), op)()

    stage_in()
    small("start")
    comm.barrier()
    exchange("start")
    place()

    def row(ref, l):
        return ref[pl.ds(l, 1), :]

    def cols(i, width=BLK):
        return pl.ds(pl.multiple_of(i * width, width), width)

    lanes = lax.broadcasted_iota(jnp.int32, (T, 2 * HEAD), 1)
    halves = (lanes < HEAD, lanes >= HEAD)

    def init_x():
        exchange("wait")
        small("wait")
        t0 = type_table[0:1, :].astype(F32)
        t1 = type_table[1:2, :].astype(F32)
        sep = separators[c]

        def rows_of(i, carry):
            rs = pl.ds(pl.multiple_of(i * ROWS, ROWS), ROWS)
            at = i * ROWS + lax.broadcasted_iota(jnp.int32, (ROWS, D), 0)
            second = (at > sep).astype(F32)
            x = xin[rs, :].astype(F32) + t0 + second * (t1 - t0)
            xs[rs, :] = x
            xb[rs, :] = x.astype(BF)
            return carry

        lax.fori_loop(0, T // ROWS, rows_of, 0)

    def load_unit(u, slot):
        pltpu.make_async_copy(G.at[u], wbuf.at[slot], wsem.at[slot]).start()

    def load_rows(l, f, slot):
        q = nz // 4
        for j in range(4):
            pltpu.make_async_copy(
                G.at[l * PER + 8 + j, pl.ds(f * q, q)], wbuf.at[slot, pl.ds(j * q, q)], wsem.at[slot]
            ).start()

    def loaded(slot):
        pltpu.make_async_copy(G.at[0], wbuf.at[slot], wsem.at[slot]).wait()

    def w_cols(slot, g):
        return wbuf[slot, :, :, :, :, cols(g)].reshape(D, BLK)

    def w_rows(slot, i):
        return wbuf[slot, pl.ds(i * (nz // 4), nz // 4)].reshape(BLK, D)

    def stacked(chips):
        return jnp.concatenate([w[:, g * BLK : (g + 1) * BLK] for w in chips for g in range(4)], axis=0)

    def chip(slot, i):
        return wbuf[slot, i // (n * n), (i // n) % n, i % n]

    def o_rows(slot, i):
        per = nb // 16
        return jnp.concatenate(
            [stacked([chip(slot, j * quarter + i * per + w) for w in range(per)]) for j in range(4)], axis=1
        )

    def o_cols(slot, i):
        return stacked([chip(slot, i * quarter + w) for w in range(quarter)])

    def norm_rows(z, gain, shift):
        average = jnp.mean(z, axis=1, keepdims=True)
        centred = z - average
        r = lax.rsqrt(jnp.mean(centred * centred, axis=1, keepdims=True) + EPSILON)
        normed = centred * r
        return normed, r, normed * gain + shift

    def do_qkv(l, j, slot, lo, hi):
        is_q, is_v = (j == 0).astype(F32), (j == 2).astype(F32)
        at = jnp.where(j == 0, 0, 2 * l + j)

        for g in range(lo, hi):
            sl = slice(g * BLK, (g + 1) * BLK)
            bias = query_bias[pl.ds(l, 1), sl] * is_q + value_bias[pl.ds(l, 1), sl] * is_v
            qkv[at, :, sl] = (dot(xb[...], w_cols(slot, g)) + bias).astype(BF)

    def do_attention(l, lo, hi):
        key_ok = lax.broadcasted_iota(jnp.int32, (1, T), 1) < lengths[c]

        def pair(hp, carry):
            cs = cols(hp, 2 * HEAD)
            q2, k2, v2 = qkv[0, :, cs], qkv[2 * l + 1, :, cs], qkv[2 * l + 2, :, cs]
            outs = []
            for hh in (0, 1):
                qm = jnp.where(halves[hh], q2 * BF(HEAD**-0.5), BF(0))
                s = jnp.where(key_ok, dot(qm, k2, 1, 1), MASKED)
                e = jnp.exp(s - jnp.max(s, axis=1, keepdims=True))
                p = (e * (1.0 / jnp.sum(e, axis=1, keepdims=True))).astype(BF)
                prob[2 * hp + hh] = p
                outs.append(dot(p, v2))
            ctx[:, cs] = jnp.where(halves[0], outs[0], outs[1]).astype(BF)
            qT[l, cs, :] = q2.T
            return carry

        lax.fori_loop(lo, hi, pair, 0)

    def do_out(l, slot, part):
        if part == 2:
            return do_norm1(l)
        for g in range(4):
            sl = slice(g * BLK, (g + 1) * BLK)
            mid[:, sl] = xs[:, sl] + dot(ctx[...], w_cols(slot, g)) + output_bias[pl.ds(l, 1), sl]

    def do_norm1(l):
        gain, shift = row(first_gain, l), row(first_shift, l)

        def rows_of(i, carry):
            rs = pl.ds(pl.multiple_of(i * ROWS, ROWS), ROWS)
            normed, r, y = norm_rows(mid[rs, :], gain, shift)
            n1[l, rs, :] = normed.astype(BF)
            r1[l, rs, :] = r
            mid[rs, :] = y
            xb[rs, :] = y.astype(BF)
            return carry

        lax.fori_loop(0, T // ROWS, rows_of, 0)

    def do_inner(l, lo, hi):
        def block(i, carry):
            cs = cols(i)
            h = dot(xb[...], w_cols((l * PER + 4 + i // 4) % 3, i % 4)) + inner_bias[pl.ds(l, 1), cs]
            cdf = 0.5 + 0.5 * lax.erf(h * (0.5**0.5))
            act[:, cs] = (h * cdf).astype(BF)
            gp[l, :, cs] = (cdf + h * (jnp.exp(-0.5 * h * h) * 0.3989422804014327)).astype(BF)
            return carry

        lax.fori_loop(lo, hi, block, 0)

    def do_outer(l, j, slot, part):
        cs = cols(j)
        rs = pl.ds(pl.multiple_of(part * half, half), half)
        y = mid[rs, cs] + outer_bias[pl.ds(l, 1), cs]
        for i in range(4):
            y = y + dot(act[rs, i * D : (i + 1) * D], o_cols(slot, i))
        xs[rs, cs] = y

    def do_norm2(l):
        gain, shift = row(second_gain, l), row(second_shift, l)

        def rows_of(i, carry):
            rs = pl.ds(pl.multiple_of(i * ROWS, ROWS), ROWS)
            normed, r, y = norm_rows(xs[rs, :], gain, shift)
            n2[l, rs, :] = normed.astype(BF)
            r2[l, rs, :] = r
            yb = y.astype(BF)
            xb[rs, :] = yb
            ctx[rs, :] = yb
            xs[rs, :] = jnp.where(l == LAYERS - 1, cot[rs, :].astype(F32), y)
            return carry

        lax.fori_loop(0, T // ROWS, rows_of, 0)

    def save_prob(op):
        getattr(pltpu.make_async_copy(prob, P0, psem), op)()

    def compute(v, slot, part):
        l, k = v // PER, v % PER

        def choose(*of_k):
            out = jnp.int32(of_k[-1])
            for i, value in enumerate(of_k[:-1]):
                out = jnp.where(k == i, value, out)
            return out

        pl.when(k < 3)(lambda: do_qkv(l, k, slot, (0, 2, 3)[part], (2, 3, 4)[part]))

        first = {0: (0, 0, 0, 1, 4, 7), 1: (0, 0, 0, 2, 5), 2: (0, 0, 0, 3, 6)}[part]
        when = {0: (k >= 3) & (k <= 5), 1: (k == 3) | (k == 4), 2: (k >= 2) & (k <= 4)}[part]
        pl.when(when)(lambda: do_attention(l, choose(*first), choose(*first) + 1))

        if part:

            @pl.when(k == 5)
            def _():
                if part == 1:
                    pl.when(l == 0)(lambda: save_prob("start"))
                do_out(l, (v + 1) % 3, part)

        lo = {0: (0, 0, 0, 0, 0, 0, 0, 7, 14), 1: (0, 0, 0, 0, 0, 0, 3, 10), 2: (0, 0, 0, 0, 0, 0, 5, 12)}[part]
        hi = {0: (0, 0, 0, 0, 0, 0, 3, 10, 16), 1: (0, 0, 0, 0, 0, 0, 5, 12), 2: (0, 0, 0, 0, 0, 0, 7, 14)}[part]
        pl.when((k >= 6) & (k <= (8 if part == 0 else 7)))(lambda: do_inner(l, choose(*lo), choose(*hi)))

        when = {0: k > 8, 1: k >= 8, 2: k == 8}[part]
        pl.when(when)(lambda: do_outer(l, k - 8, slot, jnp.where(k == 8, part - 1, part)))
        if part == 1:

            @pl.when(k == PER - 1)
            def _():
                pl.when(l == 0)(lambda: save_prob("wait"))
                do_norm2(l)

    def load(s, slot):
        l, k = 1 - s // PER, s % PER
        rows = (k < 8) & (k % 2 == 0)
        pl.when(rows)(lambda: load_rows(l, k // 2, slot))
        unit = l * PER + jnp.where(k < 8, 4 + k // 2, jnp.where(k == 8, 3, k - 9))
        pl.when(jnp.logical_not(rows))(lambda: load_unit(unit, slot))

    lag = (comm.stages - 1) * gap + 1

    def main(t, carry):
        v = t - lag
        slot = (v + 3 * lag) % 3
        ready = (v >= 0) & (v < UNITS)

        comm.tick(t, 0)
        pl.when(t == 1)(init_x)

        @pl.when(ready)
        def _():
            loaded(slot)

            @pl.when(v == UNITS - 1)
            def _():
                load(0, 0)
                load(1, 1)

            compute(v, slot, 0)

        comm.tick(t, 1)
        pl.when(ready)(lambda: compute(v, slot, 1))
        comm.tick(t, 2)

        @pl.when((v >= -1) & (v < UNITS - 1))
        def _():
            for core in (0, 1):

                @pl.when(c == core)
                def _():
                    comm.sibling(1 - core, v + 1).wait_recv()

            load_unit(v + 1, (slot + 1) % 3)

        pl.when(ready)(lambda: compute(v, slot, 2))
        return carry

    lax.fori_loop(0, UNITS + comm.stages * gap, main, 0)

    def results(src, out, base, op):
        mine = pl.ds(pl.multiple_of(c * half, half), half)
        theirs = pl.ds(pl.multiple_of((1 - c) * half, half), half)
        lc = pltpu.make_async_copy(src.at[mine], out.at[c], osem.at[base])
        rc = pltpu.make_async_remote_copy(
            src_ref=src.at[theirs],
            dst_ref=out.at[c],
            send_sem=osem.at[base + 1],
            recv_sem=osem.at[base + 2],
            device_id=other,
            device_id_type=MESH,
        )
        if op == "start":
            rc.start()
            lc.start()
        else:
            rc.wait_send()
            lc.wait()

    def arrived(src, out, base):
        rows = pl.ds(0, half)
        pltpu.make_async_remote_copy(
            src_ref=src.at[rows],
            dst_ref=out.at[1 - c],
            send_sem=osem.at[base + 1],
            recv_sem=osem.at[base + 2],
            device_id=other,
            device_id_type=MESH,
        ).wait_recv()

    def next_weights(s):
        loaded(s % 3)
        pl.when(s + 2 < UNITS)(lambda: load(s + 2, (s + 2) % 3))
        return s % 3

    def keep_sum(l, k, values):
        for i in range(values.shape[1] // 128):
            bg[l, k, i : i + 1, :] = values[:, i * 128 : (i + 1) * 128]

    def norm_back(l, source, normed, r_ref, gain_ref, at_shift, at_bias, keep):
        gain = row(gain_ref, l)

        def rows_of(i, carry):
            sum_g, sum_z = carry
            rs = pl.ds(pl.multiple_of(i * ROWS, ROWS), ROWS)
            g = source[rs, :]
            nv = normed[l, rs, :].astype(F32)
            u = g * gain
            gz = r_ref[l, rs, :] * (
                u - jnp.mean(u, axis=1, keepdims=True) - nv * jnp.mean(u * nv, axis=1, keepdims=True)
            )
            keep[rs, :] = gz
            xb[rs, :] = gz.astype(BF)
            return sum_g + fold(g), sum_z + fold(gz)

        zero = jnp.zeros((8, D), F32)
        sum_g, sum_z = lax.fori_loop(0, T // ROWS, rows_of, (zero, zero))
        keep_sum(l, at_shift, colsum(sum_g))
        keep_sum(l, at_bias, colsum(sum_z))

    results(ctx, layer_output, 0, "start")

    def layer_back(i, carry):
        l = LAYERS - 1 - i
        s0 = i * PER
        norm_back(l, xs, n2, r2, second_gain, 8, 6, mid)
        pl.when(i == 1)(totals[0].start)

        def ff(f, carry):
            slot = next_weights(s0 + 2 * f)
            for i4 in range(4):
                cs = cols(f * 4 + i4)
                gh = dot(xb[...], o_rows(slot, i4), 1, 1) * gp[l, :, cs].astype(F32)
                sums = colsum(fold(gh))
                bg[l, 2 + f, 2 * i4 : 2 * i4 + 1, :] = sums[:, :128]
                bg[l, 2 + f, 2 * i4 + 1 : 2 * i4 + 2, :] = sums[:, 128:]
                act[:, cs] = gh.astype(BF)
            slot = next_weights(s0 + 2 * f + 1)
            for i4 in range(4):
                sl = slice(i4 * BLK, (i4 + 1) * BLK)
                mid[:, sl] += dot(act[:, cols(f, D)], w_rows(slot, i4), 1, 1)
            return carry

        lax.fori_loop(0, 4, ff, 0)
        pl.when(i == 1)(totals[0].middle)
        norm_back(l, mid, n1, r1, first_gain, 7, 1, mid)
        slot = next_weights(s0 + 8)
        for i4 in range(4):
            sl = slice(i4 * BLK, (i4 + 1) * BLK)
            gc = dot(xb[...], w_rows(slot, i4), 1, 1).astype(BF)
            sums = colsum(fold(gc.astype(F32)))
            bg[l, 0, 2 * i4 : 2 * i4 + 1, :] = sums[:, :128]
            bg[l, 0, 2 * i4 + 1 : 2 * i4 + 2, :] = sums[:, 128:]
            qkv[0, :, sl] = gc
            gcT[sl, :] = gc.T

        pl.when(i == 0)(lambda: results(ctx, layer_output, 0, "wait"))

        @pl.when(i == 1)
        def _():
            load_prob("wait")
            totals[0].finish()
            totals[1].start()

        def pair(hp, carry):
            cs = cols(hp, 2 * HEAD)
            gc2, k2, v2 = qkv[0, :, cs], qkv[2 * l + 1, :, cs], qkv[2 * l + 2, :, cs]
            dqs = []
            for hh in (0, 1):
                hs = pl.ds(pl.multiple_of((2 * hp + hh) * HEAD, HEAD), HEAD)
                p = prob[2 * hp + hh]
                pf = p.astype(F32)
                gm = jnp.where(halves[hh], gc2 * BF(HEAD**-0.5), BF(0))
                dp = dot(gm, v2, 1, 1)
                total = jnp.sum(dp * pf, axis=1, keepdims=True)
                ds = (pf * (dp - total)).astype(BF)
                dqs.append(dot(ds, k2))
                dkT[hs, :] = dot(qT[l, hs, :], ds).astype(BF)
                dvT[hs, :] = dot(gcT[hs, :], p).astype(BF)
            dq = jnp.where(halves[0], dqs[0], dqs[1])
            dqs8[:, cs] = fold(dq)
            ctx[:, cs] = dq.astype(BF)
            return carry

        lax.fori_loop(0, HEADS // 2, pair, 0, unroll=2)
        keep_sum(l, 9, colsum(dqs8[...]))

        @pl.when(i == 0)
        def _():
            load_prob("start")

        @pl.when(i == 1)
        def _():
            totals[2].start()
            totals[1].middle()


        slot = next_weights(s0 + 9)
        for i4 in range(4):
            sl = slice(i4 * BLK, (i4 + 1) * BLK)
            mid[:, sl] += dot(ctx[...], w_rows(slot, i4), 1, 1)
        slot = next_weights(s0 + 10)
        for i4 in range(4):
            sl = slice(i4 * BLK, (i4 + 1) * BLK)
            mid[:, sl] += dot(dkT[...], w_rows(slot, i4), 0, 1)
        pl.when(i == 1)(totals[2].middle)
        slot = next_weights(s0 + 11)
        for i4 in range(4):
            sl = slice(i4 * BLK, (i4 + 1) * BLK)
            y = mid[:, sl] + dot(dvT[...], w_rows(slot, i4), 0, 1)
            xs[:, sl] = y
            xb[:, sl] = y.astype(BF)
        return carry

    def load_prob(op):
        getattr(pltpu.make_async_copy(P0, prob, psem), op)()

    totals = [
        Total(comm, phase, l, lo, hi, bg, planes, part, lines, total, asems)
        for phase, (l, lo, hi) in enumerate(((1, 0, 10), (0, 0, 9), (0, 9, 10)))
    ]
    lax.fori_loop(0, LAYERS, layer_back, 0)
    results(xb, input_gradient, 3, "start")
    totals[1].finish()
    totals[2].finish()
    results(xb, input_gradient, 3, "wait")
    arrived(xb, layer_output, 0)
    arrived(xb, input_gradient, 3)


def finish(first, second, total, *rest):
    outs, (buf, into, outof) = rest[:9], rest[9:]
    half = first.shape[1] // 2
    moves = []
    for i, (src, dst) in enumerate(((first, outs[0]), (second, outs[1]))):
        for j in range(2):
            rows = pl.ds(j * half, half)
            k = 2 * i + j
            moves.append(
                (
                    pltpu.make_async_copy(src.at[:, rows], buf.at[k], into.at[k]),
                    pltpu.make_async_copy(buf.at[k], dst.at[:, rows], outof.at[k]),
                )
            )
    for here, _ in moves:
        here.start()
    for l in range(LAYERS):
        for k, out, at in (
            (9, outs[2], 0),
            (0, outs[3], 0),
            (1, outs[4], 0),
            (2, outs[5], 0),
            (3, outs[5], 1),
            (4, outs[5], 2),
            (5, outs[5], 3),
            (6, outs[6], 0),
            (7, outs[7], 0),
            (8, outs[8], 0),
        ):
            for i in range(8):
                out[l : l + 1, at * D + i * 128 : at * D + (i + 1) * 128] = total[l, k, i : i + 1, :]
    for here, there in moves:
        here.wait()
        there.start()
    for _, there in moves:
        there.wait()


def on_device(
    hidden,
    cotangent,
    lengths,
    separators,
    type_table,
    projection_weight,
    output_weight,
    inner_weight,
    outer_weight,
    query_bias,
    value_bias,
    output_bias,
    inner_bias,
    outer_bias,
    first_gain,
    first_shift,
    second_gain,
    second_shift,
):
    nb = lax.axis_size("batch")
    nz, n = sizes(nb)
    gap = 2 if nb <= 16 else 1
    stages = 1 + (n - 1) + (nz - 1) + (n - 1)
    slots = (stages + 1) * gap
    plane = 2 * n * n
    T = 2 * hidden.shape[1]
    R = D // nb
    smem = pl.BlockSpec(memory_space=pltpu.SMEM)
    vmem = pl.BlockSpec(memory_space=pltpu.VMEM)
    hbm = pl.BlockSpec(memory_space=pl.ANY)
    sems = Comm.sems(nz, n)
    out_shape = (
        jax.ShapeDtypeStruct(hidden.shape, BF),
        jax.ShapeDtypeStruct(hidden.shape, BF),
        jax.ShapeDtypeStruct((LAYERS, 10, 8, 128), F32),
        jax.ShapeDtypeStruct((UNITS, nz, n, n, R, D), BF),
        jax.ShapeDtypeStruct((HEADS, T, T), BF),
    )
    dma = pltpu.SemaphoreType.DMA
    scratch = [
        pltpu.VMEM((2, D), BF),
        *(pltpu.VMEM((LAYERS, w), F32) for w in (D, D, D, FF, D, D, D, D, D)),
        pltpu.VMEM((UNITS, R, D), BF),
        pltpu.VMEM((T, D), BF),
        pltpu.VMEM((T, D), BF),
        pltpu.VMEM((T, D), F32),
        pltpu.VMEM((T, D), BF),
        pltpu.VMEM((5, T, D), BF),
        pltpu.VMEM((LAYERS, D, T), BF),
        pltpu.VMEM((HEADS, T, T), BF),
        pltpu.VMEM((T, D), F32),
        pltpu.VMEM((T, FF), BF),
        pltpu.VMEM((LAYERS, T, FF), BF),
        pltpu.VMEM((LAYERS, T, D), BF),
        pltpu.VMEM((LAYERS, T, D), BF),
        pltpu.VMEM((LAYERS, T, 1), F32),
        pltpu.VMEM((LAYERS, T, 1), F32),
        pltpu.VMEM((D, T), BF),
        pltpu.VMEM((D, T), BF),
        pltpu.VMEM((D, T), BF),
        pltpu.VMEM((3, nz, n, n, R, D), BF),
        pltpu.VMEM((LAYERS, 10, 8, 128), F32),
        pltpu.VMEM((LAYERS, plane, 10, 8, 128), F32),
        pltpu.VMEM((LAYERS, 10, 8, 128), F32),
        pltpu.VMEM((LAYERS, nz, 10, 8, 128), F32),
        pltpu.VMEM((8, D), F32),
        dma((slots,)),
        dma((slots, sems)),
        dma((slots,)),
        dma((slots,)),
        dma((2,)),
        dma((3,)),
        dma((6,)),
        dma(()),
        dma((10,)),
        dma((6,)),
        dma((3, 4)),
    ]
    out = pl.pallas_call(
        functools.partial(kernel, nz, n, gap, slots),
        out_shape=out_shape,
        in_specs=[smem, smem] + [hbm] * 16,
        out_specs=(hbm, hbm, vmem, hbm, hbm),
        scratch_shapes=scratch,
        compiler_params=pltpu.CompilerParams(
            collective_id=0, has_side_effects=True, vmem_limit_bytes=60 * 2**20
        ),
        cost_estimate=pl.CostEstimate(flops=60 * 10**9, bytes_accessed=200 * 10**6, transcendentals=20 * 10**6),
    )(
        lengths,
        separators,
        hidden,
        cotangent,
        type_table,
        projection_weight,
        output_weight,
        inner_weight,
        outer_weight,
        query_bias,
        value_bias,
        output_bias,
        inner_bias,
        outer_bias,
        first_gain,
        first_shift,
        second_gain,
        second_shift,
    )
    half = hidden.shape[1] // 2
    return tuple(
        pl.pallas_call(
            finish,
            out_shape=(
                jax.ShapeDtypeStruct(hidden.shape, BF),
                jax.ShapeDtypeStruct(hidden.shape, BF),
                *(jax.ShapeDtypeStruct(b.shape, F32) for b in (
                    query_bias, value_bias, output_bias, inner_bias, outer_bias, first_shift, second_shift
                )),
            ),
            in_specs=[hbm, hbm, vmem],
            out_specs=(hbm, hbm) + (vmem,) * 7,
            scratch_shapes=[pltpu.VMEM((4, 2, half, D), BF), dma((4,)), dma((4,))],
        )(out[0], out[1], out[2])
    )


def solution(mesh):
    batched = P("batch", "blk", None)
    rows = P(None, "batch", None)
    return jax.shard_map(
        on_device,
        mesh=mesh,
        in_specs=(batched, batched, P("batch"), P("batch"), P(), rows, rows, rows, rows) + (P(),) * 9,
        out_specs=(batched, batched) + (P(),) * 7,
        check_vma=False,
    )
```

```python
import functools

import jax
import jax.numpy as jnp
from jax import lax
from jax.experimental import pallas as pl
from jax.experimental.pallas import tpu as pltpu
from jax.sharding import PartitionSpec as P

D = 1024
HEADS = 16
HEAD = 64
FF = 4096
LAYERS = 2
UNITS = 24
PER = 12
SPLIT = 640
BLK = 256
ROWS = 256
EPSILON = 1e-12
MASKED = -1000000000.0
MESH = pl.DeviceIdType.MESH
BF = jnp.bfloat16
F32 = jnp.float32


def sizes(batch):
    side = 2 ** ((batch.bit_length() - 1) // 3)
    return batch // (side * side), side


def lane(n):
    return 1 if n == 2 else 2 * (n - 1)


class Comm:
    def __init__(self, nz, n, gathered, stg, ssem, rsem, sib_s, sib_r, slots, ticks):
        self.nz, self.n, self.G, self.stg = nz, n, gathered, stg
        self.ssem, self.rsem, self.sib_s, self.sib_r = ssem, rsem, sib_s, sib_r
        self.slots, self.ticks = slots, ticks
        self.b = lax.axis_index("batch")
        self.c = lax.axis_index("blk")
        self.z, self.y, self.x = self.b // (n * n), (self.b // n) % n, self.b % n
        self.stages = 1 + (n - 1) + (nz - 1) + (n - 1)
        self.fbase = nz

    @staticmethod
    def sems(nz, n):
        return 2 * nz + 1 if n == 2 else nz + 2 * nz * lane(n)

    def cols(self, core):
        return pl.ds(0, SPLIT) if core == 0 else pl.ds(SPLIT, D - SPLIT)

    def setup(self, core, par, u):
        first_x = (core == 0) == (par == 0)
        cs, g, n = self.cols(core), self.G, self.n
        self.f, self.s = (self.x, self.y) if first_x else (self.y, self.x)
        self.fstr, self.sstr = (1, n) if first_x else (n, 1)
        if first_x:
            self.sl = lambda zi, fi, si: g.at[u, zi, si, fi, :, cs]
        else:
            self.sl = lambda zi, fi, si: g.at[u, zi, fi, si, :, cs]
        self.slot = u % self.slots

    def copy(self, ref, idx, to):
        return pltpu.make_async_remote_copy(
            src_ref=ref,
            dst_ref=ref,
            send_sem=self.ssem.at[self.slot],
            recv_sem=self.rsem.at[self.slot, idx],
            device_id=(to, self.c),
            device_id_type=MESH,
        )

    def dirs(self, length):
        return (0,) if length == 2 else (0, 1)

    def act(self, cp, mode):
        if mode == "start":
            cp.start()
        else:
            cp.wait_send()

    def arrive(self, ref, base, pos, length, stride, j, e, mode, last=False):
        if length == 2:
            to = self.b + stride * (1 - 2 * pos)
            if j == 0:
                self.act(self.copy(ref(pos), base, to), mode)
            elif mode == "start" and not last:
                self.copy(ref(1 - pos), base, to).wait_recv()
            return
        if j == 0:
            for d in (0, 1):

                @pl.when((pos + 1 < length) if d == 0 else (pos >= 1))
                def _():
                    self.act(self.copy(ref(pos), base + d, self.b + (stride if d == 0 else -stride)), mode)

            return
        src = pos - j if e == 0 else pos + j
        ok = (src >= 0) if e == 0 else (src < length)
        fwd = (pos + 1 < length) if e == 0 else (pos >= 1)
        to = self.b + (stride if e == 0 else -stride)
        if mode == "start":

            @pl.when(ok)
            def _():
                self.copy(ref(src), base + 2 * (j - 1) + e, to).wait_recv()

        if j < length - 1:

            @pl.when(ok & fwd)
            def _():
                self.act(self.copy(ref(src), base + 2 * j + e, to), mode)

    def hops(self):
        yield 0, 0
        for h in range(1, self.nz):
            for d in (0, 1):
                yield h, d

    def run(self, core, par, u, k, mode):
        self.setup(core, par, u)
        n, nz, z, b = self.n, self.nz, self.z, self.b
        lw = lane(n)
        sbase = self.fbase + nz * lw
        f, s = self.f, self.s
        pre = 0
        if core == 0:
            for j in range(n):
                if k is None or k == j:
                    for e in self.dirs(n) if j else (0,):
                        self.arrive(lambda i: self.sl(z, i, s), self.fbase, f, n, self.fstr, j, e, mode)
            pre = n - 1
        last = (n - 1) if core == 0 else 2 * (n - 1)
        for h, d in self.hops():
            zi = z - h if d == 0 else z + h
            fi = f if core == 1 else slice(None)

            def along_z():
                ref = self.sl(zi, fi, s)
                if h and mode == "start":
                    self.copy(ref, zi, b).wait_recv()
                if h < nz - 1:
                    for dd in (0, 1) if h == 0 else (d,):

                        @pl.when((z + 1 < nz) if dd == 0 else (z >= 1))
                        def _():
                            self.act(self.copy(ref, zi, b + (n * n if dd == 0 else -n * n)), mode)

            def in_plane(step):
                q = step
                if core == 1:
                    if step < n:
                        for e in self.dirs(n) if step else (0,):
                            self.arrive(
                                lambda i: self.sl(zi, i, s), self.fbase + zi * lw, f, n, self.fstr, step, e, mode
                            )
                    q = step - (n - 1)
                if q >= 0:
                    for e in self.dirs(n) if q else (0,):
                        at = sbase if n == 2 else sbase + zi * lw
                        self.arrive(lambda i: self.sl(zi, slice(None), i), at, s, n, self.sstr, q, e, mode, True)

            def events():
                for step in range(last + 1):
                    if k is None or k == pre + h + step:
                        if step == 0:
                            along_z()
                        in_plane(step)

            if k is None or 0 <= k - pre - h <= last:
                if h == 0:
                    events()
                else:
                    pl.when((zi >= 0) if d == 0 else (zi < nz))(events)
        if k == self.stages - 1:
            if n == 2:
                self.copy(self.sl(slice(None), slice(None), 1 - s), sbase, b).wait_recv()
            self.sibling(core, u).start()

    def drain(self, core, par, u):
        n, nz = self.n, self.nz
        if n == 2:
            slot, cs = u % self.slots, self.cols(core)
            for z in range(nz):
                along = (z + 1 if z < nz - 1 else 0) + (nz - z if z else 0)
                pieces = 1 + 2 * along + 2 * nz if core == 0 else along + 3 * nz
                same = self.stg.at[0:pieces, :, cs]

                @pl.when(self.z == z)
                def _():
                    pltpu.make_async_remote_copy(
                        src_ref=same,
                        dst_ref=same,
                        send_sem=self.ssem.at[slot],
                        recv_sem=self.rsem.at[slot, 0],
                        device_id=(self.b, 1 - self.c),
                        device_id_type=MESH,
                    ).wait_send()

        else:
            self.run(core, par, u, None, "drain")
        self.sibling(core, u).wait_send()

    def sibling(self, core, u):
        ref = self.G.at[u, :, :, :, :, self.cols(core)]
        return pltpu.make_async_remote_copy(
            src_ref=ref,
            dst_ref=ref,
            send_sem=self.sib_s.at[u % self.slots],
            recv_sem=self.sib_r.at[u % self.slots],
            device_id=(self.b, 1 - self.c),
            device_id_type=MESH,
        )

    def tick(self, t, part):
        order = [self.stages, *reversed(range(self.stages))]
        cuts = (0, len(order) // 3 + 1, 2 * len(order) // 3 + 1, len(order))
        for core in (0, 1):

            @pl.when(self.c == core)
            def _():
                for k in order[cuts[part] : cuts[part + 1]]:
                    u = t - self.ticks[k]
                    for par in (0, 1):

                        @pl.when((u >= 0) & (u < UNITS) & (u % 2 == par))
                        def _():
                            if k == self.stages:
                                self.drain(core, par, u)
                            else:
                                self.run(core, par, u, k, "start")

    def barrier(self, meanwhile):
        bar = pltpu.get_barrier_semaphore()
        plane, me = 2 * self.n * self.n, self.place()

        def in_plane(i, carry):
            to = (me + i) % plane
            pl.semaphore_signal(bar, inc=1, device_id=self.at(to), device_id_type=MESH)
            return carry

        def along_z(i, carry):
            pl.semaphore_signal(bar, inc=1, device_id=self.along((self.z + i) % self.nz), device_id_type=MESH)
            return carry

        lax.fori_loop(1, plane, in_plane, 0, unroll=plane <= 8)
        lax.fori_loop(1, self.nz, along_z, 0, unroll=plane <= 8)
        meanwhile()
        pl.semaphore_wait(bar, plane - 1 + self.nz - 1)

    def place(self):
        return (self.b % (self.n * self.n)) * 2 + self.c

    def at(self, p):
        return (self.z * self.n * self.n + p // 2, p % 2)

    def along(self, z):
        return (z * self.n * self.n + self.b % (self.n * self.n), self.c)


class Total:
    def __init__(self, comm, phase, lo, hi, bg, planes, part, lines, total, sems):
        self.comm, self.phase, self.rows = comm, phase, pl.ds(lo, hi - lo)
        self.bg, self.planes, self.part, self.lines, self.total = bg, planes, part, lines, total
        self.sems = sems

    def ends(self, second):
        if second:
            return self.part, self.lines, self.comm.z, self.comm.nz
        return self.bg, self.planes, self.comm.place(), 2 * self.comm.n * self.comm.n

    def copy(self, second, src, dst, to):
        return pltpu.make_async_remote_copy(
            src_ref=src,
            dst_ref=dst,
            send_sem=self.sems.at[self.phase, 2 * second],
            recv_sem=self.sems.at[self.phase, 2 * second + 1],
            device_id=to,
            device_id_type=MESH,
        )

    def send(self, second):
        comm, rows = self.comm, self.rows
        src, dst, me, count = self.ends(second)

        def one(i, carry):
            peer = (me + i) % count
            to = comm.along(peer) if second else comm.at(peer)
            self.copy(second, src.at[rows], dst.at[me, rows], to).start()
            return carry

        lax.fori_loop(1, count, one, 0, unroll=count <= 8)

    def every(self, second):
        _, dst, _, count = self.ends(second)
        all_of = dst.at[pl.ds(0, count - 1), self.rows]
        return self.copy(second, all_of, all_of, (self.comm.b, 1 - self.comm.c))

    def add(self, second):
        src, buf, me, count = self.ends(second)
        out = self.total if second else self.part
        self.every(second).wait_recv()
        buf[me, self.rows] = src[self.rows]

        def one(i, acc):
            return acc + buf[i, self.rows]

        out[self.rows] = lax.fori_loop(1, count, one, buf[0, self.rows], unroll=count <= 8)
        self.every(second).wait_send()

    def start(self):
        self.send(0)

    def middle(self):
        self.add(0)
        self.send(1)

    def finish(self):
        self.add(1)


def dot(a, b, ca=1, cb=0):
    return lax.dot_general(a, b, (((ca,), (cb,)), ((), ())), preferred_element_type=F32)


def fold(values):
    rows, cols = values.shape
    return jnp.sum(values.reshape(rows // 8, 8, cols), axis=0)


def colsum(values):
    return jnp.sum(values, axis=0, keepdims=True)


def kernel(
    nz,
    n,
    ticks,
    slots,
    lengths,
    separators,
    hidden,
    cotangent,
    type_table_in,
    proj,
    outw,
    inner,
    outer,
    query_bias_in,
    value_bias_in,
    output_bias_in,
    inner_bias_in,
    outer_bias_in,
    first_gain_in,
    first_shift_in,
    second_gain_in,
    second_shift_in,
    layer_output,
    input_gradient,
    total,
    G,
    P0,
    type_table,
    query_bias,
    value_bias,
    output_bias,
    inner_bias,
    outer_bias,
    first_gain,
    first_shift,
    second_gain,
    second_shift,
    stg,
    xin,
    cot,
    xs,
    xb,
    qkv,
    qT,
    prob,
    mid,
    act,
    gp,
    n1,
    n2,
    r1,
    r2,
    gcT,
    dkT,
    dvT,
    wbuf,
    bg,
    planes,
    part,
    lines,
    dqs8,
    ssem,
    rsem,
    sib_s,
    sib_r,
    lsem,
    wsem,
    xsem,
    psem,
    vsem,
    osem,
    asems,
):
    nb = nz * n * n
    R = D // nb
    T = xs.shape[0]
    half = T // 2
    quarter = nb // 4
    comm = Comm(nz, n, G, stg, ssem, rsem, sib_s, sib_r, slots, ticks)
    c = comm.c
    other = (comm.b, 1 - c)
    ctx = xin

    def stage_in():
        for l in range(LAYERS):
            for u in range(8):
                m, j = (proj, u) if u < 3 else (outw, 0) if u == 3 else (inner, u - 4)
                pltpu.make_async_copy(m.at[l, :, pl.ds(j * D, D)], stg.at[l * PER + u], lsem.at[0]).start()
            for j in range(4):
                for g in range(4):
                    pltpu.make_async_copy(
                        outer.at[l, pl.ds(g * R, R), pl.ds(j * BLK, BLK)],
                        stg.at[l * PER + 8 + j, :, pl.ds(g * BLK, BLK)],
                        lsem.at[0],
                    ).start()

    def place():
        pltpu.make_async_copy(stg, stg, lsem.at[0]).wait()
        for core in (0, 1):

            @pl.when(c == core)
            def _():
                cs = comm.cols(core)
                to = G.at[:, comm.z, comm.y, comm.x, :, cs]
                cp = pltpu.make_async_copy(stg.at[:, :, cs], to, lsem.at[1])
                cp.start()
                cp.wait()

    def exchange(op):
        for i, (src, dst) in enumerate(((hidden, xin), (cotangent, cot))):
            rows = pl.ds(pl.multiple_of(c * half, half), half)
            lc = pltpu.make_async_copy(src.at[c], dst.at[rows], xsem.at[3 * i])
            rc = pltpu.make_async_remote_copy(
                src_ref=src.at[1 - c],
                dst_ref=dst.at[rows],
                send_sem=xsem.at[3 * i + 1],
                recv_sem=xsem.at[3 * i + 2],
                device_id=other,
                device_id_type=MESH,
            )
            getattr(lc, op)()
            getattr(rc, op)()

    vectors = (
        (type_table_in, type_table),
        (query_bias_in, query_bias),
        (value_bias_in, value_bias),
        (output_bias_in, output_bias),
        (inner_bias_in, inner_bias),
        (outer_bias_in, outer_bias),
        (first_gain_in, first_gain),
        (first_shift_in, first_shift),
        (second_gain_in, second_gain),
        (second_shift_in, second_shift),
    )

    def small(op):
        for i, (src, dst) in enumerate(vectors):
            getattr(pltpu.make_async_copy(src, dst, vsem.at[i]), op)()

    def begin():
        stage_in()
        small("start")

    comm.barrier(begin)
    exchange("start")
    place()

    def row(ref, l):
        return ref[pl.ds(l, 1), :]

    def cols(i, width=BLK):
        return pl.ds(pl.multiple_of(i * width, width), width)

    lanes = lax.broadcasted_iota(jnp.int32, (T, 2 * HEAD), 1)
    halves = (lanes < HEAD, lanes >= HEAD)

    def init_x():
        exchange("wait")
        small("wait")
        t0 = type_table[0:1, :].astype(F32)
        t1 = type_table[1:2, :].astype(F32)
        sep = separators[c]

        def rows_of(i, carry):
            rs = pl.ds(pl.multiple_of(i * ROWS, ROWS), ROWS)
            at = i * ROWS + lax.broadcasted_iota(jnp.int32, (ROWS, D), 0)
            second = (at > sep).astype(F32)
            x = xin[rs, :].astype(F32) + t0 + second * (t1 - t0)
            xs[rs, :] = x
            xb[rs, :] = x.astype(BF)
            return carry

        lax.fori_loop(0, T // ROWS, rows_of, 0)

    def load_unit(u, slot):
        pltpu.make_async_copy(G.at[u], wbuf.at[slot], wsem.at[slot]).start()

    def load_rows(l, f, slot):
        q = nz // 4
        for j in range(4):
            pltpu.make_async_copy(
                G.at[l * PER + 8 + j, pl.ds(f * q, q)], wbuf.at[slot, pl.ds(j * q, q)], wsem.at[slot]
            ).start()

    def loaded(slot):
        pltpu.make_async_copy(G.at[0], wbuf.at[slot], wsem.at[slot]).wait()

    def w_cols(slot, g):
        return wbuf[slot, :, :, :, :, cols(g)].reshape(D, BLK)

    def w_rows(slot, i):
        return wbuf[slot, pl.ds(i * (nz // 4), nz // 4)].reshape(BLK, D)

    def stacked(chips):
        return jnp.concatenate([w[:, g * BLK : (g + 1) * BLK] for w in chips for g in range(4)], axis=0)

    def chip(slot, i):
        return wbuf[slot, i // (n * n), (i // n) % n, i % n]

    def o_rows(slot, i):
        per = nb // 16
        return jnp.concatenate(
            [stacked([chip(slot, j * quarter + i * per + w) for w in range(per)]) for j in range(4)], axis=1
        )

    def o_cols(slot, i):
        return stacked([chip(slot, i * quarter + w) for w in range(quarter)])

    def norm_rows(z, gain, shift):
        average = jnp.mean(z, axis=1, keepdims=True)
        centred = z - average
        r = lax.rsqrt(jnp.mean(centred * centred, axis=1, keepdims=True) + EPSILON)
        normed = centred * r
        return normed, r, normed * gain + shift

    def do_qkv(l, j, slot, lo, hi):
        is_q, is_v = (j == 0).astype(F32), (j == 2).astype(F32)
        at = jnp.where(j == 0, 0, 2 * l + j)

        for g in range(lo, hi):
            sl = slice(g * BLK, (g + 1) * BLK)
            bias = query_bias[pl.ds(l, 1), sl] * is_q + value_bias[pl.ds(l, 1), sl] * is_v
            qkv[at, :, sl] = (dot(xb[...], w_cols(slot, g)) + bias).astype(BF)

    def do_attention(l, lo, hi):
        key_ok = lax.broadcasted_iota(jnp.int32, (1, T), 1) < lengths[c]

        def pair(hp, carry):
            cs = cols(hp, 2 * HEAD)
            q2, k2, v2 = qkv[0, :, cs], qkv[2 * l + 1, :, cs], qkv[2 * l + 2, :, cs]
            outs = []
            for hh in (0, 1):
                qm = jnp.where(halves[hh], q2 * BF(HEAD**-0.5), BF(0))
                s = jnp.where(key_ok, dot(qm, k2, 1, 1), MASKED)
                e = jnp.exp(s - jnp.max(s, axis=1, keepdims=True))
                p = (e * (1.0 / jnp.sum(e, axis=1, keepdims=True))).astype(BF)
                prob[2 * hp + hh] = p
                outs.append(dot(p, v2))
            ctx[:, cs] = jnp.where(halves[0], outs[0], outs[1]).astype(BF)
            qT[l, cs, :] = q2.T
            return carry

        lax.fori_loop(lo, hi, pair, 0)

    def do_out(l, slot, part):
        if part == 2:
            return do_norm1(l)
        for g in range(4):
            sl = slice(g * BLK, (g + 1) * BLK)
            mid[:, sl] = xs[:, sl] + dot(ctx[...], w_cols(slot, g)) + output_bias[pl.ds(l, 1), sl]

    def do_norm1(l):
        gain, shift = row(first_gain, l), row(first_shift, l)

        def rows_of(i, carry):
            rs = pl.ds(pl.multiple_of(i * ROWS, ROWS), ROWS)
            normed, r, y = norm_rows(mid[rs, :], gain, shift)
            n1[l, rs, :] = normed.astype(BF)
            r1[l, rs, :] = r
            mid[rs, :] = y
            xb[rs, :] = y.astype(BF)
            return carry

        lax.fori_loop(0, T // ROWS, rows_of, 0)

    def do_inner(l, lo, hi):
        def block(i, carry):
            cs = cols(i)
            h = dot(xb[...], w_cols((l * PER + 4 + i // 4) % 3, i % 4)) + inner_bias[pl.ds(l, 1), cs]
            cdf = 0.5 + 0.5 * lax.erf(h * (0.5**0.5))
            act[:, cs] = (h * cdf).astype(BF)
            gp[l, :, cs] = (cdf + h * (jnp.exp(-0.5 * h * h) * 0.3989422804014327)).astype(BF)
            return carry

        lax.fori_loop(lo, hi, block, 0)

    def do_outer(l, j, slot, part):
        cs = cols(j)
        rs = pl.ds(pl.multiple_of(part * half, half), half)
        y = mid[rs, cs] + outer_bias[pl.ds(l, 1), cs]
        for i in range(4):
            y = y + dot(act[rs, i * D : (i + 1) * D], o_cols(slot, i))
        xs[rs, cs] = y

    def do_norm2(l):
        gain, shift = row(second_gain, l), row(second_shift, l)

        def rows_of(i, carry):
            rs = pl.ds(pl.multiple_of(i * ROWS, ROWS), ROWS)
            normed, r, y = norm_rows(xs[rs, :], gain, shift)
            n2[l, rs, :] = normed.astype(BF)
            r2[l, rs, :] = r
            yb = y.astype(BF)
            xb[rs, :] = yb
            ctx[rs, :] = yb
            xs[rs, :] = jnp.where(l == LAYERS - 1, cot[rs, :].astype(F32), y)
            return carry

        lax.fori_loop(0, T // ROWS, rows_of, 0)

    def save_prob(op):
        getattr(pltpu.make_async_copy(prob, P0, psem), op)()

    def compute(v, slot, part):
        l, k = v // PER, v % PER

        def choose(*of_k):
            out = jnp.int32(of_k[-1])
            for i, value in enumerate(of_k[:-1]):
                out = jnp.where(k == i, value, out)
            return out

        pl.when(k < 3)(lambda: do_qkv(l, k, slot, (0, 2, 3)[part], (2, 3, 4)[part]))

        first = {0: (0, 0, 0, 1, 4, 7), 1: (0, 0, 0, 2, 5), 2: (0, 0, 0, 3, 6)}[part]
        when = {0: (k >= 3) & (k <= 5), 1: (k == 3) | (k == 4), 2: (k >= 2) & (k <= 4)}[part]
        pl.when(when)(lambda: do_attention(l, choose(*first), choose(*first) + 1))

        if part:

            @pl.when(k == 5)
            def _():
                if part == 1:
                    pl.when(l == 0)(lambda: save_prob("start"))
                do_out(l, (v + 1) % 3, part)

        lo = {0: (0, 0, 0, 0, 0, 0, 0, 7, 14), 1: (0, 0, 0, 0, 0, 0, 3, 10), 2: (0, 0, 0, 0, 0, 0, 5, 12)}[part]
        hi = {0: (0, 0, 0, 0, 0, 0, 3, 10, 16), 1: (0, 0, 0, 0, 0, 0, 5, 12), 2: (0, 0, 0, 0, 0, 0, 7, 14)}[part]
        pl.when((k >= 6) & (k <= (8 if part == 0 else 7)))(lambda: do_inner(l, choose(*lo), choose(*hi)))

        when = {0: k > 8, 1: k >= 8, 2: k == 8}[part]
        pl.when(when)(lambda: do_outer(l, k - 8, slot, jnp.where(k == 8, part - 1, part)))
        if part == 1:

            @pl.when(k == PER - 1)
            def _():
                pl.when(l == 0)(lambda: save_prob("wait"))
                do_norm2(l)

    def load(s, slot):
        l, k = 1 - s // PER, s % PER
        rows = (k < 8) & (k % 2 == 0)
        pl.when(rows)(lambda: load_rows(l, k // 2, slot))
        unit = l * PER + jnp.where(k < 8, 4 + k // 2, jnp.where(k == 8, 3, k - 9))
        pl.when(jnp.logical_not(rows))(lambda: load_unit(unit, slot))

    lag = ticks[comm.stages - 1] + 1

    def main(t, carry):
        v = t - lag
        slot = (v + 3 * lag) % 3
        ready = (v >= 0) & (v < UNITS)

        comm.tick(t, 0)
        pl.when(t == 1)(init_x)

        @pl.when(ready)
        def _():
            loaded(slot)

            @pl.when(v == UNITS - 1)
            def _():
                load(0, 0)
                load(1, 1)

            compute(v, slot, 0)

        comm.tick(t, 1)
        pl.when(ready)(lambda: compute(v, slot, 1))
        comm.tick(t, 2)

        @pl.when((v >= -1) & (v < UNITS - 1))
        def _():
            for core in (0, 1):

                @pl.when(c == core)
                def _():
                    comm.sibling(1 - core, v + 1).wait_recv()

            load_unit(v + 1, (slot + 1) % 3)

        pl.when(ready)(lambda: compute(v, slot, 2))
        return carry

    lax.fori_loop(0, UNITS + ticks[comm.stages], main, 0)

    def results(src, out, base, op):
        mine = pl.ds(pl.multiple_of(c * half, half), half)
        theirs = pl.ds(pl.multiple_of((1 - c) * half, half), half)
        lc = pltpu.make_async_copy(src.at[mine], out.at[c], osem.at[base])
        rc = pltpu.make_async_remote_copy(
            src_ref=src.at[theirs],
            dst_ref=out.at[c],
            send_sem=osem.at[base + 1],
            recv_sem=osem.at[base + 2],
            device_id=other,
            device_id_type=MESH,
        )
        if op == "start":
            rc.start()
            lc.start()
        else:
            rc.wait_send()
            lc.wait()

    def arrived(src, out, base):
        rows = pl.ds(0, half)
        pltpu.make_async_remote_copy(
            src_ref=src.at[rows],
            dst_ref=out.at[1 - c],
            send_sem=osem.at[base + 1],
            recv_sem=osem.at[base + 2],
            device_id=other,
            device_id_type=MESH,
        ).wait_recv()

    def next_weights(s):
        loaded(s % 3)
        pl.when(s + 2 < UNITS)(lambda: load(s + 2, (s + 2) % 3))
        return s % 3

    def keep_sum(l, k, values):
        for i in range(values.shape[1] // 128):
            bg[(1 - l) * 10 + k, i : i + 1, :] = values[:, i * 128 : (i + 1) * 128]

    def norm_back(l, source, normed, r_ref, gain_ref, at_shift, at_bias, keep):
        gain = row(gain_ref, l)

        def rows_of(i, carry):
            sum_g, sum_z = carry
            rs = pl.ds(pl.multiple_of(i * ROWS, ROWS), ROWS)
            g = source[rs, :]
            nv = normed[l, rs, :].astype(F32)
            u = g * gain
            gz = r_ref[l, rs, :] * (
                u - jnp.mean(u, axis=1, keepdims=True) - nv * jnp.mean(u * nv, axis=1, keepdims=True)
            )
            keep[rs, :] = gz
            xb[rs, :] = gz.astype(BF)
            return sum_g + fold(g), sum_z + fold(gz)

        zero = jnp.zeros((8, D), F32)
        sum_g, sum_z = lax.fori_loop(0, T // ROWS, rows_of, (zero, zero))
        keep_sum(l, at_shift, colsum(sum_g))
        keep_sum(l, at_bias, colsum(sum_z))

    results(ctx, layer_output, 0, "start")

    def layer_back(i, carry):
        l = LAYERS - 1 - i
        s0 = i * PER
        norm_back(l, xs, n2, r2, second_gain, 7, 5, mid)

        def ff(f, carry):
            slot = next_weights(s0 + 2 * f)
            for i4 in range(4):
                cs = cols(f * 4 + i4)
                gh = dot(xb[...], o_rows(slot, i4), 1, 1) * gp[l, :, cs].astype(F32)
                sums = colsum(fold(gh))
                bg[(1 - l) * 10 + 1 + f, 2 * i4 : 2 * i4 + 1, :] = sums[:, :128]
                bg[(1 - l) * 10 + 1 + f, 2 * i4 + 1 : 2 * i4 + 2, :] = sums[:, 128:]
                act[:, cs] = gh.astype(BF)
            slot = next_weights(s0 + 2 * f + 1)
            for i4 in range(4):
                sl = slice(i4 * BLK, (i4 + 1) * BLK)
                mid[:, sl] += dot(act[:, cols(f, D)], w_rows(slot, i4), 1, 1)
            return carry

        lax.fori_loop(0, 4, ff, 0)
        norm_back(l, mid, n1, r1, first_gain, 6, 0, mid)
        pl.when(i == 1)(totals[0].start)
        slot = next_weights(s0 + 8)
        for i4 in range(4):
            sl = slice(i4 * BLK, (i4 + 1) * BLK)
            gc = dot(xb[...], w_rows(slot, i4), 1, 1).astype(BF)
            sums = colsum(fold(gc.astype(F32)))
            bg[(1 - l) * 10 + 8, 2 * i4 : 2 * i4 + 1, :] = sums[:, :128]
            bg[(1 - l) * 10 + 8, 2 * i4 + 1 : 2 * i4 + 2, :] = sums[:, 128:]
            qkv[0, :, sl] = gc
            gcT[sl, :] = gc.T

        pl.when(i == 0)(lambda: results(ctx, layer_output, 0, "wait"))

        @pl.when(i == 1)
        def _():
            load_prob("wait")

        def pair(hp, carry):
            cs = cols(hp, 2 * HEAD)
            gc2, k2, v2 = qkv[0, :, cs], qkv[2 * l + 1, :, cs], qkv[2 * l + 2, :, cs]
            dqs = []
            for hh in (0, 1):
                hs = pl.ds(pl.multiple_of((2 * hp + hh) * HEAD, HEAD), HEAD)
                p = prob[2 * hp + hh]
                pf = p.astype(F32)
                gm = jnp.where(halves[hh], gc2 * BF(HEAD**-0.5), BF(0))
                dp = dot(gm, v2, 1, 1)
                total = jnp.sum(dp * pf, axis=1, keepdims=True)
                ds = (pf * (dp - total)).astype(BF)
                dqs.append(dot(ds, k2))
                dkT[hs, :] = dot(qT[l, hs, :], ds).astype(BF)
                dvT[hs, :] = dot(gcT[hs, :], p).astype(BF)
            dq = jnp.where(halves[0], dqs[0], dqs[1])
            dqs8[:, cs] = fold(dq)
            ctx[:, cs] = dq.astype(BF)
            return carry

        def four(j, carry):
            lax.fori_loop(0, 4, lambda h, x: pair(4 * j + h, x), 0, unroll=2)
            pl.when((i == 1) & (j == 0))(totals[0].middle)
            return carry

        lax.fori_loop(0, HEADS // 8, four, 0)
        keep_sum(l, 9, colsum(dqs8[...]))

        @pl.when(i == 0)
        def _():
            load_prob("start")

        @pl.when(i == 1)
        def _():
            totals[1].start()


        slot = next_weights(s0 + 9)
        for i4 in range(4):
            sl = slice(i4 * BLK, (i4 + 1) * BLK)
            mid[:, sl] += dot(ctx[...], w_rows(slot, i4), 1, 1)
        slot = next_weights(s0 + 10)
        for i4 in range(4):
            sl = slice(i4 * BLK, (i4 + 1) * BLK)
            mid[:, sl] += dot(dkT[...], w_rows(slot, i4), 0, 1)

        @pl.when(i == 1)
        def _():
            totals[1].middle()
            totals[0].finish()

        slot = next_weights(s0 + 11)
        for i4 in range(4):
            sl = slice(i4 * BLK, (i4 + 1) * BLK)
            y = mid[:, sl] + dot(dvT[...], w_rows(slot, i4), 0, 1)
            xs[:, sl] = y
            xb[:, sl] = y.astype(BF)
        return carry

    def load_prob(op):
        getattr(pltpu.make_async_copy(P0, prob, psem), op)()

    totals = [
        Total(comm, phase, lo, hi, bg, planes, part, lines, total, asems)
        for phase, (lo, hi) in enumerate(((0, 18), (18, 20)))
    ]
    lax.fori_loop(0, LAYERS, layer_back, 0)
    results(xb, input_gradient, 3, "start")
    totals[1].finish()
    results(xb, input_gradient, 3, "wait")
    arrived(xb, layer_output, 0)
    arrived(xb, input_gradient, 3)


def finish(first, second, total, *rest):
    outs, (buf, rows, *sums), (into, outof) = rest[:9], rest[9:18], rest[18:]
    half = first.shape[1] // 2
    moves = []
    for i, (src, dst) in enumerate(((first, outs[0]), (second, outs[1]))):
        for j in range(2):
            part = pl.ds(j * half, half)
            k = 2 * i + j
            moves.append(
                (
                    pltpu.make_async_copy(src.at[:, part], buf.at[k], into.at[k]),
                    pltpu.make_async_copy(buf.at[k], dst.at[:, part], outof.at[k]),
                )
            )
    small = pltpu.make_async_copy(total, rows, into.at[4])
    small.start()
    for here, _ in moves:
        here.start()
    small.wait()
    done = [there for _, there in moves]
    for m, ks in enumerate(((9,), (8,), (0,), (1, 2, 3, 4), (5,), (6,), (7,))):
        for l in range(LAYERS):
            for at, k in enumerate(ks):
                for i in range(8):
                    sums[m][l : l + 1, at * D + i * 128 : at * D + (i + 1) * 128] = rows[(1 - l) * 10 + k, i : i + 1, :]
        done.append(pltpu.make_async_copy(sums[m], outs[2 + m], outof.at[4 + m]))
        done[-1].start()
    for here, there in moves:
        here.wait()
        there.start()
    for there in done:
        there.wait()


def on_device(
    hidden,
    cotangent,
    lengths,
    separators,
    type_table,
    projection_weight,
    output_weight,
    inner_weight,
    outer_weight,
    query_bias,
    value_bias,
    output_bias,
    inner_bias,
    outer_bias,
    first_gain,
    first_shift,
    second_gain,
    second_shift,
):
    nb = lax.axis_size("batch")
    nz, n = sizes(nb)
    gap = 2 if nb <= 16 else 1
    stages = 1 + (n - 1) + (nz - 1) + (n - 1)
    ticks = [k * gap for k in range(stages + 1)]
    if gap == 2:
        ticks[-2:] = ticks[-2] - 1, ticks[-1] - 1
    slots = ticks[-1] + gap
    plane = 2 * n * n
    T = 2 * hidden.shape[1]
    R = D // nb
    smem = pl.BlockSpec(memory_space=pltpu.SMEM)
    vmem = pl.BlockSpec(memory_space=pltpu.VMEM)
    hbm = pl.BlockSpec(memory_space=pl.ANY)
    sems = Comm.sems(nz, n)
    out_shape = (
        jax.ShapeDtypeStruct(hidden.shape, BF),
        jax.ShapeDtypeStruct(hidden.shape, BF),
        jax.ShapeDtypeStruct((LAYERS * 10, 8, 128), F32),
        jax.ShapeDtypeStruct((UNITS, nz, n, n, R, D), BF),
        jax.ShapeDtypeStruct((HEADS, T, T), BF),
    )
    dma = pltpu.SemaphoreType.DMA
    scratch = [
        pltpu.VMEM((2, D), BF),
        *(pltpu.VMEM((LAYERS, w), F32) for w in (D, D, D, FF, D, D, D, D, D)),
        pltpu.VMEM((UNITS, R, D), BF),
        pltpu.VMEM((T, D), BF),
        pltpu.VMEM((T, D), BF),
        pltpu.VMEM((T, D), F32),
        pltpu.VMEM((T, D), BF),
        pltpu.VMEM((5, T, D), BF),
        pltpu.VMEM((LAYERS, D, T), BF),
        pltpu.VMEM((HEADS, T, T), BF),
        pltpu.VMEM((T, D), F32),
        pltpu.VMEM((T, FF), BF),
        pltpu.VMEM((LAYERS, T, FF), BF),
        pltpu.VMEM((LAYERS, T, D), BF),
        pltpu.VMEM((LAYERS, T, D), BF),
        pltpu.VMEM((LAYERS, T, 1), F32),
        pltpu.VMEM((LAYERS, T, 1), F32),
        pltpu.VMEM((D, T), BF),
        pltpu.VMEM((D, T), BF),
        pltpu.VMEM((D, T), BF),
        pltpu.VMEM((3, nz, n, n, R, D), BF),
        pltpu.VMEM((LAYERS * 10, 8, 128), F32),
        pltpu.VMEM((plane, LAYERS * 10, 8, 128), F32),
        pltpu.VMEM((LAYERS * 10, 8, 128), F32),
        pltpu.VMEM((nz, LAYERS * 10, 8, 128), F32),
        pltpu.VMEM((8, D), F32),
        dma((slots,)),
        dma((slots, sems)),
        dma((slots,)),
        dma((slots,)),
        dma((2,)),
        dma((3,)),
        dma((6,)),
        dma(()),
        dma((10,)),
        dma((6,)),
        dma((2, 4)),
    ]
    out = pl.pallas_call(
        functools.partial(kernel, nz, n, ticks, slots),
        out_shape=out_shape,
        in_specs=[smem, smem] + [hbm] * 16,
        out_specs=(hbm, hbm, vmem, hbm, hbm),
        scratch_shapes=scratch,
        compiler_params=pltpu.CompilerParams(
            collective_id=0, has_side_effects=True, vmem_limit_bytes=60 * 2**20
        ),
        cost_estimate=pl.CostEstimate(flops=60 * 10**9, bytes_accessed=200 * 10**6, transcendentals=20 * 10**6),
    )(
        lengths,
        separators,
        hidden,
        cotangent,
        type_table,
        projection_weight,
        output_weight,
        inner_weight,
        outer_weight,
        query_bias,
        value_bias,
        output_bias,
        inner_bias,
        outer_bias,
        first_gain,
        first_shift,
        second_gain,
        second_shift,
    )
    half = hidden.shape[1] // 2
    sums = [query_bias, value_bias, output_bias, inner_bias, outer_bias, first_shift, second_shift]
    return tuple(
        pl.pallas_call(
            finish,
            out_shape=(
                jax.ShapeDtypeStruct(hidden.shape, BF),
                jax.ShapeDtypeStruct(hidden.shape, BF),
                *(jax.ShapeDtypeStruct(b.shape, F32) for b in sums),
            ),
            in_specs=[hbm] * 3,
            out_specs=(hbm,) * 9,
            scratch_shapes=[
                pltpu.VMEM((4, 2, half, D), BF),
                pltpu.VMEM((LAYERS * 10, 8, 128), F32),
                *(pltpu.VMEM(b.shape, F32) for b in sums),
                dma((5,)),
                dma((11,)),
            ],
        )(out[0], out[1], out[2])
    )


def solution(mesh):
    batched = P("batch", "blk", None)
    rows = P(None, "batch", None)
    return jax.shard_map(
        on_device,
        mesh=mesh,
        in_specs=(batched, batched, P("batch"), P("batch"), P(), rows, rows, rows, rows) + (P(),) * 9,
        out_specs=(batched, batched) + (P(),) * 7,
        check_vma=False,
    )
```

```python
import functools

import jax
import jax.numpy as jnp
from jax import lax
from jax.experimental import pallas as pl
from jax.experimental.pallas import tpu as pltpu
from jax.sharding import PartitionSpec as P

D = 1024
HEADS = 16
HEAD = 64
FF = 4096
LAYERS = 2
UNITS = 24
PER = 12
SPLIT = 640
BLK = 256
ROWS = 512
EPSILON = 1e-12
MASKED = -1000000000.0
MESH = pl.DeviceIdType.MESH
BF = jnp.bfloat16
F32 = jnp.float32


def sizes(batch):
    side = 2 ** ((batch.bit_length() - 1) // 3)
    return batch // (side * side), side


def lane(n):
    return 1 if n == 2 else 2 * (n - 1)


class Comm:
    def __init__(self, nz, n, gathered, stg, ssem, rsem, sib_s, sib_r, slots, ticks):
        self.nz, self.n, self.G, self.stg = nz, n, gathered, stg
        self.ssem, self.rsem, self.sib_s, self.sib_r = ssem, rsem, sib_s, sib_r
        self.slots, self.ticks = slots, ticks
        self.b = lax.axis_index("batch")
        self.c = lax.axis_index("blk")
        self.z, self.y, self.x = self.b // (n * n), (self.b // n) % n, self.b % n
        self.stages = 1 + (n - 1) + (nz - 1) + (n - 1)
        self.fbase = nz

    @staticmethod
    def sems(nz, n):
        return 2 * nz + 1 if n == 2 else nz + 2 * nz * lane(n)

    def cols(self, core):
        return pl.ds(0, SPLIT) if core == 0 else pl.ds(SPLIT, D - SPLIT)

    def setup(self, core, par, u):
        first_x = (core == 0) == (par == 0)
        cs, g, n = self.cols(core), self.G, self.n
        self.f, self.s = (self.x, self.y) if first_x else (self.y, self.x)
        self.fstr, self.sstr = (1, n) if first_x else (n, 1)
        if first_x:
            self.sl = lambda zi, fi, si: g.at[u, zi, si, fi, :, cs]
        else:
            self.sl = lambda zi, fi, si: g.at[u, zi, fi, si, :, cs]
        self.slot = u % self.slots

    def copy(self, ref, idx, to):
        return pltpu.make_async_remote_copy(
            src_ref=ref,
            dst_ref=ref,
            send_sem=self.ssem.at[self.slot],
            recv_sem=self.rsem.at[self.slot, idx],
            device_id=(to, self.c),
            device_id_type=MESH,
        )

    def dirs(self, length):
        return (0,) if length == 2 else (0, 1)

    def act(self, cp, mode):
        if mode == "start":
            cp.start()
        else:
            cp.wait_send()

    def arrive(self, ref, base, pos, length, stride, j, e, mode, last=False):
        if length == 2:
            to = self.b + stride * (1 - 2 * pos)
            if j == 0:
                self.act(self.copy(ref(pos), base, to), mode)
            elif mode == "start" and not last:
                self.copy(ref(1 - pos), base, to).wait_recv()
            return
        if j == 0:
            for d in (0, 1):

                @pl.when((pos + 1 < length) if d == 0 else (pos >= 1))
                def _():
                    self.act(self.copy(ref(pos), base + d, self.b + (stride if d == 0 else -stride)), mode)

            return
        src = pos - j if e == 0 else pos + j
        ok = (src >= 0) if e == 0 else (src < length)
        fwd = (pos + 1 < length) if e == 0 else (pos >= 1)
        to = self.b + (stride if e == 0 else -stride)
        if mode == "start":

            @pl.when(ok)
            def _():
                self.copy(ref(src), base + 2 * (j - 1) + e, to).wait_recv()

        if j < length - 1:

            @pl.when(ok & fwd)
            def _():
                self.act(self.copy(ref(src), base + 2 * j + e, to), mode)

    def hops(self):
        yield 0, 0
        for h in range(1, self.nz):
            for d in (0, 1):
                yield h, d

    def run(self, core, par, u, k, mode):
        self.setup(core, par, u)
        n, nz, z, b = self.n, self.nz, self.z, self.b
        lw = lane(n)
        sbase = self.fbase + nz * lw
        f, s = self.f, self.s
        pre = 0
        if core == 0:
            for j in range(n):
                if k is None or k == j:
                    for e in self.dirs(n) if j else (0,):
                        self.arrive(lambda i: self.sl(z, i, s), self.fbase, f, n, self.fstr, j, e, mode)
            pre = n - 1
        last = (n - 1) if core == 0 else 2 * (n - 1)
        for h, d in self.hops():
            zi = z - h if d == 0 else z + h
            fi = f if core == 1 else slice(None)

            def along_z():
                ref = self.sl(zi, fi, s)
                if h and mode == "start":
                    self.copy(ref, zi, b).wait_recv()
                if h < nz - 1:
                    for dd in (0, 1) if h == 0 else (d,):

                        @pl.when((z + 1 < nz) if dd == 0 else (z >= 1))
                        def _():
                            self.act(self.copy(ref, zi, b + (n * n if dd == 0 else -n * n)), mode)

            def in_plane(step):
                q = step
                if core == 1:
                    if step < n:
                        for e in self.dirs(n) if step else (0,):
                            self.arrive(
                                lambda i: self.sl(zi, i, s), self.fbase + zi * lw, f, n, self.fstr, step, e, mode
                            )
                    q = step - (n - 1)
                if q >= 0:
                    for e in self.dirs(n) if q else (0,):
                        at = sbase if n == 2 else sbase + zi * lw
                        self.arrive(lambda i: self.sl(zi, slice(None), i), at, s, n, self.sstr, q, e, mode, True)

            def events():
                for step in range(last + 1):
                    if k is None or k == pre + h + step:
                        if step == 0:
                            along_z()
                        in_plane(step)

            if k is None or 0 <= k - pre - h <= last:
                if h == 0:
                    events()
                else:
                    pl.when((zi >= 0) if d == 0 else (zi < nz))(events)
        if k == self.stages - 1:
            if n == 2:
                self.copy(self.sl(slice(None), slice(None), 1 - s), sbase, b).wait_recv()
            self.sibling(core, u).start()

    def drain(self, core, par, u):
        n, nz = self.n, self.nz
        if n == 2:
            slot, cs = u % self.slots, self.cols(core)
            for z in range(nz):
                along = (z + 1 if z < nz - 1 else 0) + (nz - z if z else 0)
                pieces = 1 + 2 * along + 2 * nz if core == 0 else along + 3 * nz
                same = self.stg.at[0:pieces, :, cs]

                @pl.when(self.z == z)
                def _():
                    pltpu.make_async_remote_copy(
                        src_ref=same,
                        dst_ref=same,
                        send_sem=self.ssem.at[slot],
                        recv_sem=self.rsem.at[slot, 0],
                        device_id=(self.b, 1 - self.c),
                        device_id_type=MESH,
                    ).wait_send()

        else:
            self.run(core, par, u, None, "drain")
        self.sibling(core, u).wait_send()

    def sibling(self, core, u):
        ref = self.G.at[u, :, :, :, :, self.cols(core)]
        return pltpu.make_async_remote_copy(
            src_ref=ref,
            dst_ref=ref,
            send_sem=self.sib_s.at[u % self.slots],
            recv_sem=self.sib_r.at[u % self.slots],
            device_id=(self.b, 1 - self.c),
            device_id_type=MESH,
        )

    def tick(self, t, part):
        order = [self.stages, *reversed(range(self.stages))]
        cuts = (0, len(order) // 3 + 1, 2 * len(order) // 3 + 1, len(order))
        for core in (0, 1):
            for odd in (0, 1):

                @pl.when((self.c == core) & (t % 2 == odd))
                def _():
                    for k in order[cuts[part] : cuts[part + 1]]:
                        u = t - self.ticks[k]
                        par = (odd + self.ticks[k]) % 2

                        @pl.when((u >= 0) & (u < UNITS))
                        def _():
                            if k == self.stages:
                                self.drain(core, par, u)
                            else:
                                self.run(core, par, u, k, "start")

    def barrier(self, meanwhile):
        bar = pltpu.get_barrier_semaphore()
        plane, me = 2 * self.n * self.n, self.place()

        def in_plane(i, carry):
            to = (me + i) % plane
            pl.semaphore_signal(bar, inc=1, device_id=self.at(to), device_id_type=MESH)
            return carry

        def along_z(i, carry):
            pl.semaphore_signal(bar, inc=1, device_id=self.along((self.z + i) % self.nz), device_id_type=MESH)
            return carry

        lax.fori_loop(1, plane, in_plane, 0, unroll=plane <= 8)
        lax.fori_loop(1, self.nz, along_z, 0, unroll=plane <= 8)
        meanwhile()
        pl.semaphore_wait(bar, plane - 1 + self.nz - 1)

    def place(self):
        return (self.b % (self.n * self.n)) * 2 + self.c

    def at(self, p):
        return (self.z * self.n * self.n + p // 2, p % 2)

    def along(self, z):
        return (z * self.n * self.n + self.b % (self.n * self.n), self.c)


class Total:
    def __init__(self, comm, phase, lo, hi, bg, planes, part, lines, total, sems):
        self.comm, self.phase, self.rows = comm, phase, pl.ds(lo, hi - lo)
        self.bg, self.planes, self.part, self.lines, self.total = bg, planes, part, lines, total
        self.sems = sems

    def ends(self, second):
        if second:
            return self.part, self.lines, self.comm.z, self.comm.nz
        return self.bg, self.planes, self.comm.place(), 2 * self.comm.n * self.comm.n

    def copy(self, second, src, dst, to):
        return pltpu.make_async_remote_copy(
            src_ref=src,
            dst_ref=dst,
            send_sem=self.sems.at[self.phase, 2 * second],
            recv_sem=self.sems.at[self.phase, 2 * second + 1],
            device_id=to,
            device_id_type=MESH,
        )

    def send(self, second):
        comm, rows = self.comm, self.rows
        src, dst, me, count = self.ends(second)

        def one(i, carry):
            peer = (me + i) % count
            to = comm.along(peer) if second else comm.at(peer)
            self.copy(second, src.at[rows], dst.at[me, rows], to).start()
            return carry

        lax.fori_loop(1, count, one, 0, unroll=count <= 8)

    def every(self, second):
        _, dst, _, count = self.ends(second)
        all_of = dst.at[pl.ds(0, count - 1), self.rows]
        return self.copy(second, all_of, all_of, (self.comm.b, 1 - self.comm.c))

    def add(self, second):
        src, buf, me, count = self.ends(second)
        out = self.total if second else self.part
        self.every(second).wait_recv()
        buf[me, self.rows] = src[self.rows]

        def one(i, acc):
            return acc + buf[i, self.rows]

        out[self.rows] = lax.fori_loop(1, count, one, buf[0, self.rows], unroll=count <= 8)
        self.every(second).wait_send()

    def start(self):
        self.send(0)

    def middle(self):
        self.add(0)
        self.send(1)

    def finish(self):
        self.add(1)


def dot(a, b, ca=1, cb=0):
    return lax.dot_general(a, b, (((ca,), (cb,)), ((), ())), preferred_element_type=F32)


def fold(values):
    rows, cols = values.shape
    return jnp.sum(values.reshape(rows // 8, 8, cols), axis=0)


def colsum(values):
    return jnp.sum(values, axis=0, keepdims=True)


def kernel(
    nz,
    n,
    ticks,
    slots,
    lengths,
    separators,
    hidden,
    cotangent,
    type_table_in,
    proj,
    outw,
    inner,
    outer,
    query_bias_in,
    value_bias_in,
    output_bias_in,
    inner_bias_in,
    outer_bias_in,
    first_gain_in,
    first_shift_in,
    second_gain_in,
    second_shift_in,
    layer_output,
    input_gradient,
    total,
    G,
    P0,
    type_table,
    query_bias,
    value_bias,
    output_bias,
    inner_bias,
    outer_bias,
    first_gain,
    first_shift,
    second_gain,
    second_shift,
    stg,
    xin,
    cot,
    xs,
    xb,
    qkv,
    qT,
    prob,
    mid,
    act,
    gp,
    n1,
    n2,
    r1,
    r2,
    gcT,
    dkT,
    dvT,
    wbuf,
    bg,
    planes,
    part,
    lines,
    dqs8,
    ssem,
    rsem,
    sib_s,
    sib_r,
    lsem,
    wsem,
    xsem,
    psem,
    vsem,
    osem,
    asems,
):
    nb = nz * n * n
    R = D // nb
    T = xs.shape[0]
    half = T // 2
    quarter = nb // 4
    comm = Comm(nz, n, G, stg, ssem, rsem, sib_s, sib_r, slots, ticks)
    c = comm.c
    other = (comm.b, 1 - c)
    ctx = xin

    def stage_in():
        for l in range(LAYERS):
            for u in range(8):
                m, j = (proj, u) if u < 3 else (outw, 0) if u == 3 else (inner, u - 4)
                pltpu.make_async_copy(m.at[l, :, pl.ds(j * D, D)], stg.at[l * PER + u], lsem.at[0]).start()
            for j in range(4):
                for g in range(4):
                    pltpu.make_async_copy(
                        outer.at[l, pl.ds(g * R, R), pl.ds(j * BLK, BLK)],
                        stg.at[l * PER + 8 + j, :, pl.ds(g * BLK, BLK)],
                        lsem.at[0],
                    ).start()

    def place():
        pltpu.make_async_copy(stg, stg, lsem.at[0]).wait()
        for core in (0, 1):

            @pl.when(c == core)
            def _():
                cs = comm.cols(core)
                to = G.at[:, comm.z, comm.y, comm.x, :, cs]
                cp = pltpu.make_async_copy(stg.at[:, :, cs], to, lsem.at[1])
                cp.start()
                cp.wait()

    def exchange(op):
        for i, (src, dst) in enumerate(((hidden, xin), (cotangent, cot))):
            rows = pl.ds(pl.multiple_of(c * half, half), half)
            lc = pltpu.make_async_copy(src.at[c], dst.at[rows], xsem.at[3 * i])
            rc = pltpu.make_async_remote_copy(
                src_ref=src.at[1 - c],
                dst_ref=dst.at[rows],
                send_sem=xsem.at[3 * i + 1],
                recv_sem=xsem.at[3 * i + 2],
                device_id=other,
                device_id_type=MESH,
            )
            getattr(lc, op)()
            getattr(rc, op)()

    vectors = (
        (type_table_in, type_table),
        (query_bias_in, query_bias),
        (value_bias_in, value_bias),
        (output_bias_in, output_bias),
        (inner_bias_in, inner_bias),
        (outer_bias_in, outer_bias),
        (first_gain_in, first_gain),
        (first_shift_in, first_shift),
        (second_gain_in, second_gain),
        (second_shift_in, second_shift),
    )

    def small(op):
        for i, (src, dst) in enumerate(vectors):
            getattr(pltpu.make_async_copy(src, dst, vsem.at[i]), op)()

    def begin():
        stage_in()
        small("start")

    comm.barrier(begin)
    exchange("start")
    place()

    def row(ref, l):
        return ref[pl.ds(l, 1), :]

    def cols(i, width=BLK):
        return pl.ds(pl.multiple_of(i * width, width), width)

    lanes = lax.broadcasted_iota(jnp.int32, (T, 2 * HEAD), 1)
    halves = (lanes < HEAD, lanes >= HEAD)

    def init_x():
        exchange("wait")
        small("wait")
        t0 = type_table[0:1, :].astype(F32)
        t1 = type_table[1:2, :].astype(F32)
        sep = separators[c]

        def rows_of(i, carry):
            rs = pl.ds(pl.multiple_of(i * ROWS, ROWS), ROWS)
            at = i * ROWS + lax.broadcasted_iota(jnp.int32, (ROWS, D), 0)
            second = (at > sep).astype(F32)
            x = xin[rs, :].astype(F32) + t0 + second * (t1 - t0)
            xs[rs, :] = x
            xb[rs, :] = x.astype(BF)
            return carry

        lax.fori_loop(0, T // ROWS, rows_of, 0)

    def load_unit(u, slot):
        pltpu.make_async_copy(G.at[u], wbuf.at[slot], wsem.at[slot]).start()

    def load_rows(l, f, slot):
        q = nz // 4
        for j in range(4):
            pltpu.make_async_copy(
                G.at[l * PER + 8 + j, pl.ds(f * q, q)], wbuf.at[slot, pl.ds(j * q, q)], wsem.at[slot]
            ).start()

    def loaded(slot):
        pltpu.make_async_copy(G.at[0], wbuf.at[slot], wsem.at[slot]).wait()

    def w_cols(slot, g):
        return wbuf[slot, :, :, :, :, cols(g)].reshape(D, BLK)

    def w_rows(slot, i):
        return wbuf[slot, pl.ds(i * (nz // 4), nz // 4)].reshape(BLK, D)

    def stacked(chips):
        return jnp.concatenate([w[:, g * BLK : (g + 1) * BLK] for w in chips for g in range(4)], axis=0)

    def chip(slot, i):
        return wbuf[slot, i // (n * n), (i // n) % n, i % n]

    def o_rows(slot, i):
        per = nb // 16
        return jnp.concatenate(
            [stacked([chip(slot, j * quarter + i * per + w) for w in range(per)]) for j in range(4)], axis=1
        )

    def o_cols(slot, i):
        return stacked([chip(slot, i * quarter + w) for w in range(quarter)])

    def norm_rows(z, gain, shift):
        average = jnp.mean(z, axis=1, keepdims=True)
        centred = z - average
        r = lax.rsqrt(jnp.mean(centred * centred, axis=1, keepdims=True) + EPSILON)
        normed = centred * r
        return normed, r, normed * gain + shift

    def do_qkv(l, j, slot, lo, hi):
        is_q, is_v = (j == 0).astype(F32), (j == 2).astype(F32)
        at = jnp.where(j == 0, 0, 2 * l + j)

        for g in range(lo, hi):
            sl = slice(g * BLK, (g + 1) * BLK)
            bias = query_bias[pl.ds(l, 1), sl] * is_q + value_bias[pl.ds(l, 1), sl] * is_v
            qkv[at, :, sl] = (dot(xb[...], w_cols(slot, g)) + bias).astype(BF)

    def do_attention(l, lo, hi):
        key_ok = lax.broadcasted_iota(jnp.int32, (1, T), 1) < lengths[c]

        def pair(hp, carry):
            cs = cols(hp, 2 * HEAD)
            q2, k2, v2 = qkv[0, :, cs], qkv[2 * l + 1, :, cs], qkv[2 * l + 2, :, cs]
            outs = []
            for hh in (0, 1):
                qm = jnp.where(halves[hh], q2 * BF(HEAD**-0.5), BF(0))
                s = jnp.where(key_ok, dot(qm, k2, 1, 1), MASKED)
                e = jnp.exp(s - jnp.max(s, axis=1, keepdims=True))
                p = (e * (1.0 / jnp.sum(e, axis=1, keepdims=True))).astype(BF)
                prob[2 * hp + hh] = p
                outs.append(dot(p, v2))
            ctx[:, cs] = jnp.where(halves[0], outs[0], outs[1]).astype(BF)
            qT[l, cs, :] = q2.T
            return carry

        lax.fori_loop(lo, hi, pair, 0)

    def do_out(l, slot, part):
        if part == 2:
            return do_norm1(l)
        for g in range(4):
            sl = slice(g * BLK, (g + 1) * BLK)
            mid[:, sl] = xs[:, sl] + dot(ctx[...], w_cols(slot, g)) + output_bias[pl.ds(l, 1), sl]

    def do_norm1(l):
        gain, shift = row(first_gain, l), row(first_shift, l)

        def rows_of(i, carry):
            rs = pl.ds(pl.multiple_of(i * ROWS, ROWS), ROWS)
            normed, r, y = norm_rows(mid[rs, :], gain, shift)
            n1[l, rs, :] = normed.astype(BF)
            r1[l, rs, :] = r
            mid[rs, :] = y
            xb[rs, :] = y.astype(BF)
            return carry

        lax.fori_loop(0, T // ROWS, rows_of, 0)

    def do_inner(l, pair):
        for of in (0, 1):
            i = 2 * pair + of
            cs = cols(i)
            h = dot(xb[...], w_cols((l * PER + 4 + pair // 2) % 3, i % 4)) + inner_bias[pl.ds(l, 1), cs]
            cdf = 0.5 + 0.5 * lax.erf(h * (0.5**0.5))
            act[:, cs] = (h * cdf).astype(BF)
            gp[l, :, cs] = (cdf + h * (jnp.exp(-0.5 * h * h) * 0.3989422804014327)).astype(BF)

    def do_outer(l, j, slot):
        cs = cols(j)
        y = mid[:, cs] + outer_bias[pl.ds(l, 1), cs]
        for i in range(4):
            y = y + dot(act[:, i * D : (i + 1) * D], o_cols(slot, i))
        xs[:, cs] = y

    def do_norm2(l):
        gain, shift = row(second_gain, l), row(second_shift, l)

        def rows_of(i, carry):
            rs = pl.ds(pl.multiple_of(i * ROWS, ROWS), ROWS)
            normed, r, y = norm_rows(xs[rs, :], gain, shift)
            n2[l, rs, :] = normed.astype(BF)
            r2[l, rs, :] = r
            yb = y.astype(BF)
            xb[rs, :] = yb
            ctx[rs, :] = yb
            xs[rs, :] = jnp.where(l == LAYERS - 1, cot[rs, :].astype(F32), y)
            return carry

        lax.fori_loop(0, T // ROWS, rows_of, 0)

    def save_prob(op):
        getattr(pltpu.make_async_copy(prob, P0, psem), op)()

    def compute(v, slot, part):
        l, k = v // PER, v % PER

        def choose(*of_k):
            out = jnp.int32(of_k[-1])
            for i, value in enumerate(of_k[:-1]):
                out = jnp.where(k == i, value, out)
            return out

        pl.when(k < 3)(lambda: do_qkv(l, k, slot, (0, 2, 3)[part], (2, 3, 4)[part]))

        first = {0: (0, 0, 0, 1, 4, 7), 1: (0, 0, 0, 2, 5), 2: (0, 0, 0, 3, 6)}[part]
        when = {0: (k >= 3) & (k <= 5), 1: (k == 3) | (k == 4), 2: (k >= 2) & (k <= 4)}[part]
        pl.when(when)(lambda: do_attention(l, choose(*first), choose(*first) + 1))

        if part:

            @pl.when(k == 5)
            def _():
                if part == 1:
                    pl.when(l == 0)(lambda: save_prob("start"))
                do_out(l, (v + 1) % 3, part)

        last = 7 if part == 2 else 8
        pl.when((k >= 6) & (k <= last))(lambda: do_inner(l, 3 * (k - 6) + part))
        if part != 1:
            pl.when(k > 8 if part == 0 else k == 8)(lambda: do_outer(l, k - 8, slot))
        if part == 1:

            @pl.when(k == PER - 1)
            def _():
                pl.when(l == 0)(lambda: save_prob("wait"))
                do_norm2(l)

    def load(s, slot):
        l, k = 1 - s // PER, s % PER
        rows = (k < 8) & (k % 2 == 0)
        pl.when(rows)(lambda: load_rows(l, k // 2, slot))
        unit = l * PER + jnp.where(k < 8, 4 + k // 2, jnp.where(k == 8, 3, k - 9))
        pl.when(jnp.logical_not(rows))(lambda: load_unit(unit, slot))

    lag = ticks[comm.stages - 1] + 1

    def main(t, carry):
        v = t - lag
        slot = (v + 3 * lag) % 3
        ready = (v >= 0) & (v < UNITS)

        comm.tick(t, 0)
        pl.when(t == 1)(init_x)

        @pl.when(ready)
        def _():
            loaded(slot)

            @pl.when(v == UNITS - 1)
            def _():
                load(0, 0)
                load(1, 1)

            compute(v, slot, 0)

        comm.tick(t, 1)
        pl.when(ready)(lambda: compute(v, slot, 1))
        comm.tick(t, 2)

        @pl.when((v >= -1) & (v < UNITS - 1))
        def _():
            for core in (0, 1):

                @pl.when(c == core)
                def _():
                    comm.sibling(1 - core, v + 1).wait_recv()

            load_unit(v + 1, (slot + 1) % 3)

        pl.when(ready)(lambda: compute(v, slot, 2))
        return carry

    lax.fori_loop(0, UNITS + ticks[comm.stages], main, 0)

    def results(src, out, base, op):
        mine = pl.ds(pl.multiple_of(c * half, half), half)
        theirs = pl.ds(pl.multiple_of((1 - c) * half, half), half)
        lc = pltpu.make_async_copy(src.at[mine], out.at[c], osem.at[base])
        rc = pltpu.make_async_remote_copy(
            src_ref=src.at[theirs],
            dst_ref=out.at[c],
            send_sem=osem.at[base + 1],
            recv_sem=osem.at[base + 2],
            device_id=other,
            device_id_type=MESH,
        )
        if op == "start":
            rc.start()
            lc.start()
        else:
            rc.wait_send()
            lc.wait()

    def arrived(src, out, base):
        rows = pl.ds(0, half)
        pltpu.make_async_remote_copy(
            src_ref=src.at[rows],
            dst_ref=out.at[1 - c],
            send_sem=osem.at[base + 1],
            recv_sem=osem.at[base + 2],
            device_id=other,
            device_id_type=MESH,
        ).wait_recv()

    def next_weights(s):
        loaded(s % 3)
        pl.when(s + 2 < UNITS)(lambda: load(s + 2, (s + 2) % 3))
        return s % 3

    def keep_sum(l, k, values):
        for i in range(values.shape[1] // 128):
            bg[(1 - l) * 10 + k, i : i + 1, :] = values[:, i * 128 : (i + 1) * 128]

    def norm_back(l, source, normed, r_ref, gain_ref, at_shift, at_bias, keep):
        gain = row(gain_ref, l)

        def rows_of(i, carry):
            sum_g, sum_z = carry
            rs = pl.ds(pl.multiple_of(i * ROWS, ROWS), ROWS)
            g = source[rs, :]
            nv = normed[l, rs, :].astype(F32)
            u = g * gain
            gz = r_ref[l, rs, :] * (
                u - jnp.mean(u, axis=1, keepdims=True) - nv * jnp.mean(u * nv, axis=1, keepdims=True)
            )
            keep[rs, :] = gz
            xb[rs, :] = gz.astype(BF)
            return sum_g + fold(g), sum_z + fold(gz)

        zero = jnp.zeros((8, D), F32)
        sum_g, sum_z = lax.fori_loop(0, T // ROWS, rows_of, (zero, zero))
        keep_sum(l, at_shift, colsum(sum_g))
        keep_sum(l, at_bias, colsum(sum_z))

    results(ctx, layer_output, 0, "start")

    def layer_back(i, carry):
        l = LAYERS - 1 - i
        s0 = i * PER
        norm_back(l, xs, n2, r2, second_gain, 7, 5, mid)

        def ff(f, carry):
            slot = next_weights(s0 + 2 * f)
            for i4 in range(4):
                cs = cols(f * 4 + i4)
                gh = dot(xb[...], o_rows(slot, i4), 1, 1) * gp[l, :, cs].astype(F32)
                sums = colsum(fold(gh))
                bg[(1 - l) * 10 + 1 + f, 2 * i4 : 2 * i4 + 1, :] = sums[:, :128]
                bg[(1 - l) * 10 + 1 + f, 2 * i4 + 1 : 2 * i4 + 2, :] = sums[:, 128:]
                act[:, cs] = gh.astype(BF)
            slot = next_weights(s0 + 2 * f + 1)
            for i4 in range(4):
                sl = slice(i4 * BLK, (i4 + 1) * BLK)
                mid[:, sl] += dot(act[:, cols(f, D)], w_rows(slot, i4), 1, 1)
            return carry

        lax.fori_loop(0, 4, ff, 0)
        norm_back(l, mid, n1, r1, first_gain, 6, 0, mid)
        pl.when(i == 1)(totals[0].start)
        slot = next_weights(s0 + 8)
        for i4 in range(4):
            sl = slice(i4 * BLK, (i4 + 1) * BLK)
            gc = dot(xb[...], w_rows(slot, i4), 1, 1).astype(BF)
            sums = colsum(fold(gc.astype(F32)))
            bg[(1 - l) * 10 + 8, 2 * i4 : 2 * i4 + 1, :] = sums[:, :128]
            bg[(1 - l) * 10 + 8, 2 * i4 + 1 : 2 * i4 + 2, :] = sums[:, 128:]
            qkv[0, :, sl] = gc
            gcT[sl, :] = gc.T

        pl.when(i == 0)(lambda: results(ctx, layer_output, 0, "wait"))

        @pl.when(i == 1)
        def _():
            load_prob("wait")

        def pair(hp, carry):
            cs = cols(hp, 2 * HEAD)
            gc2, k2, v2 = qkv[0, :, cs], qkv[2 * l + 1, :, cs], qkv[2 * l + 2, :, cs]
            dqs = []
            for hh in (0, 1):
                hs = pl.ds(pl.multiple_of((2 * hp + hh) * HEAD, HEAD), HEAD)
                p = prob[2 * hp + hh]
                pf = p.astype(F32)
                gm = jnp.where(halves[hh], gc2 * BF(HEAD**-0.5), BF(0))
                dp = dot(gm, v2, 1, 1)
                total = jnp.sum(dp * pf, axis=1, keepdims=True)
                ds = (pf * (dp - total)).astype(BF)
                dqs.append(dot(ds, k2))
                dkT[hs, :] = dot(qT[l, hs, :], ds).astype(BF)
                dvT[hs, :] = dot(gcT[hs, :], p).astype(BF)
            dq = jnp.where(halves[0], dqs[0], dqs[1])
            dqs8[:, cs] = fold(dq)
            ctx[:, cs] = dq.astype(BF)
            return carry

        def four(j, carry):
            lax.fori_loop(0, 4, lambda h, x: pair(4 * j + h, x), 0, unroll=4)
            pl.when((i == 1) & (j == 0))(totals[0].middle)
            return carry

        lax.fori_loop(0, HEADS // 8, four, 0)
        keep_sum(l, 9, colsum(dqs8[...]))

        @pl.when(i == 0)
        def _():
            load_prob("start")

        @pl.when(i == 1)
        def _():
            totals[1].start()


        slot = next_weights(s0 + 9)
        for i4 in range(4):
            sl = slice(i4 * BLK, (i4 + 1) * BLK)
            mid[:, sl] += dot(ctx[...], w_rows(slot, i4), 1, 1)
        slot = next_weights(s0 + 10)
        for i4 in range(4):
            sl = slice(i4 * BLK, (i4 + 1) * BLK)
            mid[:, sl] += dot(dkT[...], w_rows(slot, i4), 0, 1)

        @pl.when(i == 1)
        def _():
            totals[1].middle()
            totals[0].finish()

        slot = next_weights(s0 + 11)
        for i4 in range(4):
            sl = slice(i4 * BLK, (i4 + 1) * BLK)
            y = mid[:, sl] + dot(dvT[...], w_rows(slot, i4), 0, 1)
            xs[:, sl] = y
            xb[:, sl] = y.astype(BF)
        return carry

    def load_prob(op):
        getattr(pltpu.make_async_copy(P0, prob, psem), op)()

    totals = [
        Total(comm, phase, lo, hi, bg, planes, part, lines, total, asems)
        for phase, (lo, hi) in enumerate(((0, 18), (18, 20)))
    ]
    lax.fori_loop(0, LAYERS, layer_back, 0)
    results(xb, input_gradient, 3, "start")
    totals[1].finish()
    results(xb, input_gradient, 3, "wait")
    arrived(xb, layer_output, 0)
    arrived(xb, input_gradient, 3)


def finish(first, second, total, *rest):
    outs, (buf, rows, *sums), (into, outof) = rest[:9], rest[9:18], rest[18:]
    half = first.shape[1] // 2
    moves = []
    for i, (src, dst) in enumerate(((first, outs[0]), (second, outs[1]))):
        for j in range(2):
            part = pl.ds(j * half, half)
            k = 2 * i + j
            moves.append(
                (
                    pltpu.make_async_copy(src.at[:, part], buf.at[k], into.at[k]),
                    pltpu.make_async_copy(buf.at[k], dst.at[:, part], outof.at[k]),
                )
            )
    small = pltpu.make_async_copy(total, rows, into.at[4])
    small.start()
    for here, _ in moves:
        here.start()
    small.wait()
    done = [there for _, there in moves]
    for m, ks in enumerate(((9,), (8,), (0,), (1, 2, 3, 4), (5,), (6,), (7,))):
        for l in range(LAYERS):
            for at, k in enumerate(ks):
                for i in range(8):
                    sums[m][l : l + 1, at * D + i * 128 : at * D + (i + 1) * 128] = rows[(1 - l) * 10 + k, i : i + 1, :]
        done.append(pltpu.make_async_copy(sums[m], outs[2 + m], outof.at[4 + m]))
        done[-1].start()
    for here, there in moves:
        here.wait()
        there.start()
    for there in done:
        there.wait()


def on_device(
    hidden,
    cotangent,
    lengths,
    separators,
    type_table,
    projection_weight,
    output_weight,
    inner_weight,
    outer_weight,
    query_bias,
    value_bias,
    output_bias,
    inner_bias,
    outer_bias,
    first_gain,
    first_shift,
    second_gain,
    second_shift,
):
    nb = lax.axis_size("batch")
    nz, n = sizes(nb)
    gap = 2 if nb <= 16 else 1
    stages = 1 + (n - 1) + (nz - 1) + (n - 1)
    ticks = [k * gap for k in range(stages + 1)]
    if gap == 2:
        ticks[-2:] = ticks[-2] - 1, ticks[-1] - 1
    slots = ticks[-1] + gap
    plane = 2 * n * n
    T = 2 * hidden.shape[1]
    R = D // nb
    smem = pl.BlockSpec(memory_space=pltpu.SMEM)
    vmem = pl.BlockSpec(memory_space=pltpu.VMEM)
    hbm = pl.BlockSpec(memory_space=pl.ANY)
    sems = Comm.sems(nz, n)
    out_shape = (
        jax.ShapeDtypeStruct(hidden.shape, BF),
        jax.ShapeDtypeStruct(hidden.shape, BF),
        jax.ShapeDtypeStruct((LAYERS * 10, 8, 128), F32),
        jax.ShapeDtypeStruct((UNITS, nz, n, n, R, D), BF),
        jax.ShapeDtypeStruct((HEADS, T, T), BF),
    )
    dma = pltpu.SemaphoreType.DMA
    scratch = [
        pltpu.VMEM((2, D), BF),
        *(pltpu.VMEM((LAYERS, w), F32) for w in (D, D, D, FF, D, D, D, D, D)),
        pltpu.VMEM((UNITS, R, D), BF),
        pltpu.VMEM((T, D), BF),
        pltpu.VMEM((T, D), BF),
        pltpu.VMEM((T, D), F32),
        pltpu.VMEM((T, D), BF),
        pltpu.VMEM((5, T, D), BF),
        pltpu.VMEM((LAYERS, D, T), BF),
        pltpu.VMEM((HEADS, T, T), BF),
        pltpu.VMEM((T, D), F32),
        pltpu.VMEM((T, FF), BF),
        pltpu.VMEM((LAYERS, T, FF), BF),
        pltpu.VMEM((LAYERS, T, D), BF),
        pltpu.VMEM((LAYERS, T, D), BF),
        pltpu.VMEM((LAYERS, T, 1), F32),
        pltpu.VMEM((LAYERS, T, 1), F32),
        pltpu.VMEM((D, T), BF),
        pltpu.VMEM((D, T), BF),
        pltpu.VMEM((D, T), BF),
        pltpu.VMEM((3, nz, n, n, R, D), BF),
        pltpu.VMEM((LAYERS * 10, 8, 128), F32),
        pltpu.VMEM((plane, LAYERS * 10, 8, 128), F32),
        pltpu.VMEM((LAYERS * 10, 8, 128), F32),
        pltpu.VMEM((nz, LAYERS * 10, 8, 128), F32),
        pltpu.VMEM((8, D), F32),
        dma((slots,)),
        dma((slots, sems)),
        dma((slots,)),
        dma((slots,)),
        dma((2,)),
        dma((3,)),
        dma((6,)),
        dma(()),
        dma((10,)),
        dma((6,)),
        dma((2, 4)),
    ]
    out = pl.pallas_call(
        functools.partial(kernel, nz, n, ticks, slots),
        out_shape=out_shape,
        in_specs=[smem, smem] + [hbm] * 16,
        out_specs=(hbm, hbm, vmem, hbm, hbm),
        scratch_shapes=scratch,
        compiler_params=pltpu.CompilerParams(
            collective_id=0, has_side_effects=True, vmem_limit_bytes=60 * 2**20
        ),
        cost_estimate=pl.CostEstimate(flops=60 * 10**9, bytes_accessed=200 * 10**6, transcendentals=20 * 10**6),
    )(
        lengths,
        separators,
        hidden,
        cotangent,
        type_table,
        projection_weight,
        output_weight,
        inner_weight,
        outer_weight,
        query_bias,
        value_bias,
        output_bias,
        inner_bias,
        outer_bias,
        first_gain,
        first_shift,
        second_gain,
        second_shift,
    )
    half = hidden.shape[1] // 2
    sums = [query_bias, value_bias, output_bias, inner_bias, outer_bias, first_shift, second_shift]
    return tuple(
        pl.pallas_call(
            finish,
            out_shape=(
                jax.ShapeDtypeStruct(hidden.shape, BF),
                jax.ShapeDtypeStruct(hidden.shape, BF),
                *(jax.ShapeDtypeStruct(b.shape, F32) for b in sums),
            ),
            in_specs=[hbm] * 3,
            out_specs=(hbm,) * 9,
            scratch_shapes=[
                pltpu.VMEM((4, 2, half, D), BF),
                pltpu.VMEM((LAYERS * 10, 8, 128), F32),
                *(pltpu.VMEM(b.shape, F32) for b in sums),
                dma((5,)),
                dma((11,)),
            ],
        )(out[0], out[1], out[2])
    )


def solution(mesh):
    batched = P("batch", "blk", None)
    rows = P(None, "batch", None)
    return jax.shard_map(
        on_device,
        mesh=mesh,
        in_specs=(batched, batched, P("batch"), P("batch"), P(), rows, rows, rows, rows) + (P(),) * 9,
        out_specs=(batched, batched) + (P(),) * 7,
        check_vma=False,
    )
```

```python
import functools

import jax
import jax.numpy as jnp
from jax import lax
from jax.experimental import pallas as pl
from jax.experimental.pallas import tpu as pltpu
from jax.sharding import PartitionSpec as P

D = 1024
HEADS = 16
HEAD = 64
FF = 4096
LAYERS = 2
UNITS = 24
PER = 12
SPLIT = 640
BLK = 256
ROWS = 512
EPSILON = 1e-12
MASKED = -1000000000.0
MESH = pl.DeviceIdType.MESH
BF = jnp.bfloat16
F32 = jnp.float32


def sizes(batch):
    side = 2 ** ((batch.bit_length() - 1) // 3)
    return batch // (side * side), side


def lane(n):
    return 1 if n == 2 else 2 * (n - 1)


class Comm:
    def __init__(self, nz, n, gathered, stg, ssem, rsem, sib_s, sib_r, slots, ticks):
        self.nz, self.n, self.G, self.stg = nz, n, gathered, stg
        self.ssem, self.rsem, self.sib_s, self.sib_r = ssem, rsem, sib_s, sib_r
        self.slots, self.ticks = slots, ticks
        self.b = lax.axis_index("batch")
        self.c = lax.axis_index("blk")
        self.z, self.y, self.x = self.b // (n * n), (self.b // n) % n, self.b % n
        self.stages = 1 + (n - 1) + (nz - 1) + (n - 1)
        self.fbase = nz

    @staticmethod
    def sems(nz, n):
        return 2 * nz + 1 if n == 2 else nz + 2 * nz * lane(n)

    def cols(self, core):
        return pl.ds(0, SPLIT) if core == 0 else pl.ds(SPLIT, D - SPLIT)

    def setup(self, core, par, u):
        first_x = (core == 0) == (par == 0)
        cs, g, n = self.cols(core), self.G, self.n
        self.f, self.s = (self.x, self.y) if first_x else (self.y, self.x)
        self.fstr, self.sstr = (1, n) if first_x else (n, 1)
        if first_x:
            self.sl = lambda zi, fi, si: g.at[u, zi, si, fi, :, cs]
        else:
            self.sl = lambda zi, fi, si: g.at[u, zi, fi, si, :, cs]
        self.slot = u % self.slots

    def copy(self, ref, idx, to):
        return pltpu.make_async_remote_copy(
            src_ref=ref,
            dst_ref=ref,
            send_sem=self.ssem.at[self.slot],
            recv_sem=self.rsem.at[self.slot, idx],
            device_id=(to, self.c),
            device_id_type=MESH,
        )

    def dirs(self, length):
        return (0,) if length == 2 else (0, 1)

    def act(self, cp, mode):
        if mode == "start":
            cp.start()
        else:
            cp.wait_send()

    def arrive(self, ref, base, pos, length, stride, j, e, mode, last=False):
        if length == 2:
            to = self.b + stride * (1 - 2 * pos)
            if j == 0:
                self.act(self.copy(ref(pos), base, to), mode)
            elif mode == "start" and not last:
                self.copy(ref(1 - pos), base, to).wait_recv()
            return
        if j == 0:
            for d in (0, 1):

                @pl.when((pos + 1 < length) if d == 0 else (pos >= 1))
                def _():
                    self.act(self.copy(ref(pos), base + d, self.b + (stride if d == 0 else -stride)), mode)

            return
        src = pos - j if e == 0 else pos + j
        ok = (src >= 0) if e == 0 else (src < length)
        fwd = (pos + 1 < length) if e == 0 else (pos >= 1)
        to = self.b + (stride if e == 0 else -stride)
        if mode == "start":

            @pl.when(ok)
            def _():
                self.copy(ref(src), base + 2 * (j - 1) + e, to).wait_recv()

        if j < length - 1:

            @pl.when(ok & fwd)
            def _():
                self.act(self.copy(ref(src), base + 2 * j + e, to), mode)

    def hops(self):
        yield 0, 0
        for h in range(1, self.nz):
            for d in (0, 1):
                yield h, d

    def run(self, core, par, u, k, mode):
        self.setup(core, par, u)
        n, nz, z, b = self.n, self.nz, self.z, self.b
        lw = lane(n)
        sbase = self.fbase + nz * lw
        f, s = self.f, self.s
        pre = 0
        if core == 0:
            for j in range(n):
                if k is None or k == j:
                    for e in self.dirs(n) if j else (0,):
                        self.arrive(lambda i: self.sl(z, i, s), self.fbase, f, n, self.fstr, j, e, mode)
            pre = n - 1
        last = (n - 1) if core == 0 else 2 * (n - 1)
        for h, d in self.hops():
            zi = z - h if d == 0 else z + h
            fi = f if core == 1 else slice(None)

            def along_z():
                ref = self.sl(zi, fi, s)
                if h and mode == "start":
                    self.copy(ref, zi, b).wait_recv()
                if h < nz - 1:
                    for dd in (0, 1) if h == 0 else (d,):

                        @pl.when((z + 1 < nz) if dd == 0 else (z >= 1))
                        def _():
                            self.act(self.copy(ref, zi, b + (n * n if dd == 0 else -n * n)), mode)

            def in_plane(step):
                q = step
                if core == 1:
                    if step < n:
                        for e in self.dirs(n) if step else (0,):
                            self.arrive(
                                lambda i: self.sl(zi, i, s), self.fbase + zi * lw, f, n, self.fstr, step, e, mode
                            )
                    q = step - (n - 1)
                if q >= 0:
                    for e in self.dirs(n) if q else (0,):
                        at = sbase if n == 2 else sbase + zi * lw
                        self.arrive(lambda i: self.sl(zi, slice(None), i), at, s, n, self.sstr, q, e, mode, True)

            def events():
                for step in range(last + 1):
                    if k is None or k == pre + h + step:
                        if step == 0:
                            along_z()
                        in_plane(step)

            if k is None or 0 <= k - pre - h <= last:
                if h == 0:
                    events()
                else:
                    pl.when((zi >= 0) if d == 0 else (zi < nz))(events)
        if k == self.stages - 1:
            if n == 2:
                self.copy(self.sl(slice(None), slice(None), 1 - s), sbase, b).wait_recv()
            self.sibling(core, u).start()

    def drain(self, core, par, u):
        n, nz = self.n, self.nz
        if n == 2:
            slot, cs = u % self.slots, self.cols(core)
            for z in range(nz):
                along = (z + 1 if z < nz - 1 else 0) + (nz - z if z else 0)
                pieces = 1 + 2 * along + 2 * nz if core == 0 else along + 3 * nz
                same = self.stg.at[0:pieces, :, cs]

                @pl.when(self.z == z)
                def _():
                    pltpu.make_async_remote_copy(
                        src_ref=same,
                        dst_ref=same,
                        send_sem=self.ssem.at[slot],
                        recv_sem=self.rsem.at[slot, 0],
                        device_id=(self.b, 1 - self.c),
                        device_id_type=MESH,
                    ).wait_send()

        else:
            self.run(core, par, u, None, "drain")
        self.sibling(core, u).wait_send()

    def sibling(self, core, u):
        ref = self.G.at[u, :, :, :, :, self.cols(core)]
        return pltpu.make_async_remote_copy(
            src_ref=ref,
            dst_ref=ref,
            send_sem=self.sib_s.at[u % self.slots],
            recv_sem=self.sib_r.at[u % self.slots],
            device_id=(self.b, 1 - self.c),
            device_id_type=MESH,
        )

    def tick(self, t, part):
        order = [self.stages, *reversed(range(self.stages))]
        cuts = (0, 4, 6, 7) if len(order) == 7 else (0, len(order) // 3 + 1, 2 * len(order) // 3 + 1, len(order))
        for core in (0, 1):
            for odd in (0, 1):

                @pl.when((self.c == core) & (t % 2 == odd))
                def _():
                    for k in order[cuts[part] : cuts[part + 1]]:
                        u = t - self.ticks[k]
                        par = (odd + self.ticks[k]) % 2

                        @pl.when((u >= 0) & (u < UNITS))
                        def _():
                            if k == self.stages:
                                self.drain(core, par, u)
                            else:
                                self.run(core, par, u, k, "start")

    def barrier(self, meanwhile):
        bar = pltpu.get_barrier_semaphore()
        plane, me = 2 * self.n * self.n, self.place()

        def in_plane(i, carry):
            to = (me + i) % plane
            pl.semaphore_signal(bar, inc=1, device_id=self.at(to), device_id_type=MESH)
            return carry

        def along_z(i, carry):
            pl.semaphore_signal(bar, inc=1, device_id=self.along((self.z + i) % self.nz), device_id_type=MESH)
            return carry

        lax.fori_loop(1, plane, in_plane, 0, unroll=plane <= 8)
        lax.fori_loop(1, self.nz, along_z, 0, unroll=plane <= 8)
        meanwhile()
        pl.semaphore_wait(bar, plane - 1 + self.nz - 1)

    def place(self):
        return (self.b % (self.n * self.n)) * 2 + self.c

    def at(self, p):
        return (self.z * self.n * self.n + p // 2, p % 2)

    def along(self, z):
        return (z * self.n * self.n + self.b % (self.n * self.n), self.c)


class Total:
    def __init__(self, comm, phase, lo, hi, bg, planes, part, lines, total, sems):
        self.comm, self.phase, self.rows = comm, phase, pl.ds(lo, hi - lo)
        self.bg, self.planes, self.part, self.lines, self.total = bg, planes, part, lines, total
        self.sems = sems

    def ends(self, second):
        if second:
            return self.part, self.lines, self.comm.z, self.comm.nz
        return self.bg, self.planes, self.comm.place(), 2 * self.comm.n * self.comm.n

    def copy(self, second, src, dst, to):
        return pltpu.make_async_remote_copy(
            src_ref=src,
            dst_ref=dst,
            send_sem=self.sems.at[self.phase, 2 * second],
            recv_sem=self.sems.at[self.phase, 2 * second + 1],
            device_id=to,
            device_id_type=MESH,
        )

    def send(self, second):
        comm, rows = self.comm, self.rows
        src, dst, me, count = self.ends(second)

        def one(i, carry):
            peer = (me + i) % count
            to = comm.along(peer) if second else comm.at(peer)
            self.copy(second, src.at[rows], dst.at[me, rows], to).start()
            return carry

        lax.fori_loop(1, count, one, 0, unroll=count <= 8)

    def every(self, second):
        _, dst, _, count = self.ends(second)
        all_of = dst.at[pl.ds(0, count - 1), self.rows]
        return self.copy(second, all_of, all_of, (self.comm.b, 1 - self.comm.c))

    def add(self, second):
        src, buf, me, count = self.ends(second)
        out = self.total if second else self.part
        self.every(second).wait_recv()
        buf[me, self.rows] = src[self.rows]

        def one(i, acc):
            return acc + buf[i, self.rows]

        out[self.rows] = lax.fori_loop(1, count, one, buf[0, self.rows], unroll=count <= 8)
        self.every(second).wait_send()

    def start(self):
        self.send(0)

    def middle(self):
        self.add(0)
        self.send(1)

    def finish(self):
        self.add(1)


def dot(a, b, ca=1, cb=0):
    return lax.dot_general(a, b, (((ca,), (cb,)), ((), ())), preferred_element_type=F32)


def fold(values):
    rows, cols = values.shape
    return jnp.sum(values.reshape(rows // 8, 8, cols), axis=0)


def colsum(values):
    return jnp.sum(values, axis=0, keepdims=True)


def kernel(
    nz,
    n,
    ticks,
    slots,
    lengths,
    separators,
    hidden,
    cotangent,
    type_table_in,
    proj,
    outw,
    inner,
    outer,
    query_bias_in,
    value_bias_in,
    output_bias_in,
    inner_bias_in,
    outer_bias_in,
    first_gain_in,
    first_shift_in,
    second_gain_in,
    second_shift_in,
    layer_output,
    input_gradient,
    total,
    G,
    P0,
    type_table,
    query_bias,
    value_bias,
    output_bias,
    inner_bias,
    outer_bias,
    first_gain,
    first_shift,
    second_gain,
    second_shift,
    stg,
    xin,
    cot,
    xs,
    xb,
    qkv,
    qT,
    prob,
    mid,
    act,
    gp,
    n1,
    n2,
    r1,
    r2,
    gcT,
    dkT,
    dvT,
    wbuf,
    bg,
    planes,
    part,
    lines,
    dqs8,
    ssem,
    rsem,
    sib_s,
    sib_r,
    lsem,
    wsem,
    xsem,
    psem,
    vsem,
    osem,
    asems,
):
    nb = nz * n * n
    R = D // nb
    T = xs.shape[0]
    half = T // 2
    quarter = nb // 4
    comm = Comm(nz, n, G, stg, ssem, rsem, sib_s, sib_r, slots, ticks)
    c = comm.c
    other = (comm.b, 1 - c)
    ctx = xin

    def stage_in():
        for l in range(LAYERS):
            for u in range(8):
                m, j = (proj, u) if u < 3 else (outw, 0) if u == 3 else (inner, u - 4)
                pltpu.make_async_copy(m.at[l, :, pl.ds(j * D, D)], stg.at[l * PER + u], lsem.at[0]).start()
            for j in range(4):
                for g in range(4):
                    pltpu.make_async_copy(
                        outer.at[l, pl.ds(g * R, R), pl.ds(j * BLK, BLK)],
                        stg.at[l * PER + 8 + j, :, pl.ds(g * BLK, BLK)],
                        lsem.at[0],
                    ).start()

    def place():
        pltpu.make_async_copy(stg, stg, lsem.at[0]).wait()
        for core in (0, 1):

            @pl.when(c == core)
            def _():
                cs = comm.cols(core)
                to = G.at[:, comm.z, comm.y, comm.x, :, cs]
                cp = pltpu.make_async_copy(stg.at[:, :, cs], to, lsem.at[1])
                cp.start()
                cp.wait()

    def exchange(op):
        for i, (src, dst) in enumerate(((hidden, xin), (cotangent, cot))):
            rows = pl.ds(pl.multiple_of(c * half, half), half)
            lc = pltpu.make_async_copy(src.at[c], dst.at[rows], xsem.at[3 * i])
            rc = pltpu.make_async_remote_copy(
                src_ref=src.at[1 - c],
                dst_ref=dst.at[rows],
                send_sem=xsem.at[3 * i + 1],
                recv_sem=xsem.at[3 * i + 2],
                device_id=other,
                device_id_type=MESH,
            )
            getattr(lc, op)()
            getattr(rc, op)()

    vectors = (
        (type_table_in, type_table),
        (query_bias_in, query_bias),
        (value_bias_in, value_bias),
        (output_bias_in, output_bias),
        (inner_bias_in, inner_bias),
        (outer_bias_in, outer_bias),
        (first_gain_in, first_gain),
        (first_shift_in, first_shift),
        (second_gain_in, second_gain),
        (second_shift_in, second_shift),
    )

    def small(op):
        for i, (src, dst) in enumerate(vectors):
            getattr(pltpu.make_async_copy(src, dst, vsem.at[i]), op)()

    def begin():
        stage_in()
        small("start")

    comm.barrier(begin)
    exchange("start")
    place()

    def row(ref, l):
        return ref[pl.ds(l, 1), :]

    def cols(i, width=BLK):
        return pl.ds(pl.multiple_of(i * width, width), width)

    lanes = lax.broadcasted_iota(jnp.int32, (T, 2 * HEAD), 1)
    halves = (lanes < HEAD, lanes >= HEAD)

    def init_x():
        exchange("wait")
        small("wait")
        t0 = type_table[0:1, :].astype(F32)
        t1 = type_table[1:2, :].astype(F32)
        sep = separators[c]

        def rows_of(i, carry):
            rs = pl.ds(pl.multiple_of(i * ROWS, ROWS), ROWS)
            at = i * ROWS + lax.broadcasted_iota(jnp.int32, (ROWS, D), 0)
            second = (at > sep).astype(F32)
            x = xin[rs, :].astype(F32) + t0 + second * (t1 - t0)
            xs[rs, :] = x
            xb[rs, :] = x.astype(BF)
            return carry

        lax.fori_loop(0, T // ROWS, rows_of, 0)

    def load_unit(u, slot):
        pltpu.make_async_copy(G.at[u], wbuf.at[slot], wsem.at[slot]).start()

    def load_rows(l, f, slot):
        q = nz // 4
        for j in range(4):
            pltpu.make_async_copy(
                G.at[l * PER + 8 + j, pl.ds(f * q, q)], wbuf.at[slot, pl.ds(j * q, q)], wsem.at[slot]
            ).start()

    def loaded(slot):
        pltpu.make_async_copy(G.at[0], wbuf.at[slot], wsem.at[slot]).wait()

    def w_cols(slot, g):
        return wbuf[slot, :, :, :, :, cols(g)].reshape(D, BLK)

    def w_rows(slot, i):
        return wbuf[slot, pl.ds(i * (nz // 4), nz // 4)].reshape(BLK, D)

    def stacked(chips):
        return jnp.concatenate([w[:, g * BLK : (g + 1) * BLK] for w in chips for g in range(4)], axis=0)

    def chip(slot, i):
        return wbuf[slot, i // (n * n), (i // n) % n, i % n]

    def o_rows(slot, i):
        per = nb // 16
        return jnp.concatenate(
            [stacked([chip(slot, j * quarter + i * per + w) for w in range(per)]) for j in range(4)], axis=1
        )

    def o_cols(slot, i):
        return stacked([chip(slot, i * quarter + w) for w in range(quarter)])

    def norm_rows(z, gain, shift):
        average = jnp.mean(z, axis=1, keepdims=True)
        centred = z - average
        r = lax.rsqrt(jnp.mean(centred * centred, axis=1, keepdims=True) + EPSILON)
        normed = centred * r
        return normed, r, normed * gain + shift

    def do_qkv(l, j, slot, lo, hi):
        is_q, is_v = (j == 0).astype(F32), (j == 2).astype(F32)
        at = jnp.where(j == 0, 0, 2 * l + j)

        for g in range(lo, hi):
            sl = slice(g * BLK, (g + 1) * BLK)
            bias = query_bias[pl.ds(l, 1), sl] * is_q + value_bias[pl.ds(l, 1), sl] * is_v
            qkv[at, :, sl] = (dot(xb[...], w_cols(slot, g)) + bias).astype(BF)

    def do_attention(l, lo, hi):
        key_ok = lax.broadcasted_iota(jnp.int32, (1, T), 1) < lengths[c]

        def pair(hp, carry):
            cs = cols(hp, 2 * HEAD)
            q2, k2, v2 = qkv[0, :, cs], qkv[2 * l + 1, :, cs], qkv[2 * l + 2, :, cs]
            outs = []
            for hh in (0, 1):
                qm = jnp.where(halves[hh], q2 * BF(HEAD**-0.5), BF(0))
                s = jnp.where(key_ok, dot(qm, k2, 1, 1), MASKED)
                e = jnp.exp(s - jnp.max(s, axis=1, keepdims=True))
                p = (e * (1.0 / jnp.sum(e, axis=1, keepdims=True))).astype(BF)
                prob[2 * hp + hh] = p
                outs.append(dot(p, v2))
            ctx[:, cs] = jnp.where(halves[0], outs[0], outs[1]).astype(BF)
            qT[l, cs, :] = q2.T
            return carry

        lax.fori_loop(lo, hi, pair, 0)

    def do_out(l, slot, part):
        if part == 2:
            return do_norm1(l)
        for g in range(4):
            sl = slice(g * BLK, (g + 1) * BLK)
            mid[:, sl] = xs[:, sl] + dot(ctx[...], w_cols(slot, g)) + output_bias[pl.ds(l, 1), sl]

    def do_norm1(l):
        gain, shift = row(first_gain, l), row(first_shift, l)

        def rows_of(i, carry):
            rs = pl.ds(pl.multiple_of(i * ROWS, ROWS), ROWS)
            normed, r, y = norm_rows(mid[rs, :], gain, shift)
            n1[l, rs, :] = normed.astype(BF)
            r1[l, rs, :] = r
            mid[rs, :] = y
            xb[rs, :] = y.astype(BF)
            return carry

        lax.fori_loop(0, T // ROWS, rows_of, 0)

    def do_inner(l, pair):
        for of in (0, 1):
            i = 2 * pair + of
            cs = cols(i)
            h = dot(xb[...], w_cols((l * PER + 4 + pair // 2) % 3, i % 4)) + inner_bias[pl.ds(l, 1), cs]
            cdf = 0.5 + 0.5 * lax.erf(h * (0.5**0.5))
            act[:, cs] = (h * cdf).astype(BF)
            gp[l, :, cs] = (cdf + h * (jnp.exp(-0.5 * h * h) * 0.3989422804014327)).astype(BF)

    def do_outer(l, j, slot):
        cs = cols(j)
        y = mid[:, cs] + outer_bias[pl.ds(l, 1), cs]
        for i in range(4):
            y = y + dot(act[:, i * D : (i + 1) * D], o_cols(slot, i))
        xs[:, cs] = y

    def do_norm2(l):
        gain, shift = row(second_gain, l), row(second_shift, l)

        def rows_of(i, carry):
            rs = pl.ds(pl.multiple_of(i * ROWS, ROWS), ROWS)
            normed, r, y = norm_rows(xs[rs, :], gain, shift)
            n2[l, rs, :] = normed.astype(BF)
            r2[l, rs, :] = r
            yb = y.astype(BF)
            xb[rs, :] = yb
            ctx[rs, :] = yb
            xs[rs, :] = jnp.where(l == LAYERS - 1, cot[rs, :].astype(F32), y)
            return carry

        lax.fori_loop(0, T // ROWS, rows_of, 0)

    def save_prob(op):
        getattr(pltpu.make_async_copy(prob, P0, psem), op)()

    def compute(v, slot, part):
        l, k = v // PER, v % PER

        def choose(*of_k):
            out = jnp.int32(of_k[-1])
            for i, value in enumerate(of_k[:-1]):
                out = jnp.where(k == i, value, out)
            return out

        pl.when(k < 3)(lambda: do_qkv(l, k, slot, (0, 2, 3)[part], (2, 3, 4)[part]))

        first = {0: (0, 0, 0, 1, 4, 7), 1: (0, 0, 0, 2, 5), 2: (0, 0, 0, 3, 6)}[part]
        when = {0: (k >= 3) & (k <= 5), 1: (k == 3) | (k == 4), 2: (k >= 2) & (k <= 4)}[part]
        pl.when(when)(lambda: do_attention(l, choose(*first), choose(*first) + 1))

        if part:

            @pl.when(k == 5)
            def _():
                if part == 1:
                    pl.when(l == 0)(lambda: save_prob("start"))
                do_out(l, (v + 1) % 3, part)

        last = 7 if part == 2 else 8
        pl.when((k >= 6) & (k <= last))(lambda: do_inner(l, 3 * (k - 6) + part))
        if part != 1:
            pl.when(k > 8 if part == 0 else k == 8)(lambda: do_outer(l, k - 8, slot))
        if part == 1:

            @pl.when(k == PER - 1)
            def _():
                pl.when(l == 0)(lambda: save_prob("wait"))
                do_norm2(l)

    def load(s, slot):
        l, k = 1 - s // PER, s % PER
        rows = (k < 8) & (k % 2 == 0)
        pl.when(rows)(lambda: load_rows(l, k // 2, slot))
        unit = l * PER + jnp.where(k < 8, 4 + k // 2, jnp.where(k == 8, 3, k - 9))
        pl.when(jnp.logical_not(rows))(lambda: load_unit(unit, slot))

    lag = ticks[comm.stages - 1] + 1

    def main(t, carry):
        v = t - lag
        slot = (v + 3 * lag) % 3
        ready = (v >= 0) & (v < UNITS)

        comm.tick(t, 0)
        pl.when(t == 1)(init_x)

        @pl.when(ready)
        def _():
            loaded(slot)

            @pl.when(v == UNITS - 1)
            def _():
                load(0, 0)
                load(1, 1)

            compute(v, slot, 0)

        comm.tick(t, 1)
        pl.when(ready)(lambda: compute(v, slot, 1))
        comm.tick(t, 2)

        @pl.when((v >= -1) & (v < UNITS - 1))
        def _():
            for core in (0, 1):

                @pl.when(c == core)
                def _():
                    comm.sibling(1 - core, v + 1).wait_recv()

            load_unit(v + 1, (slot + 1) % 3)

        pl.when(ready)(lambda: compute(v, slot, 2))
        return carry

    lax.fori_loop(0, UNITS + ticks[comm.stages], main, 0)

    def results(src, out, base, op):
        mine = pl.ds(pl.multiple_of(c * half, half), half)
        theirs = pl.ds(pl.multiple_of((1 - c) * half, half), half)
        lc = pltpu.make_async_copy(src.at[mine], out.at[c], osem.at[base])
        rc = pltpu.make_async_remote_copy(
            src_ref=src.at[theirs],
            dst_ref=out.at[c],
            send_sem=osem.at[base + 1],
            recv_sem=osem.at[base + 2],
            device_id=other,
            device_id_type=MESH,
        )
        if op == "start":
            rc.start()
            lc.start()
        else:
            rc.wait_send()
            lc.wait()

    def arrived(src, out, base):
        rows = pl.ds(0, half)
        pltpu.make_async_remote_copy(
            src_ref=src.at[rows],
            dst_ref=out.at[1 - c],
            send_sem=osem.at[base + 1],
            recv_sem=osem.at[base + 2],
            device_id=other,
            device_id_type=MESH,
        ).wait_recv()

    def next_weights(s):
        loaded(s % 3)
        pl.when(s + 2 < UNITS)(lambda: load(s + 2, (s + 2) % 3))
        return s % 3

    def keep_sum(l, k, values):
        for i in range(values.shape[1] // 128):
            bg[(1 - l) * 10 + k, i : i + 1, :] = values[:, i * 128 : (i + 1) * 128]

    def norm_back(l, source, normed, r_ref, gain_ref, at_shift, at_bias, keep):
        gain = row(gain_ref, l)

        def rows_of(i, carry):
            sum_g, sum_z = carry
            rs = pl.ds(pl.multiple_of(i * ROWS, ROWS), ROWS)
            g = source[rs, :]
            nv = normed[l, rs, :].astype(F32)
            u = g * gain
            gz = r_ref[l, rs, :] * (
                u - jnp.mean(u, axis=1, keepdims=True) - nv * jnp.mean(u * nv, axis=1, keepdims=True)
            )
            keep[rs, :] = gz
            xb[rs, :] = gz.astype(BF)
            return sum_g + fold(g), sum_z + fold(gz)

        zero = jnp.zeros((8, D), F32)
        sum_g, sum_z = lax.fori_loop(0, T // ROWS, rows_of, (zero, zero))
        keep_sum(l, at_shift, colsum(sum_g))
        keep_sum(l, at_bias, colsum(sum_z))

    results(ctx, layer_output, 0, "start")

    def layer_back(i, carry):
        l = LAYERS - 1 - i
        s0 = i * PER
        norm_back(l, xs, n2, r2, second_gain, 7, 5, mid)

        def ff(f, carry):
            slot = next_weights(s0 + 2 * f)
            for i4 in range(4):
                cs = cols(f * 4 + i4)
                gh = dot(xb[...], o_rows(slot, i4), 1, 1) * gp[l, :, cs].astype(F32)
                sums = colsum(fold(gh))
                bg[(1 - l) * 10 + 1 + f, 2 * i4 : 2 * i4 + 1, :] = sums[:, :128]
                bg[(1 - l) * 10 + 1 + f, 2 * i4 + 1 : 2 * i4 + 2, :] = sums[:, 128:]
                act[:, cs] = gh.astype(BF)
            slot = next_weights(s0 + 2 * f + 1)
            for i4 in range(4):
                sl = slice(i4 * BLK, (i4 + 1) * BLK)
                mid[:, sl] += dot(act[:, cols(f, D)], w_rows(slot, i4), 1, 1)
            return carry

        lax.fori_loop(0, 4, ff, 0)
        norm_back(l, mid, n1, r1, first_gain, 6, 0, mid)
        pl.when(i == 1)(totals[0].start)
        slot = next_weights(s0 + 8)
        for i4 in range(4):
            sl = slice(i4 * BLK, (i4 + 1) * BLK)
            gc = dot(xb[...], w_rows(slot, i4), 1, 1).astype(BF)
            sums = colsum(fold(gc.astype(F32)))
            bg[(1 - l) * 10 + 8, 2 * i4 : 2 * i4 + 1, :] = sums[:, :128]
            bg[(1 - l) * 10 + 8, 2 * i4 + 1 : 2 * i4 + 2, :] = sums[:, 128:]
            qkv[0, :, sl] = gc
            gcT[sl, :] = gc.T

        pl.when(i == 0)(lambda: results(ctx, layer_output, 0, "wait"))

        @pl.when(i == 1)
        def _():
            load_prob("wait")

        def pair(hp, carry):
            cs = cols(hp, 2 * HEAD)
            gc2, k2, v2 = qkv[0, :, cs], qkv[2 * l + 1, :, cs], qkv[2 * l + 2, :, cs]
            dqs = []
            for hh in (0, 1):
                hs = pl.ds(pl.multiple_of((2 * hp + hh) * HEAD, HEAD), HEAD)
                p = prob[2 * hp + hh]
                pf = p.astype(F32)
                gm = jnp.where(halves[hh], gc2 * BF(HEAD**-0.5), BF(0))
                dp = dot(gm, v2, 1, 1)
                total = jnp.sum(dp * pf, axis=1, keepdims=True)
                ds = (pf * (dp - total)).astype(BF)
                dqs.append(dot(ds, k2))
                dkT[hs, :] = dot(qT[l, hs, :], ds).astype(BF)
                dvT[hs, :] = dot(gcT[hs, :], p).astype(BF)
            dq = jnp.where(halves[0], dqs[0], dqs[1])
            dqs8[:, cs] = fold(dq)
            ctx[:, cs] = dq.astype(BF)
            return carry

        def four(j, carry):
            lax.fori_loop(0, 4, lambda h, x: pair(4 * j + h, x), 0, unroll=4)
            pl.when((i == 1) & (j == 0))(totals[0].middle)
            return carry

        lax.fori_loop(0, HEADS // 8, four, 0)
        keep_sum(l, 9, colsum(dqs8[...]))

        @pl.when(i == 0)
        def _():
            load_prob("start")

        @pl.when(i == 1)
        def _():
            totals[1].start()


        slot = next_weights(s0 + 9)
        for i4 in range(4):
            sl = slice(i4 * BLK, (i4 + 1) * BLK)
            mid[:, sl] += dot(ctx[...], w_rows(slot, i4), 1, 1)
        slot = next_weights(s0 + 10)
        for i4 in range(4):
            sl = slice(i4 * BLK, (i4 + 1) * BLK)
            mid[:, sl] += dot(dkT[...], w_rows(slot, i4), 0, 1)

        @pl.when(i == 1)
        def _():
            totals[1].middle()
            totals[0].finish()

        slot = next_weights(s0 + 11)
        for i4 in range(4):
            sl = slice(i4 * BLK, (i4 + 1) * BLK)
            y = mid[:, sl] + dot(dvT[...], w_rows(slot, i4), 0, 1)
            xs[:, sl] = y
            xb[:, sl] = y.astype(BF)
        return carry

    def load_prob(op):
        getattr(pltpu.make_async_copy(P0, prob, psem), op)()

    totals = [
        Total(comm, phase, lo, hi, bg, planes, part, lines, total, asems)
        for phase, (lo, hi) in enumerate(((0, 18), (18, 20)))
    ]
    lax.fori_loop(0, LAYERS, layer_back, 0)
    results(xb, input_gradient, 3, "start")
    totals[1].finish()
    results(xb, input_gradient, 3, "wait")
    arrived(xb, layer_output, 0)
    arrived(xb, input_gradient, 3)


def finish(first, second, total, *rest):
    outs, (buf, rows, *sums), (into, outof) = rest[:9], rest[9:18], rest[18:]
    half = first.shape[1] // 2
    moves = []
    for i, (src, dst) in enumerate(((first, outs[0]), (second, outs[1]))):
        for j in range(2):
            part = pl.ds(j * half, half)
            k = 2 * i + j
            moves.append(
                (
                    pltpu.make_async_copy(src.at[:, part], buf.at[k], into.at[k]),
                    pltpu.make_async_copy(buf.at[k], dst.at[:, part], outof.at[k]),
                )
            )
    small = pltpu.make_async_copy(total, rows, into.at[4])
    small.start()
    for here, _ in moves:
        here.start()
    small.wait()
    done = [there for _, there in moves]
    for m, ks in enumerate(((9,), (8,), (0,), (1, 2, 3, 4), (5,), (6,), (7,))):
        for l in range(LAYERS):
            for at, k in enumerate(ks):
                for i in range(8):
                    sums[m][l : l + 1, at * D + i * 128 : at * D + (i + 1) * 128] = rows[(1 - l) * 10 + k, i : i + 1, :]
        done.append(pltpu.make_async_copy(sums[m], outs[2 + m], outof.at[4 + m]))
        done[-1].start()
    for here, there in moves:
        here.wait()
        there.start()
    for there in done:
        there.wait()


def on_device(
    hidden,
    cotangent,
    lengths,
    separators,
    type_table,
    projection_weight,
    output_weight,
    inner_weight,
    outer_weight,
    query_bias,
    value_bias,
    output_bias,
    inner_bias,
    outer_bias,
    first_gain,
    first_shift,
    second_gain,
    second_shift,
):
    nb = lax.axis_size("batch")
    nz, n = sizes(nb)
    gap = 2 if nb <= 16 else 1
    stages = 1 + (n - 1) + (nz - 1) + (n - 1)
    ticks = [k * gap for k in range(stages + 1)]
    if gap == 2:
        ticks = [0, 2, 4, 6, 7, 9, 11]
    slots = ticks[-1] + gap
    plane = 2 * n * n
    T = 2 * hidden.shape[1]
    R = D // nb
    smem = pl.BlockSpec(memory_space=pltpu.SMEM)
    vmem = pl.BlockSpec(memory_space=pltpu.VMEM)
    hbm = pl.BlockSpec(memory_space=pl.ANY)
    sems = Comm.sems(nz, n)
    out_shape = (
        jax.ShapeDtypeStruct(hidden.shape, BF),
        jax.ShapeDtypeStruct(hidden.shape, BF),
        jax.ShapeDtypeStruct((LAYERS * 10, 8, 128), F32),
        jax.ShapeDtypeStruct((UNITS, nz, n, n, R, D), BF),
        jax.ShapeDtypeStruct((HEADS, T, T), BF),
    )
    dma = pltpu.SemaphoreType.DMA
    scratch = [
        pltpu.VMEM((2, D), BF),
        *(pltpu.VMEM((LAYERS, w), F32) for w in (D, D, D, FF, D, D, D, D, D)),
        pltpu.VMEM((UNITS, R, D), BF),
        pltpu.VMEM((T, D), BF),
        pltpu.VMEM((T, D), BF),
        pltpu.VMEM((T, D), F32),
        pltpu.VMEM((T, D), BF),
        pltpu.VMEM((5, T, D), BF),
        pltpu.VMEM((LAYERS, D, T), BF),
        pltpu.VMEM((HEADS, T, T), BF),
        pltpu.VMEM((T, D), F32),
        pltpu.VMEM((T, FF), BF),
        pltpu.VMEM((LAYERS, T, FF), BF),
        pltpu.VMEM((LAYERS, T, D), BF),
        pltpu.VMEM((LAYERS, T, D), BF),
        pltpu.VMEM((LAYERS, T, 1), F32),
        pltpu.VMEM((LAYERS, T, 1), F32),
        pltpu.VMEM((D, T), BF),
        pltpu.VMEM((D, T), BF),
        pltpu.VMEM((D, T), BF),
        pltpu.VMEM((3, nz, n, n, R, D), BF),
        pltpu.VMEM((LAYERS * 10, 8, 128), F32),
        pltpu.VMEM((plane, LAYERS * 10, 8, 128), F32),
        pltpu.VMEM((LAYERS * 10, 8, 128), F32),
        pltpu.VMEM((nz, LAYERS * 10, 8, 128), F32),
        pltpu.VMEM((8, D), F32),
        dma((slots,)),
        dma((slots, sems)),
        dma((slots,)),
        dma((slots,)),
        dma((2,)),
        dma((3,)),
        dma((6,)),
        dma(()),
        dma((10,)),
        dma((6,)),
        dma((2, 4)),
    ]
    out = pl.pallas_call(
        functools.partial(kernel, nz, n, ticks, slots),
        out_shape=out_shape,
        in_specs=[smem, smem] + [hbm] * 16,
        out_specs=(hbm, hbm, vmem, hbm, hbm),
        scratch_shapes=scratch,
        compiler_params=pltpu.CompilerParams(
            collective_id=0, has_side_effects=True, vmem_limit_bytes=60 * 2**20
        ),
        cost_estimate=pl.CostEstimate(flops=60 * 10**9, bytes_accessed=200 * 10**6, transcendentals=20 * 10**6),
    )(
        lengths,
        separators,
        hidden,
        cotangent,
        type_table,
        projection_weight,
        output_weight,
        inner_weight,
        outer_weight,
        query_bias,
        value_bias,
        output_bias,
        inner_bias,
        outer_bias,
        first_gain,
        first_shift,
        second_gain,
        second_shift,
    )
    half = hidden.shape[1] // 2
    sums = [query_bias, value_bias, output_bias, inner_bias, outer_bias, first_shift, second_shift]
    return tuple(
        pl.pallas_call(
            finish,
            out_shape=(
                jax.ShapeDtypeStruct(hidden.shape, BF),
                jax.ShapeDtypeStruct(hidden.shape, BF),
                *(jax.ShapeDtypeStruct(b.shape, F32) for b in sums),
            ),
            in_specs=[hbm] * 3,
            out_specs=(hbm,) * 9,
            scratch_shapes=[
                pltpu.VMEM((4, 2, half, D), BF),
                pltpu.VMEM((LAYERS * 10, 8, 128), F32),
                *(pltpu.VMEM(b.shape, F32) for b in sums),
                dma((5,)),
                dma((11,)),
            ],
        )(out[0], out[1], out[2])
    )


def solution(mesh):
    batched = P("batch", "blk", None)
    rows = P(None, "batch", None)
    return jax.shard_map(
        on_device,
        mesh=mesh,
        in_specs=(batched, batched, P("batch"), P("batch"), P(), rows, rows, rows, rows) + (P(),) * 9,
        out_specs=(batched, batched) + (P(),) * 7,
        check_vma=False,
    )
```
